32 devices in a mesh: ctx: 2 (over y), shard: 16 (over z, x, core).
Axes of the slice: x: 2, y: 2, z: 4, core: 2. Of those that a mesh axis runs over, the one named last changes fastest.
Arguments:
- table_weight: float32 [50688, 768], P(('ctx', 'shard'))
- table_moment: float32 [50688, 768], P(('ctx', 'shard')), may hold values from -1.1444092e-05 to 1.1444092e-05
- table_square: float32 [50688, 768], P(('ctx', 'shard')), may hold values from 4.4440312e-14 to 1.7776125e-13
- position_weight: float32 [1024, 768], P('shard', 'ctx'), may hold values from -0.75 to 0.75
- position_moment: float32 [1024, 768], P('shard', 'ctx'), may hold values from -1.1444092e-05 to 1.1444092e-05
- position_square: float32 [1024, 768], P('shard', 'ctx'), may hold values from 4.4440312e-14 to 1.7776125e-13
- wide_weight: float32 [768, 15360], P('shard', 'ctx'), may hold values from -0.21875 to 0.21875
- wide_moment: float32 [768, 15360], P('shard', 'ctx'), may hold values from -1.1444092e-05 to 1.1444092e-05
- wide_square: float32 [768, 15360], P('shard', 'ctx'), may hold values from 4.4440312e-14 to 1.7776125e-13
- down_weight: float32 [2, 3072, 768], P(None, 'shard', 'ctx'), may hold values from -0.109375 to 0.109375
- down_moment: float32 [2, 3072, 768], P(None, 'shard', 'ctx'), may hold values from -1.1444092e-05 to 1.1444092e-05
- down_square: float32 [2, 3072, 768], P(None, 'shard', 'ctx'), may hold values from 4.4440312e-14 to 1.7776125e-13
- vector_weight: float32 [33, 768], replicated
- vector_moment: float32 [33, 768], replicated, may hold values from -1.1444092e-05 to 1.1444092e-05
- vector_square: float32 [33, 768], replicated, may hold values from 4.4440312e-14 to 1.7776125e-13
- source_ids: int32 [16, 1024], P('shard', 'ctx'), may hold values from 0 to 50264
- target_ids: int32 [16, 1024], P('shard', 'ctx'), may hold values from 0 to 50264
- target_labels: int32 [16, 1024], P('shard', 'ctx'), may hold values from 0 to 50264
- source_segments: int32 [16, 1024], P('shard', 'ctx'), may hold values from 0 to 3, as said below
- target_segments: int32 [16, 1024], P('shard', 'ctx'), may hold values from 0 to 3, as said below
- completion_idx: int32 [16, 256], P('shard', 'ctx'), may hold values from 0 to 511, as said below
Outputs:
- loss_sum: float32 [], replicated
- grad_norm: float32 [], replicated
- new_table_moment: float32 [50688, 768], P(('ctx', 'shard'))
- new_table_square: float32 [50688, 768], P(('ctx', 'shard'))
- new_table_weight: float32 [50688, 768], P(('ctx', 'shard'))
- new_position_moment: float32 [1024, 768], P('shard', 'ctx')
- new_position_square: float32 [1024, 768], P('shard', 'ctx')
- new_position_weight: float32 [1024, 768], P('shard', 'ctx')
- new_wide_moment: float32 [768, 15360], P('shard', 'ctx')
- new_wide_square: float32 [768, 15360], P('shard', 'ctx')
- new_wide_weight: float32 [768, 15360], P('shard', 'ctx')
- new_down_moment: float32 [2, 3072, 768], P(None, 'shard', 'ctx')
- new_down_square: float32 [2, 3072, 768], P(None, 'shard', 'ctx')
- new_down_weight: float32 [2, 3072, 768], P(None, 'shard', 'ctx')
- new_vector_moment: float32 [33, 768], replicated
- new_vector_square: float32 [33, 768], replicated
- new_vector_weight: float32 [33, 768], replicated
The draws below stay inside these ranges and needn't reach their ends.
Inputs may be any that keep to these rules, and one draw needn't show every extreme that they name: `source_segments`: in each sequence the document numbers never fall, start at 0 and end at 3; one document of each sequence is long, the others hold 32 to 170 tokens each; source and target sequences of one row hold documents of the same numbers. `target_segments`: as for source_segments. `completion_idx`: the 128 entries of each block are distinct and increasing.
All inputs are finite; a program needn't handle non-finite values.
Results may differ from the reference program's by a relative error of at most 0.0053.
Values may be sent and summed in bfloat16 or wider, within the bound.
No kernel may reach another device: no remote copies, remote signals or barrier semaphores. Data moves between devices by JAX's collectives and lax.ppermute only.
A program may use at most 448 MiB of HBM per device.

```python
import math
from functools import partial
import jax
import jax.numpy as jnp
import numpy as np
from jax import lax

D = 768
H = 12
HD = 64
FF = 3072
V = 50265
P_SIZE = 1024
VP = 50688
NDOC = 4
STEP = 10
TOK_DEV = 512
SEQ = 1024
SEQS = 16
COMP = 128
DOC_LO = 32
DOC_HI = 170
NVEC = 33
NPARAM = 56255232
N_CTX = 2


def draw_table_weight(key, part):
    key = jax.random.fold_in(key, 11)
    ramp = jnp.arange(VP, dtype=jnp.float32)[:, None] / VP
    base = jax.random.normal(key, (VP, D), jnp.float32)
    factor = 1.0 + 2.0 * ramp
    return base * factor * D ** (-0.5)


def draw_vector_weight(key, part):
    key = jax.random.fold_in(key, 12)
    gain_rows = jnp.zeros((NVEC, 1), jnp.float32).at[np.array([0, 5, 8, 10, 15, 20, 23])].set(1.0)
    noise = 0.25 * jax.random.normal(key, (NVEC, D), jnp.float32)
    return gain_rows + noise


def document_numbers(key):
    shorter = jax.random.randint(key, (SEQS, NDOC - 1), DOC_LO, DOC_HI + 1)
    longest = SEQ - jnp.sum(shorter, axis=1, keepdims=True)
    slot = jax.random.randint(jax.random.fold_in(key, 1), (SEQS, 1), 0, NDOC)
    zero_col = jnp.zeros((SEQS, 1), jnp.int32)
    left_side = jnp.concatenate([shorter, zero_col], 1)
    right_side = jnp.concatenate([zero_col, shorter], 1)
    columns = jnp.arange(NDOC)[None, :]
    lengths = jnp.where(columns < slot, left_side, jnp.where(columns == slot, longest, right_side))
    ends = jnp.cumsum(lengths, axis=1)
    places = jnp.arange(SEQ)[None, :, None]
    return jnp.sum((places >= ends[:, None, :NDOC - 1]).astype(jnp.int32), axis=2).astype(jnp.int32)


def draw_source_segments(key, part):
    key = jax.random.fold_in(key, 21)
    return document_numbers(key)


def draw_target_segments(key, part):
    key = jax.random.fold_in(key, 22)
    return document_numbers(key)


def draw_completion_idx(key, part):
    key = jax.random.fold_in(key, 23)
    blocks = SEQS * (SEQ // TOK_DEV)
    keys_all = jax.random.split(key, blocks)

    def pick_block(block_key):
        return jnp.sort(jax.random.permutation(block_key, TOK_DEV)[:COMP]).astype(jnp.int32)
    picks = jax.vmap(pick_block)(keys_all)
    return picks.reshape(SEQS, SEQ // TOK_DEV * COMP).astype(jnp.int32)


def place_ends(result, stream_key, low, high):
    shape = result.shape
    place = [jax.random.randint(jax.random.fold_in(stream_key, axis), (), 0, shape[axis]) for axis in range(len(shape))]
    result = result.at[tuple(place)].set(low)
    longest = shape.index(max(shape))
    place[longest] = (place[longest] + 1) % shape[longest]
    return result.at[tuple(place)].set(high)


def block_scale(own_key, extent, cuts, smallest, top_value):
    level = 1.0
    for axis_at, parts in cuts:
        steps = jax.random.uniform(jax.random.fold_in(jax.random.fold_in(own_key, 6), axis_at), (parts,), jnp.float32, smallest / len(cuts), top_value / len(cuts))
        level = level * jnp.repeat(jnp.exp(steps), extent[axis_at] // parts).reshape((-1,) + (1,) * (len(extent) - 1 - axis_at))
    return level


def rank_table(number_of, skew):
    loads = [(1 << 20) // math.isqrt(grade ** skew) + 1 for grade in range(1, number_of + 1)]
    scale = 1 + sum(loads) // (1 << 30)
    return np.cumsum(np.array([max(1, weight // scale) for weight in loads]))


def ranked_ids(own_key, shape, number_of, slope):
    grid = rank_table(number_of, slope)
    ticket = jax.random.randint(jax.random.fold_in(own_key, 1), shape, 0, int(grid[number_of - 1]))
    rank = jnp.searchsorted(jnp.asarray(grid, jnp.int32), ticket, side="right")
    return jax.random.permutation(jax.random.fold_in(own_key, 2), number_of)[rank].astype(jnp.int32)


def gaussian(stream_key, dims, scale, most, cuts=(), kind=jnp.bfloat16):
    drawn = scale * jax.random.normal(stream_key, dims, jnp.float32)
    if cuts:
        drawn = drawn * block_scale(stream_key, dims, cuts, -0.22, 0.18)
    return jnp.clip(drawn, -most, most).astype(kind)


def setup_inputs(seed: int = 0) -> dict:
    splits = jax.random.split(jax.random.key(seed), 22)
    return {
        "table_weight": draw_table_weight(jax.random.fold_in(splits[21], 71), 0),
        "table_moment": gaussian(splits[1], (VP, D), (0.0055 / NPARAM ** 0.5), 1.1444091796875e-05, ((0, 32),), jnp.float32),
        "table_square": jnp.clip(jnp.exp(math.log(1.7776124810412602e-13) - 1.3862944 * jax.random.uniform(splits[2], (VP, D), jnp.float32) ** block_scale(splits[2], (VP, D), ((0, 32),), -0.2, 0.2)), 4.4440312026031506e-14, 1.7776124810412602e-13),
        "position_weight": gaussian(splits[3], (P_SIZE, D), (1.5 / D ** 0.5), 0.75, ((0, 16), (1, 2)), jnp.float32),
        "position_moment": gaussian(splits[4], (P_SIZE, D), (0.0055 / NPARAM ** 0.5), 1.1444091796875e-05, ((0, 16), (1, 2)), jnp.float32),
        "position_square": jnp.clip(jnp.exp(math.log(1.7776124810412602e-13) - 1.3862944 * jax.random.uniform(splits[5], (P_SIZE, D), jnp.float32) ** block_scale(splits[5], (P_SIZE, D), ((0, 16), (1, 2)), -0.2, 0.2)), 4.4440312026031506e-14, 1.7776124810412602e-13),
        "wide_weight": gaussian(splits[6], (D, 12 * D + 2 * FF), D ** -0.5, 0.21875, ((0, 16), (1, 2)), jnp.float32),
        "wide_moment": gaussian(splits[7], (D, 12 * D + 2 * FF), (0.0055 / NPARAM ** 0.5), 1.1444091796875e-05, ((0, 16), (1, 2)), jnp.float32),
        "wide_square": jnp.clip(jnp.exp(math.log(1.7776124810412602e-13) - 1.3862944 * jax.random.uniform(splits[8], (D, 12 * D + 2 * FF), jnp.float32) ** block_scale(splits[8], (D, 12 * D + 2 * FF), ((0, 16), (1, 2)), -0.2, 0.2)), 4.4440312026031506e-14, 1.7776124810412602e-13),
        "down_weight": gaussian(splits[9], (2, FF, D), FF ** -0.5, 0.109375, ((1, 16), (2, 2)), jnp.float32),
        "down_moment": gaussian(splits[10], (2, FF, D), (0.0055 / NPARAM ** 0.5), 1.1444091796875e-05, ((1, 16), (2, 2)), jnp.float32),
        "down_square": jnp.clip(jnp.exp(math.log(1.7776124810412602e-13) - 1.3862944 * jax.random.uniform(splits[11], (2, FF, D), jnp.float32) ** block_scale(splits[11], (2, FF, D), ((1, 16), (2, 2)), -0.2, 0.2)), 4.4440312026031506e-14, 1.7776124810412602e-13),
        "vector_weight": draw_vector_weight(jax.random.fold_in(splits[21], 71), 0),
        "vector_moment": gaussian(splits[13], (NVEC, D), (0.0055 / NPARAM ** 0.5), 1.1444091796875e-05, (), jnp.float32),
        "vector_square": jnp.clip(jnp.exp(jax.random.uniform(splits[14], (NVEC, D), jnp.float32, math.log(4.4440312026031506e-14), math.log(1.7776124810412602e-13))), 4.4440312026031506e-14, 1.7776124810412602e-13),
        "source_ids": place_ends(ranked_ids(splits[15], (SEQS, SEQ), V, 2), jax.random.fold_in(splits[15], 3), 0, V - 1).astype(jnp.int32),
        "target_ids": place_ends(ranked_ids(splits[16], (SEQS, SEQ), V, 2), jax.random.fold_in(splits[16], 3), 0, V - 1).astype(jnp.int32),
        "target_labels": place_ends(ranked_ids(splits[17], (SEQS, SEQ), V, 2), jax.random.fold_in(splits[17], 3), 0, V - 1).astype(jnp.int32),
        "source_segments": draw_source_segments(jax.random.fold_in(splits[21], 71), 0),
        "target_segments": draw_target_segments(jax.random.fold_in(splits[21], 71), 0),
        "completion_idx": draw_completion_idx(jax.random.fold_in(splits[21], 71), 0),
    }


@jax.custom_vjp
def low(v):
    return lax.optimization_barrier(v.astype(jnp.bfloat16)).astype(jnp.float32)

@jax.custom_vjp
def low_back(v):
    return v

def low_keep(v):
    return (low(v), None)

def low_pass(kept, grad):
    return (grad,)

def back_keep(v):
    return (v, None)

def back_low(kept, grad):
    return (low(grad),)
low.defvjp(low_keep, low_pass)
low_back.defvjp(back_keep, back_low)
PRECISE = lax.Precision.HIGHEST
NORM_EPS = 1e-05
LEARN_RATE = 0.03
VECTOR_RATE = 0.3
BETA_ONE = 0.9
BETA_TWO = 0.999
ADAM_EPS = 1e-08
WEIGHT_DECAY = 0.01
CLIP_LIMIT = 0.05
MASKED_SCORE = -1e+30
VEC_NAMES = ['enc_norm0_gain', 'enc_norm0_bias', 'enc_query_bias', 'enc_value_bias', 'enc_out_bias', 'enc_norm1_gain', 'enc_norm1_bias', 'enc_ffn_bias', 'enc_norm2_gain', 'enc_norm2_bias', 'dec_norm0_gain', 'dec_norm0_bias', 'dec_query_bias', 'dec_value_bias', 'dec_out_bias', 'dec_norm1_gain', 'dec_norm1_bias', 'cross_query_bias', 'cross_value_bias', 'cross_out_bias', 'dec_norm2_gain', 'dec_norm2_bias', 'dec_ffn_bias', 'dec_norm3_gain', 'dec_norm3_bias']

def product(left, right):
    return jnp.dot(left, right, precision=PRECISE)

def norm_layer(values, gain, bias):
    center = values - lax.optimization_barrier(jnp.mean(values, -1, keepdims=True))
    spread = lax.optimization_barrier(jnp.mean(center * center, -1, keepdims=True))
    return center * lax.rsqrt(spread + NORM_EPS) * gain + bias

def split_columns(matrix, width, hidden):
    sizes = [3 * width, width, hidden, 3 * width, width, width, 2 * width, width, hidden]
    starts = [sum(sizes[:index]) for index in range(len(sizes))]
    return [matrix[:, start:start + size] for start, size in zip(starts, sizes)]

def doc_positions(segment):
    length = segment.shape[0]
    places = jnp.arange(length, dtype=jnp.int32)
    change = jnp.concatenate([jnp.ones((1,), bool), segment[1:] != segment[:-1]])
    starts = lax.cummax(jnp.where(change, places, 0).astype(jnp.int32), axis=0)
    return jnp.minimum(places - starts, P_SIZE - 1).astype(jnp.int32)

def attend(query_in, key_in, weight_q, bias_q, weight_k, weight_v, bias_v, weight_o, bias_o, allowed):
    query_rows = query_in.shape[0]
    key_rows = key_in.shape[0]
    query_b = low(query_in)
    key_b = low(key_in)
    queries = low(low_back((product(query_b, weight_q) + bias_q) * 0.125)).reshape(query_rows, H, HD)
    keys_f = low(low_back(product(key_b, weight_k))).reshape(key_rows, H, HD)
    values_f = low(low_back(product(key_b, weight_v) + bias_v)).reshape(key_rows, H, HD)
    scores = low_back(jnp.einsum('thd,shd->hts', queries, keys_f, precision=PRECISE))
    scores = jnp.where(allowed[None], scores, MASKED_SCORE)
    attn_probs = jax.nn.softmax(scores, axis=-1)
    mixed_out = jnp.einsum('hts,shd->thd', low(attn_probs), values_f, precision=PRECISE).reshape(query_rows, H * HD)
    return low_back(product(low(low_back(mixed_out)), weight_o) + bias_o)

def feed(inputs, first_weight, first_bias, second_weight, second_bias):
    pre_act = low_back(product(low(inputs), first_weight) + first_bias)
    act_low = low(jax.nn.gelu(pre_act, approximate=False))
    return low_back(product(act_low, second_weight) + second_bias)

def pair_loss(params, data):
    table, positions, wide, down, vectors = params
    source_ids, target_ids, target_labels, source_segments, target_segments, completion_idx = data

    def vector_row(name):
        return vectors[VEC_NAMES.index(name)]
    blocks = FF // D
    enc_first_bias = vectors[len(VEC_NAMES):len(VEC_NAMES) + blocks].reshape(-1)
    dec_first_bias = vectors[len(VEC_NAMES) + blocks:len(VEC_NAMES) + 2 * blocks].reshape(-1)
    enc_qkv, enc_out, enc_first, dec_qkv, dec_out, cross_query, cross_kv, cross_out, dec_first = split_columns(wide, D, FF)
    src_input = low_back(table[source_ids]) + positions[doc_positions(source_segments)]
    tgt_input = low_back(table[target_ids]) + positions[doc_positions(target_segments)]
    places = jnp.arange(SEQ)
    enc_allowed = source_segments[:, None] == source_segments[None, :]
    self_allowed = (target_segments[:, None] == target_segments[None, :]) & (places[:, None] >= places[None, :])
    cross_allowed = target_segments[:, None] == source_segments[None, :]
    enc_x1 = norm_layer(src_input, vector_row('enc_norm0_gain'), vector_row('enc_norm0_bias'))
    enc_branch = attend(enc_x1, enc_x1, enc_qkv[:, :D], vector_row('enc_query_bias'), enc_qkv[:, D:2 * D], enc_qkv[:, 2 * D:], vector_row('enc_value_bias'), enc_out, vector_row('enc_out_bias'), enc_allowed)
    enc_x2 = norm_layer(enc_x1 + enc_branch, vector_row('enc_norm1_gain'), vector_row('enc_norm1_bias'))
    enc_ffn = feed(enc_x2, enc_first, enc_first_bias, down[0], vector_row('enc_ffn_bias'))
    encoded = norm_layer(enc_x2 + enc_ffn, vector_row('enc_norm2_gain'), vector_row('enc_norm2_bias'))
    dec_u1 = norm_layer(tgt_input, vector_row('dec_norm0_gain'), vector_row('dec_norm0_bias'))
    self_branch = attend(dec_u1, dec_u1, dec_qkv[:, :D], vector_row('dec_query_bias'), dec_qkv[:, D:2 * D], dec_qkv[:, 2 * D:], vector_row('dec_value_bias'), dec_out, vector_row('dec_out_bias'), self_allowed)
    dec_u2 = norm_layer(dec_u1 + self_branch, vector_row('dec_norm1_gain'), vector_row('dec_norm1_bias'))
    cross_branch = attend(dec_u2, encoded, cross_query, vector_row('cross_query_bias'), cross_kv[:, :D], cross_kv[:, D:], vector_row('cross_value_bias'), cross_out, vector_row('cross_out_bias'), cross_allowed)
    dec_u3 = norm_layer(dec_u2 + cross_branch, vector_row('dec_norm2_gain'), vector_row('dec_norm2_bias'))
    dec_ffn = feed(dec_u3, dec_first, dec_first_bias, down[1], vector_row('dec_ffn_bias'))
    final = norm_layer(dec_u3 + dec_ffn, vector_row('dec_norm3_gain'), vector_row('dec_norm3_bias'))
    block_of = (jnp.arange(N_CTX * COMP) // COMP).astype(jnp.int32)
    rows_at = (completion_idx + block_of * TOK_DEV).astype(jnp.int32)
    picked = low(final[rows_at])
    labels_at = target_labels[rows_at]
    logits = low_back(product(picked, table[:V].T))
    logsum = jax.nn.logsumexp(logits, axis=-1)
    label_logit = jnp.take_along_axis(logits, labels_at[:, None], axis=1)[:, 0]
    return jnp.sum(logsum - label_logit)

def adam_step(weight, moment, square, grad, decay, rate):
    new_moment = BETA_ONE * moment + (1.0 - BETA_ONE) * grad
    new_square = BETA_TWO * square + (1.0 - BETA_TWO) * grad * grad
    direction = new_moment / (1.0 - BETA_ONE ** STEP) / (jnp.sqrt(new_square / (1.0 - BETA_TWO ** STEP)) + ADAM_EPS)
    return (new_moment, new_square, weight - rate * (direction + decay * weight))

def reference(table_weight, table_moment, table_square, position_weight, position_moment, position_square, wide_weight, wide_moment, wide_square, down_weight, down_moment, down_square, vector_weight, vector_moment, vector_square, source_ids, target_ids, target_labels, source_segments, target_segments, completion_idx):
    count = SEQS * N_CTX * COMP
    data = (source_ids, target_ids, target_labels, source_segments, target_segments, completion_idx)

    def loss_fn(table, positions, wide, down, vectors):
        params = (low(table), low(positions), low(wide), low(down), vectors)
        losses = lax.map(jax.checkpoint(partial(pair_loss, params)), data)
        total = jnp.sum(losses)
        return (total / count, total)
    scaled, back_fn, loss_sum = jax.vjp(loss_fn, table_weight, position_weight, wide_weight, down_weight, vector_weight, has_aux=True)
    grads = back_fn(jnp.ones((), scaled.dtype))
    square_sum = sum((jnp.sum(grad * grad) for grad in grads))
    grad_norm = jnp.sqrt(square_sum)
    clip = jnp.minimum(1.0, CLIP_LIMIT / (grad_norm + 1e-06))
    states = [(table_weight, table_moment, table_square, WEIGHT_DECAY, LEARN_RATE), (position_weight, position_moment, position_square, WEIGHT_DECAY, LEARN_RATE), (wide_weight, wide_moment, wide_square, WEIGHT_DECAY, LEARN_RATE), (down_weight, down_moment, down_square, WEIGHT_DECAY, LEARN_RATE), (vector_weight, vector_moment, vector_square, 0.0, VECTOR_RATE)]
    results = []
    for (weight, moment, square, decay, rate), grad in zip(states, grads):
        results.extend(adam_step(weight, moment, square, grad * clip, decay, rate))
    return (loss_sum, grad_norm, results[0], results[1], results[2], results[3], results[4], results[5], results[6], results[7], results[8], results[9], results[10], results[11], results[12], results[13], results[14])
```

```python
import jax
import jax.numpy as jnp
from jax import lax
from jax.sharding import Mesh
from jax.sharding import PartitionSpec as P

H = 12
V = 50265
STEP = 10


PRECISE = lax.Precision.HIGHEST
NORM_EPS = 1e-05
LEARN_RATE = 0.03
VECTOR_RATE = 0.3
BETA_ONE = 0.9
BETA_TWO = 0.999
ADAM_EPS = 1e-08
WEIGHT_DECAY = 0.01
CLIP_LIMIT = 0.05
MASKED_SCORE = -1e30
VEC_NAMES = [
    "enc_norm0_gain",
    "enc_norm0_bias",
    "enc_query_bias",
    "enc_value_bias",
    "enc_out_bias",
    "enc_norm1_gain",
    "enc_norm1_bias",
    "enc_ffn_bias",
    "enc_norm2_gain",
    "enc_norm2_bias",
    "dec_norm0_gain",
    "dec_norm0_bias",
    "dec_query_bias",
    "dec_value_bias",
    "dec_out_bias",
    "dec_norm1_gain",
    "dec_norm1_bias",
    "cross_query_bias",
    "cross_value_bias",
    "cross_out_bias",
    "dec_norm2_gain",
    "dec_norm2_bias",
    "dec_ffn_bias",
    "dec_norm3_gain",
    "dec_norm3_bias",
]


def product(left, right):
    return jnp.dot(left, right, preferred_element_type=jnp.float32)


def product_t(left, right):
    return lax.dot_general(
        left, right, (((1,), (1,)), ((), ())), preferred_element_type=jnp.float32
    )


def row_contract(left, right):
    return lax.dot_general(
        left, right, (((0,), (0,)), ((), ())), preferred_element_type=jnp.float32
    )


def norm_layer(values, gain, bias):
    center = values - jnp.mean(values, -1, keepdims=True)
    spread = jnp.mean(center * center, -1, keepdims=True)
    return center * lax.rsqrt(spread + NORM_EPS) * gain + bias


def gelu_exact(values):
    return jax.nn.gelu(values, approximate=False)


def doc_positions(segment, limit):
    length = segment.shape[0]
    places = jnp.arange(length, dtype=jnp.int32)
    change = jnp.concatenate([jnp.ones((1,), bool), segment[1:] != segment[:-1]])
    starts = lax.cummax(jnp.where(change, places, 0), axis=0)
    return jnp.minimum(places - starts, limit - 1)


def combine_partial(first, second):
    top_value = jnp.maximum(first[0], second[0])
    sum_value = first[1] * jnp.exp(first[0] - top_value) + second[1] * jnp.exp(
        second[0] - top_value
    )
    return (top_value, sum_value, first[2] + second[2])


def project_queries(inputs_b, weight_q, bias_q):
    return ((product(inputs_b, weight_q) + bias_q) * 0.125).astype(jnp.bfloat16)


def project_pairs(inputs_b, weight_k, weight_v, bias_v):
    return (
        product(inputs_b, weight_k).astype(jnp.bfloat16),
        (product(inputs_b, weight_v) + bias_v).astype(jnp.bfloat16),
    )


def query_backward(inputs_b, weight_q, grad_query):
    return (
        row_contract(inputs_b, grad_query),
        jnp.sum(grad_query.astype(jnp.float32), 0),
        product_t(grad_query, weight_q),
    )


def pairs_backward(inputs_b, weight_k, weight_v, grad_keys, grad_values):
    keys_grad = grad_keys.astype(jnp.bfloat16)
    values_grad = grad_values.astype(jnp.bfloat16)
    return (
        row_contract(inputs_b, keys_grad),
        row_contract(inputs_b, values_grad),
        jnp.sum(values_grad.astype(jnp.float32), 0),
        product_t(keys_grad, weight_k) + product_t(values_grad, weight_v),
    )


def attention_scores(queries, keys_b, allowed, head_count):
    query_rows = queries.shape[0]
    key_rows = keys_b.shape[0]
    head_size = queries.shape[1] // head_count
    scores = jnp.einsum(
        "thd,shd->hts",
        queries.reshape(query_rows, head_count, head_size),
        keys_b.reshape(key_rows, head_count, head_size),
        preferred_element_type=jnp.float32,
    )
    return jnp.where(allowed[None], scores, MASKED_SCORE)


def branch_forward(queries, keys_b, values_b, allowed, weight_o, bias_o, head_count):
    query_rows = queries.shape[0]
    key_rows = keys_b.shape[0]
    head_size = queries.shape[1] // head_count
    scores = attention_scores(queries, keys_b, allowed, head_count)
    row_top = jnp.max(scores, -1, keepdims=True)
    exp_terms = jnp.exp(scores - row_top)
    row_sum = jnp.sum(exp_terms, -1, keepdims=True)
    logsum = row_top + jnp.log(row_sum)
    attn_probs = (exp_terms / row_sum).astype(jnp.bfloat16)
    mixed_out = jnp.einsum(
        "hts,shd->thd",
        attn_probs,
        values_b.reshape(key_rows, head_count, head_size),
        preferred_element_type=jnp.float32,
    )
    mixed_b = mixed_out.reshape(query_rows, -1).astype(jnp.bfloat16)
    return (product(mixed_b, weight_o) + bias_o, mixed_b, logsum)


def branch_backward(
    grad_branch, queries, keys_b, values_b, allowed, logsum, mixed_b, weight_o, head_count
):
    query_rows = queries.shape[0]
    key_rows = keys_b.shape[0]
    head_size = queries.shape[1] // head_count
    branch_grad = grad_branch.astype(jnp.bfloat16)
    grad_weight_o = row_contract(mixed_b, branch_grad)
    grad_bias_o = jnp.sum(branch_grad.astype(jnp.float32), 0)
    grad_mixed = (
        product_t(branch_grad, weight_o)
        .astype(jnp.bfloat16)
        .reshape(query_rows, head_count, head_size)
    )
    scores = attention_scores(queries, keys_b, allowed, head_count)
    attn_probs = jnp.exp(scores - logsum)
    value_split = values_b.reshape(key_rows, head_count, head_size)
    grad_values = jnp.einsum(
        "hts,thd->shd",
        attn_probs.astype(jnp.bfloat16),
        grad_mixed,
        preferred_element_type=jnp.float32,
    )
    grad_probs = jnp.einsum(
        "thd,shd->hts", grad_mixed, value_split, preferred_element_type=jnp.float32
    )
    grad_scores = attn_probs * (grad_probs - jnp.sum(grad_probs * attn_probs, -1, keepdims=True))
    scores_grad = grad_scores.astype(jnp.bfloat16)
    grad_queries = jnp.einsum(
        "hts,shd->thd",
        scores_grad,
        keys_b.reshape(key_rows, head_count, head_size),
        preferred_element_type=jnp.float32,
    )
    grad_keys = jnp.einsum(
        "hts,thd->shd",
        scores_grad,
        queries.reshape(query_rows, head_count, head_size),
        preferred_element_type=jnp.float32,
    )
    query_grad = grad_queries.reshape(query_rows, -1).astype(jnp.bfloat16) * jnp.bfloat16(0.125)
    return (
        query_grad,
        grad_keys.reshape(key_rows, -1),
        grad_values.reshape(key_rows, -1),
        grad_weight_o,
        grad_bias_o,
    )


def feed_forward(inputs_b, first_weight, first_bias, second_weight, second_bias):
    pre_act = product(inputs_b, first_weight) + first_bias
    act_b = gelu_exact(pre_act).astype(jnp.bfloat16)
    return (product(act_b, second_weight) + second_bias, pre_act, act_b)


def feed_backward(grad_branch, inputs_b, pre_act, act_b, first_weight, second_weight):
    branch_grad = grad_branch.astype(jnp.bfloat16)
    grad_second = row_contract(act_b, branch_grad)
    grad_second_bias = jnp.sum(branch_grad.astype(jnp.float32), 0)
    grad_act = product_t(branch_grad, second_weight)
    grad_pre = jax.vjp(gelu_exact, pre_act)[1](grad_act)[0].astype(jnp.bfloat16)
    grad_first = row_contract(inputs_b, grad_pre)
    grad_first_bias = jnp.sum(grad_pre.astype(jnp.float32), 0)
    return (
        product_t(grad_pre, first_weight),
        grad_first,
        grad_first_bias,
        grad_second,
        grad_second_bias,
    )


def adam_step(weight, moment, square, grad, decay, rate):
    new_moment = BETA_ONE * moment + (1.0 - BETA_ONE) * grad
    new_square = BETA_TWO * square + (1.0 - BETA_TWO) * grad * grad
    direction = (
        new_moment
        / (1.0 - BETA_ONE**STEP)
        / (jnp.sqrt(new_square / (1.0 - BETA_TWO**STEP)) + ADAM_EPS)
    )
    return (new_moment, new_square, weight - rate * (direction + decay * weight))


ALL = ("q", "p", "z", "x", "c")
SWAP = [(0, 1), (1, 0)]
SLOTS = 48


def swapped(part, axis):
    return lax.ppermute(part, axis, SWAP)


def one_hot(places, count):
    return (places[:, None] == jnp.arange(count, dtype=places.dtype)[None, :]).astype(jnp.bfloat16)


def shifted(part, axis, step):
    count = lax.axis_size(axis)
    return lax.ppermute(part, axis, [(i, (i + step) % count) for i in range(count)])


def line_in(part, axis):
    count = lax.axis_size(axis)
    return jnp.stack([part] + [shifted(part, axis, count - k) for k in range(1, count)])


def pair_in(part, axis, at):
    return jnp.stack([part, swapped(part, axis)], at)


def group_in(part, first):
    part = line_in(line_in(part, "p"), "z")
    if first == "q":
        part = pair_in(pair_in(part, "q", 0), "x", 0)
    else:
        part = pair_in(pair_in(part, "x", 0), "q", 1)
    return part


def group_rows(rows):
    half = rows.shape[1] // 2
    both = [group_in(rows[:, :half], "q"), group_in(rows[:, half:], "x")]
    return jnp.concatenate(both, -1).reshape(-1, rows.shape[1])


def send_half(part, axis, at):
    own = lax.index_in_dim(part, 0, at, keepdims=False)
    other = lax.index_in_dim(part, 1, at, keepdims=False)
    return own + swapped(other.astype(jnp.bfloat16), axis).astype(jnp.float32)


def send_line(part, axis):
    total = part[0]
    for k in range(1, lax.axis_size(axis)):
        total = total + shifted(part[k].astype(jnp.bfloat16), axis, k).astype(jnp.float32)
    return total


def group_sum(rows):
    ways = (2, 2, lax.axis_size("z"), lax.axis_size("p"))
    rows = rows.reshape(ways + (-1, rows.shape[-1]))
    half = rows.shape[-1] // 2
    first, second = rows[..., :half], rows[..., half:]
    first = send_half(send_half(first, "x", 0), "q", 0)
    second = send_half(send_half(second, "q", 1), "x", 0)
    return jnp.concatenate([send_line(send_line(part, "z"), "p") for part in (first, second)], -1)


def merge_stats(stats):

    def merge(first, second):
        return jnp.stack(combine_partial(first, second))

    ways = (2, 2, lax.axis_size("z"), lax.axis_size("p"))
    stats = stats.reshape((3,) + ways + (-1,))
    stats = merge(stats[:, 0], swapped(stats[:, 1], "x"))
    stats = merge(stats[:, 0], swapped(stats[:, 1], "q"))
    for axis in ("z", "p"):
        total = stats[:, 0]
        for k in range(1, lax.axis_size(axis)):
            total = merge(total, shifted(stats[:, k], axis, k))
        stats = total
    return stats


def own_half(part, axis, at):
    index = lax.axis_index(axis)
    first = lax.index_in_dim(part, 0, at, keepdims=False)
    second = lax.index_in_dim(part, 1, at, keepdims=False)
    return jnp.where(index == 0, first, second), jnp.where(index == 0, second, first)


def sum_to_shards(grad):
    lines = lax.axis_size("z")
    grad = grad.reshape((lines, 2, 2, -1) + grad.shape[1:])
    own, other = own_half(grad, "c", 2)
    grad = own + swapped(other, "c")
    own, other = own_half(grad, "x", 1)
    grad = own + swapped(other.astype(jnp.bfloat16), "x").astype(jnp.float32)
    here = lax.axis_index("z")
    total = lax.dynamic_index_in_dim(grad, here, 0, keepdims=False)
    for k in range(1, lines):
        sent = lax.dynamic_index_in_dim(grad, (here + k) % lines, 0, keepdims=False)
        total = total + shifted(sent.astype(jnp.bfloat16), "z", k).astype(jnp.float32)
    return total


def sum_columns(grad):
    if lax.axis_size("p") > 1:
        return lax.psum_scatter(grad, ("q", "p"), scatter_dimension=1, tiled=True)
    own, other = own_half(grad.reshape(grad.shape[0], 2, -1), "q", 1)
    return own + swapped(other, "q")


def sum_units(units, total_width):
    ctx_count = lax.axis_size("q") * lax.axis_size("p")
    span = total_width // ctx_count
    units = sorted(units, key=lambda unit: unit[0])
    if ctx_count > 2 or any(start // span != (start + part.shape[1] - 1) // span for start, part in units):
        return sum_columns(jnp.concatenate([part for _, part in units], 1))
    sides = ([], [])
    for start, part in units:
        side = start // span
        sides[side].append(part + lax.ppermute(part, "q", [(1 - side, side)]))
    return jnp.where(lax.axis_index("q") == 0, jnp.concatenate(sides[0], 1), jnp.concatenate(sides[1], 1))


def keys_in(parts):

    def gather(part):
        both = jnp.concatenate([part, swapped(part, "c")], 0)
        if lax.axis_size("p") > 1:
            both = lax.all_gather(both, "p", axis=0, tiled=True)
        return both

    return jax.tree.map(gather, parts)


def keys_back(parts):

    def scatter(part):
        if lax.axis_size("p") > 1:
            part = lax.psum_scatter(part, "p", scatter_dimension=0, tiled=True)
        half = part.shape[0] // 2
        return part[:half] + swapped(part[half:], "c")

    return jax.tree.map(scatter, parts)


class Lookup:
    def __init__(self, token_ids, own_rows):
        owners = 1
        for axis in ALL:
            owners *= lax.axis_size(axis)
        self.owners = owners
        self.own_rows = own_rows
        count = token_ids.shape[0]
        places = jnp.arange(count, dtype=jnp.int32)
        owner = token_ids // own_rows
        same = token_ids[:, None] == token_ids[None, :]
        first = jnp.min(jnp.where(same, places[None, :], count), 1)
        is_first = first == places
        ahead = (owner[:, None] == owner[None, :]) & is_first[None, :] & (places[None, :] < first[:, None])
        self.rank = jnp.sum(ahead.astype(jnp.int32), 1)
        self.owner = owner
        self.is_first = is_first
        self.local_id = token_ids - owner * own_rows
        self.rounds = lax.pmax(jnp.max(self.rank) // SLOTS + 1, ALL)

    def round_places(self, turn):
        rank = self.rank - turn * SLOTS
        inside = (rank >= 0) & (rank < SLOTS)
        slot = jnp.where(inside, self.owner * SLOTS + rank, -1)
        to_owner = jnp.where(
            (self.owner[:, None] == jnp.arange(self.owners)[None, :]) & self.is_first[:, None],
            (self.local_id + 1).astype(jnp.float32)[:, None],
            0.0,
        )
        to_slot = (rank[:, None] == jnp.arange(SLOTS)[None, :]).astype(jnp.float32)
        asked = lax.dot_general(to_owner, to_slot, (((0,), (0,)), ((), ())), precision=PRECISE)
        asked = jnp.round(asked).astype(jnp.int32) - 1
        wanted = lax.all_to_all(asked, ALL, 0, 0, tiled=True).reshape(-1)
        return one_hot(slot, self.owners * SLOTS), one_hot(wanted, self.own_rows)

    def fetch_round(self, turn, table_low):
        to_slot, to_row = self.round_places(turn)
        sent = product(to_row, table_low).astype(jnp.bfloat16)
        rows = lax.all_to_all(sent, ALL, 0, 0, tiled=True)
        return product(to_slot, rows), (to_slot, to_row)

    def fetch(self, table_low):
        rows, self.kept = self.fetch_round(0, table_low)
        return lax.fori_loop(
            1, self.rounds, lambda turn, total: total + self.fetch_round(turn, table_low)[0], rows
        )

    def give_round(self, places, grads_b):
        to_slot, to_row = places
        sent = row_contract(to_slot, grads_b).astype(jnp.bfloat16)
        back = lax.all_to_all(sent, ALL, 0, 0, tiled=True)
        return row_contract(to_row, back)

    def give(self, grads_b):
        grad = self.give_round(self.kept, grads_b)
        return lax.fori_loop(
            1,
            self.rounds,
            lambda turn, total: total + self.give_round(self.round_places(turn), grads_b),
            grad,
        )


def local(
    table_weight,
    table_moment,
    table_square,
    position_weight,
    position_moment,
    position_square,
    wide_weight,
    wide_moment,
    wide_square,
    down_weight,
    down_moment,
    down_square,
    vector_weight,
    vector_moment,
    vector_square,
    source_ids,
    target_ids,
    target_labels,
    source_segments,
    target_segments,
    completion_idx,
):
    cuts = lax.axis_size("p")
    ctx_count = 2 * cuts
    shard_count = lax.axis_size("z") * 4
    core = lax.axis_index("c")
    block = lax.axis_index("p") * 2 + core
    tokens = source_ids.shape[1]
    comp_count = completion_idx.shape[1]
    width = vector_weight.shape[1]
    hidden = down_weight.shape[1] * shard_count
    head_count = H
    own_rows = table_weight.shape[0]
    table_low = table_weight.astype(jnp.bfloat16)

    small = jnp.concatenate(
        [source_ids, target_ids, target_labels, source_segments, target_segments, completion_idx], 1
    )
    small = lax.all_gather(small[0], ("q", "p", "c"))
    small = small.reshape(ctx_count, 2, -1)
    small = lax.dynamic_index_in_dim(small, lax.axis_index("q"), 1, keepdims=False)
    src_ids, tgt_ids, tgt_labels, src_seg, tgt_seg = (
        small[:, k * tokens : (k + 1) * tokens] for k in range(5)
    )

    def own_block(blocks):
        return lax.dynamic_index_in_dim(blocks, block, 0, keepdims=False)

    def key_order(blocks):
        pairs = blocks.reshape(cuts, 2, -1)
        return jnp.where(core == 0, pairs, pairs[:, ::-1]).reshape(-1)

    comp_places = own_block(small[:, 5 * tokens :])
    comp_hit = one_hot(comp_places, tokens)
    own_labels = jnp.take(own_block(tgt_labels), comp_places)
    head_labels = group_in(own_labels, "q").reshape(-1)

    lookup = Lookup(jnp.concatenate([own_block(src_ids), own_block(tgt_ids)]), own_rows)
    token_rows = lookup.fetch(table_low)

    wide_low = wide_weight.astype(jnp.bfloat16)
    down_low = down_weight.astype(jnp.bfloat16)
    shard_rows, span = wide_low.shape
    bounds = [0, span * 2 // 5, span * 4 // 5, span]
    place_pack = position_weight.astype(jnp.bfloat16).reshape(shard_rows, -1)
    extra = place_pack.shape[1]

    def gathered(part):
        return lax.all_gather(part, ALL)

    def spread(part):
        return part.reshape(ctx_count, width, part.shape[-1])

    pack = gathered(jnp.concatenate([wide_low[:, : bounds[1]], place_pack], 1))
    chunks = [spread(pack[..., : bounds[1]])]
    position_full = pack[..., bounds[1] :].reshape(
        (ctx_count, shard_count) + position_weight.shape
    )
    position_full = jnp.moveaxis(position_full, 0, 2).reshape(-1, width)
    chunks.append(spread(gathered(wide_low[:, bounds[1] : bounds[2]])))

    def down_full(part):
        part = gathered(part).reshape((ctx_count, shard_count) + part.shape)
        return jnp.moveaxis(part, 0, 2).reshape(hidden, width)

    enc_second = down_full(down_low[0])
    chunks.append(spread(gathered(wide_low[:, bounds[2] :])))
    dec_second = down_full(down_low[1])

    def columns(start, size):
        pieces = []
        while size:
            side, inner = divmod(start, span)
            turn = max(k for k in range(3) if bounds[k] <= inner)
            take = min(size, bounds[turn + 1] - inner)
            at = inner - bounds[turn]
            pieces.append(chunks[turn][side, :, at : at + take])
            start, size = start + take, size - take
        return pieces[0] if len(pieces) == 1 else jnp.concatenate(pieces, 1)

    def vector_row(name):
        return vector_weight[VEC_NAMES.index(name)]

    blocks = hidden // width
    base_row = len(VEC_NAMES)
    enc_first_bias = vector_weight[base_row : base_row + blocks].reshape(-1)
    dec_first_bias = vector_weight[base_row + blocks : base_row + 2 * blocks].reshape(-1)
    names = (
        "enc_wq enc_wk enc_wv enc_out enc_first dec_wq dec_wk dec_wv dec_out "
        "cross_wq cross_wk cross_wv cross_out dec_first"
    ).split()
    starts, offset = {}, 0
    for name in names:
        starts[name] = offset
        offset += hidden if name.endswith("first") else width
    full = {
        name: columns(starts[name], hidden if name.endswith("first") else width) for name in names
    }

    table_count = position_full.shape[0]
    src_pos = own_block(doc_positions(src_seg.reshape(-1), table_count).reshape(ctx_count, -1))
    tgt_pos = own_block(doc_positions(tgt_seg.reshape(-1), table_count).reshape(ctx_count, -1))
    src_onehot = one_hot(src_pos, table_count)
    tgt_onehot = one_hot(tgt_pos, table_count)
    src_input = token_rows[:tokens] + product(src_onehot, position_full)
    tgt_input = token_rows[tokens:] + product(tgt_onehot, position_full)

    query_places = block * tokens + jnp.arange(tokens)
    key_places = key_order(jnp.arange(ctx_count * tokens).reshape(ctx_count, tokens))
    src_keys_seg = key_order(src_seg)
    tgt_keys_seg = key_order(tgt_seg)
    own_src_seg = own_block(src_seg)
    own_tgt_seg = own_block(tgt_seg)
    enc_allowed = own_src_seg[:, None] == src_keys_seg[None, :]
    self_allowed = (own_tgt_seg[:, None] == tgt_keys_seg[None, :]) & (
        query_places[:, None] >= key_places[None, :]
    )
    cross_allowed = own_tgt_seg[:, None] == src_keys_seg[None, :]

    enc_norm0, enc_back0 = jax.vjp(
        norm_layer, src_input, vector_row("enc_norm0_gain"), vector_row("enc_norm0_bias")
    )
    enc_in_b = enc_norm0.astype(jnp.bfloat16)
    enc_queries = project_queries(enc_in_b, full["enc_wq"], vector_row("enc_query_bias"))
    enc_keys, enc_values = project_pairs(
        enc_in_b, full["enc_wk"], full["enc_wv"], vector_row("enc_value_bias")
    )
    enc_keys_all, enc_values_all = keys_in((enc_keys, enc_values))
    enc_branch, enc_mixed_b, enc_logsum = branch_forward(
        enc_queries,
        enc_keys_all,
        enc_values_all,
        enc_allowed,
        full["enc_out"],
        vector_row("enc_out_bias"),
        head_count,
    )
    enc_norm1, enc_back1 = jax.vjp(
        norm_layer,
        enc_norm0 + enc_branch,
        vector_row("enc_norm1_gain"),
        vector_row("enc_norm1_bias"),
    )
    enc_mid_b = enc_norm1.astype(jnp.bfloat16)
    enc_ffn, enc_pre, enc_act_b = feed_forward(
        enc_mid_b, full["enc_first"], enc_first_bias, enc_second, vector_row("enc_ffn_bias")
    )
    encoded, enc_back2 = jax.vjp(
        norm_layer, enc_norm1 + enc_ffn, vector_row("enc_norm2_gain"), vector_row("enc_norm2_bias")
    )
    dec_norm0, dec_back0 = jax.vjp(
        norm_layer, tgt_input, vector_row("dec_norm0_gain"), vector_row("dec_norm0_bias")
    )
    dec_in_b = dec_norm0.astype(jnp.bfloat16)
    dec_queries = project_queries(dec_in_b, full["dec_wq"], vector_row("dec_query_bias"))
    dec_keys, dec_values = project_pairs(
        dec_in_b, full["dec_wk"], full["dec_wv"], vector_row("dec_value_bias")
    )
    dec_keys_all, dec_values_all = keys_in((dec_keys, dec_values))
    self_branch, self_mixed_b, self_logsum = branch_forward(
        dec_queries,
        dec_keys_all,
        dec_values_all,
        self_allowed,
        full["dec_out"],
        vector_row("dec_out_bias"),
        head_count,
    )
    dec_norm1, dec_back1 = jax.vjp(
        norm_layer,
        dec_norm0 + self_branch,
        vector_row("dec_norm1_gain"),
        vector_row("dec_norm1_bias"),
    )
    cross_in_b = dec_norm1.astype(jnp.bfloat16)
    cross_queries = project_queries(cross_in_b, full["cross_wq"], vector_row("cross_query_bias"))
    encoded_b = encoded.astype(jnp.bfloat16)
    cross_keys, cross_values = project_pairs(
        encoded_b, full["cross_wk"], full["cross_wv"], vector_row("cross_value_bias")
    )
    cross_keys_all, cross_values_all = keys_in((cross_keys, cross_values))
    cross_branch, cross_mixed_b, cross_logsum = branch_forward(
        cross_queries,
        cross_keys_all,
        cross_values_all,
        cross_allowed,
        full["cross_out"],
        vector_row("cross_out_bias"),
        head_count,
    )
    dec_norm2, dec_back2 = jax.vjp(
        norm_layer,
        dec_norm1 + cross_branch,
        vector_row("dec_norm2_gain"),
        vector_row("dec_norm2_bias"),
    )
    dec_mid_b = dec_norm2.astype(jnp.bfloat16)
    dec_ffn, dec_pre, dec_act_b = feed_forward(
        dec_mid_b, full["dec_first"], dec_first_bias, dec_second, vector_row("dec_ffn_bias")
    )
    final, dec_back3 = jax.vjp(
        norm_layer, dec_norm2 + dec_ffn, vector_row("dec_norm3_gain"), vector_row("dec_norm3_bias")
    )
    final_b = final.astype(jnp.bfloat16)

    head_rows = group_rows(product(comp_hit, final_b).astype(jnp.bfloat16))
    table_pair = jnp.concatenate([table_low, swapped(table_low, "c")], 0)
    group_start = 0
    for axis in ("q", "p", "z", "x"):
        group_start = group_start * lax.axis_size(axis) + lax.axis_index(axis)
    own_ids = jnp.arange(own_rows, dtype=jnp.int32)
    column_ids = jnp.concatenate(
        [(group_start * 2 + core) * own_rows + own_ids, (group_start * 2 + 1 - core) * own_rows + own_ids]
    )
    label_hit = column_ids[None, :] == head_labels[:, None]
    logits = jnp.where(column_ids[None, :] < V, product_t(head_rows, table_pair), MASKED_SCORE)
    row_top = jnp.max(logits, -1)
    row_sum = jnp.sum(jnp.exp(logits - row_top[:, None]), -1)
    label_logit = jnp.sum(jnp.where(label_hit, logits, 0.0), -1)
    merged_top, merged_sum, merged_label = merge_stats(jnp.stack([row_top, row_sum, label_logit]))
    own_logsum = merged_top + jnp.log(merged_sum)
    loss_local = jnp.sum(own_logsum - merged_label)
    logsum_rows = group_in(own_logsum, "q").reshape(-1)
    loss_scale = 1.0 / (comp_count * ctx_count * shard_count)
    head_probs = jnp.exp(logits - logsum_rows[:, None])
    grad_logits = ((head_probs - label_hit.astype(jnp.float32)) * loss_scale).astype(jnp.bfloat16)
    grad_picked = group_sum(product(grad_logits, table_pair))
    table_grad = row_contract(grad_logits, head_rows)
    table_grad = table_grad[:own_rows] + swapped(table_grad[own_rows:], "c")
    grad_final = lax.dot_general(
        comp_hit.astype(jnp.float32), grad_picked, (((0,), (0,)), ((), ())), precision=PRECISE
    )

    vector_grads = {}
    units = []

    def add_unit(name, grad):
        units.append((starts[name], sum_to_shards(grad)))

    grad_sum3, vector_grads["dec_norm3_gain"], vector_grads["dec_norm3_bias"] = dec_back3(
        grad_final
    )
    grad_mid, dec_first_g, dec_first_bias_g, dec_second_g, vector_grads["dec_ffn_bias"] = (
        feed_backward(grad_sum3, dec_mid_b, dec_pre, dec_act_b, full["dec_first"], dec_second)
    )
    dec_second_own = sum_columns(sum_to_shards(dec_second_g))
    add_unit("dec_first", dec_first_g)
    grad_sum2, vector_grads["dec_norm2_gain"], vector_grads["dec_norm2_bias"] = dec_back2(
        grad_sum3 + grad_mid
    )
    (
        cross_query_grad,
        cross_keys_grad,
        cross_values_grad,
        cross_out_g,
        vector_grads["cross_out_bias"],
    ) = branch_backward(
        grad_sum2,
        cross_queries,
        cross_keys_all,
        cross_values_all,
        cross_allowed,
        cross_logsum,
        cross_mixed_b,
        full["cross_out"],
        head_count,
    )
    cross_keys_own, cross_values_own = keys_back((cross_keys_grad, cross_values_grad))
    add_unit("cross_out", cross_out_g)
    cross_query_g, vector_grads["cross_query_bias"], grad_cross_in = query_backward(
        cross_in_b, full["cross_wq"], cross_query_grad
    )
    add_unit("cross_wq", cross_query_g)
    cross_wk_g, cross_wv_g, vector_grads["cross_value_bias"], grad_encoded = pairs_backward(
        encoded_b, full["cross_wk"], full["cross_wv"], cross_keys_own, cross_values_own
    )
    add_unit("cross_wk", cross_wk_g)
    add_unit("cross_wv", cross_wv_g)
    grad_sum1, vector_grads["dec_norm1_gain"], vector_grads["dec_norm1_bias"] = dec_back1(
        grad_sum2 + grad_cross_in
    )
    dec_query_grad, dec_keys_grad, dec_values_grad, dec_out_g, vector_grads["dec_out_bias"] = (
        branch_backward(
            grad_sum1,
            dec_queries,
            dec_keys_all,
            dec_values_all,
            self_allowed,
            self_logsum,
            self_mixed_b,
            full["dec_out"],
            head_count,
        )
    )
    add_unit("dec_out", dec_out_g)
    dec_keys_own, dec_values_own = keys_back((dec_keys_grad, dec_values_grad))
    dec_wq_g, vector_grads["dec_query_bias"], grad_dec_q_in = query_backward(
        dec_in_b, full["dec_wq"], dec_query_grad
    )
    dec_wk_g, dec_wv_g, vector_grads["dec_value_bias"], grad_dec_kv_in = pairs_backward(
        dec_in_b, full["dec_wk"], full["dec_wv"], dec_keys_own, dec_values_own
    )
    add_unit("dec_wq", dec_wq_g)
    add_unit("dec_wk", dec_wk_g)
    add_unit("dec_wv", dec_wv_g)
    grad_tgt_input, vector_grads["dec_norm0_gain"], vector_grads["dec_norm0_bias"] = dec_back0(
        grad_sum1 + grad_dec_q_in + grad_dec_kv_in
    )
    grad_enc2, vector_grads["enc_norm2_gain"], vector_grads["enc_norm2_bias"] = enc_back2(
        grad_encoded
    )
    grad_enc_mid, enc_first_g, enc_first_bias_g, enc_second_g, vector_grads["enc_ffn_bias"] = (
        feed_backward(grad_enc2, enc_mid_b, enc_pre, enc_act_b, full["enc_first"], enc_second)
    )
    enc_second_own = sum_columns(sum_to_shards(enc_second_g))
    add_unit("enc_first", enc_first_g)
    grad_enc1, vector_grads["enc_norm1_gain"], vector_grads["enc_norm1_bias"] = enc_back1(
        grad_enc2 + grad_enc_mid
    )
    enc_query_grad, enc_keys_grad, enc_values_grad, enc_out_g, vector_grads["enc_out_bias"] = (
        branch_backward(
            grad_enc1,
            enc_queries,
            enc_keys_all,
            enc_values_all,
            enc_allowed,
            enc_logsum,
            enc_mixed_b,
            full["enc_out"],
            head_count,
        )
    )
    add_unit("enc_out", enc_out_g)
    enc_keys_own, enc_values_own = keys_back((enc_keys_grad, enc_values_grad))
    enc_wq_g, vector_grads["enc_query_bias"], grad_enc_q_in = query_backward(
        enc_in_b, full["enc_wq"], enc_query_grad
    )
    enc_wk_g, enc_wv_g, vector_grads["enc_value_bias"], grad_enc_kv_in = pairs_backward(
        enc_in_b, full["enc_wk"], full["enc_wv"], enc_keys_own, enc_values_own
    )
    add_unit("enc_wq", enc_wq_g)
    add_unit("enc_wk", enc_wk_g)
    add_unit("enc_wv", enc_wv_g)
    grad_src_input, vector_grads["enc_norm0_gain"], vector_grads["enc_norm0_bias"] = enc_back0(
        grad_enc1 + grad_enc_q_in + grad_enc_kv_in
    )
    table_grad = table_grad + lookup.give(
        jnp.concatenate(
            [grad_src_input.astype(jnp.bfloat16), grad_tgt_input.astype(jnp.bfloat16)], 0
        )
    )
    position_grad = lax.dot_general(
        src_onehot.astype(jnp.float32), grad_src_input, (((0,), (0,)), ((), ())), precision=PRECISE
    ) + lax.dot_general(
        tgt_onehot.astype(jnp.float32), grad_tgt_input, (((0,), (0,)), ((), ())), precision=PRECISE
    )
    position_grad = sum_columns(sum_to_shards(position_grad))
    wide_grad = sum_units(units, span * ctx_count)
    down_grad = jnp.stack([enc_second_own, dec_second_own])
    vector_grad = jnp.concatenate(
        [
            jnp.stack([vector_grads[name] for name in VEC_NAMES]),
            enc_first_bias_g.reshape(-1, width),
            dec_first_bias_g.reshape(-1, width),
        ],
        0,
    )
    vector_grad = lax.psum(vector_grad, ALL)
    owned_squares = (
        jnp.sum(wide_grad * wide_grad)
        + jnp.sum(down_grad * down_grad)
        + jnp.sum(position_grad * position_grad)
        + jnp.sum(table_grad * table_grad)
    )
    square_total, loss_sum = lax.psum((owned_squares, loss_local), ALL)
    grad_norm = jnp.sqrt(square_total + jnp.sum(vector_grad * vector_grad))
    clip_factor = jnp.minimum(1.0, CLIP_LIMIT / (grad_norm + 1e-06))
    outs = [loss_sum, grad_norm]
    for weight, moment, square, grad, decay, rate in (
        (table_weight, table_moment, table_square, table_grad, WEIGHT_DECAY, LEARN_RATE),
        (position_weight, position_moment, position_square, position_grad, WEIGHT_DECAY, LEARN_RATE),
        (wide_weight, wide_moment, wide_square, wide_grad, WEIGHT_DECAY, LEARN_RATE),
        (down_weight, down_moment, down_square, down_grad, WEIGHT_DECAY, LEARN_RATE),
        (vector_weight, vector_moment, vector_square, vector_grad, 0.0, VECTOR_RATE),
    ):
        outs.extend(adam_step(weight, moment, square, grad * clip_factor, decay, rate))
    return tuple(outs)


def solution(mesh):
    ctx_count, shard_count = mesh.devices.shape
    fine = Mesh(mesh.devices.reshape(2, ctx_count // 2, shard_count // 4, 2, 2), ALL)
    ctx, shard = ("q", "p"), ("z", "x", "c")
    table, plane, deep, whole = P(ALL, None), P(shard, ctx), P(None, shard, ctx), P()
    states = (table,) * 3 + (plane,) * 6 + (deep,) * 3 + (whole,) * 3
    return jax.shard_map(
        local,
        mesh=fine,
        in_specs=states + (plane,) * 6,
        out_specs=(whole, whole) + states,
        check_vma=False,
    )
```

```python
import functools
import math

import jax
import jax.numpy as jnp
from jax import lax
from jax.experimental import pallas as pl
from jax.experimental.pallas import tpu as pltpu
from jax.sharding import Mesh
from jax.sharding import PartitionSpec as P

H = 12
V = 50265
STEP = 10


PRECISE = lax.Precision.HIGHEST
NORM_EPS = 1e-05
LEARN_RATE = 0.03
VECTOR_RATE = 0.3
BETA_ONE = 0.9
BETA_TWO = 0.999
ADAM_EPS = 1e-08
WEIGHT_DECAY = 0.01
CLIP_LIMIT = 0.05
MASKED_SCORE = -1e30

class Row:
    (
        enc_norm0_gain,
        enc_norm0_bias,
        enc_query_bias,
        enc_value_bias,
        enc_out_bias,
        enc_norm1_gain,
        enc_norm1_bias,
        enc_ffn_bias,
        enc_norm2_gain,
        enc_norm2_bias,
        dec_norm0_gain,
        dec_norm0_bias,
        dec_query_bias,
        dec_value_bias,
        dec_out_bias,
        dec_norm1_gain,
        dec_norm1_bias,
        cross_query_bias,
        cross_value_bias,
        cross_out_bias,
        dec_norm2_gain,
        dec_norm2_bias,
        dec_ffn_bias,
        dec_norm3_gain,
        dec_norm3_bias,
    ) = range(25)


class Part:
    (
        enc_wq,
        enc_wk,
        enc_wv,
        enc_out,
        enc_first,
        dec_wq,
        dec_wk,
        dec_wv,
        dec_out,
        cross_wq,
        cross_wk,
        cross_wv,
        cross_out,
        dec_first,
        enc_second,
        dec_second,
        position,
    ) = range(17)


FIRSTS = (Part.enc_first, Part.dec_first)


def product(left, right):
    return jnp.dot(left, right, preferred_element_type=jnp.float32)


def product_t(left, right):
    return lax.dot_general(
        left, right, (((1,), (1,)), ((), ())), preferred_element_type=jnp.float32
    )


def row_contract(left, right):
    return lax.dot_general(
        left, right, (((0,), (0,)), ((), ())), preferred_element_type=jnp.float32
    )


NORMAL = (((1,), (0,)), ((), ()))
RIGHT_T = (((1,), (1,)), ((), ()))
LEFT_T = (((0,), (0,)), ((), ()))
KERNEL_BYTES = 48 * 2**20


def dot(left, right, dims):
    return lax.dot_general(left, right, dims, preferred_element_type=jnp.float32)


def norm_forward(values, gain, bias):
    center = values - jnp.mean(values, -1, keepdims=True)
    scale = lax.rsqrt(jnp.mean(center * center, -1, keepdims=True) + NORM_EPS)
    unit = center * scale
    return unit * gain + bias, (unit, scale)


def norm_backward(grad, saved, gain):
    unit, scale = saved
    grad_unit = grad * gain
    shift = jnp.mean(grad_unit, -1, keepdims=True)
    slope = jnp.mean(grad_unit * unit, -1, keepdims=True)
    return (
        scale * (grad_unit - shift - unit * slope),
        jnp.sum(grad * unit, 0, keepdims=True),
        jnp.sum(grad, 0, keepdims=True),
    )


def column_sums(part, dims=NORMAL):
    count = part.shape[dims[0][1][0]]
    return dot(jnp.ones((8, count), jnp.bfloat16), part, dims)[:1]


def doc_positions(segment, limit):
    length = segment.shape[0]
    places = jnp.arange(length, dtype=jnp.int32)
    change = jnp.concatenate([jnp.ones((1,), bool), segment[1:] != segment[:-1]])
    starts = lax.cummax(jnp.where(change, places, 0), axis=0)
    return jnp.minimum(places - starts, limit - 1)


def combine_partial(first, second):
    top_value = jnp.maximum(first[0], second[0])
    sum_value = first[1] * jnp.exp(first[0] - top_value) + second[1] * jnp.exp(
        second[0] - top_value
    )
    return (top_value, sum_value, first[2] + second[2])


def project_queries(inputs_b, weight_q, bias_q):
    return ((product(inputs_b, weight_q) + bias_q) * 0.125).astype(jnp.bfloat16)


def project_pairs(inputs_b, weight_pair, bias_v):
    bias = jnp.concatenate([jnp.zeros_like(bias_v), bias_v])
    return (product(inputs_b, weight_pair) + bias).astype(jnp.bfloat16)


def query_backward(weight_q, grad_query):
    return (column_sums(grad_query), product_t(grad_query, weight_q))


def pairs_backward(weight_pair, pairs_grad):
    width = pairs_grad.shape[2]
    return (
        column_sums(pairs_grad[1]),
        product_t(pairs_grad[0], weight_pair[:, :width])
        + product_t(pairs_grad[1], weight_pair[:, width:]),
    )


def feed_forward(inputs_b, first_weight, first_bias, second_weight, second_bias):
    pre_act = dot(first_weight, inputs_b, (((0,), (1,)), ((), ()))) + first_bias[:, None]
    share = 0.5 + 0.5 * lax.erf(pre_act * 0.5**0.5)
    act_b = (pre_act * share).astype(jnp.bfloat16)
    slope = share + pre_act * jnp.exp(-0.5 * pre_act * pre_act) * (0.5 / math.pi) ** 0.5
    return (dot(act_b, second_weight, LEFT_T) + second_bias, slope, act_b)


def feed_backward(grad_branch, slope, first_weight, second_weight):
    branch_grad = grad_branch.astype(jnp.bfloat16)
    grad_pre = (dot(second_weight, branch_grad, RIGHT_T) * slope).astype(jnp.bfloat16)
    return (
        dot(grad_pre, first_weight, (((0,), (1,)), ((), ()))),
        grad_pre,
        column_sums(grad_pre, RIGHT_T),
        branch_grad,
        column_sums(branch_grad),
    )


def adam_step(weight, moment, square, grad, decay, rate):
    new_moment = BETA_ONE * moment + (1.0 - BETA_ONE) * grad
    new_square = BETA_TWO * square + (1.0 - BETA_TWO) * grad * grad
    direction = (
        new_moment
        / (1.0 - BETA_ONE**STEP)
        / (jnp.sqrt(new_square / (1.0 - BETA_TWO**STEP)) + ADAM_EPS)
    )
    return (new_moment, new_square, weight - rate * (direction + decay * weight))


def fill_mask(query_ref, key_ref, mask_ref):

    @pl.when(pl.program_id(0) == 0)
    def _():
        allowed = (key_ref[:, 0:1] == query_ref[0:1, :]) & (key_ref[:, 1:2] <= query_ref[1:2, :])
        mask_ref[...] = jnp.where(allowed, 1.0, 0.0)


def attention_kernel(
    query_ref,
    key_ref,
    q_ref,
    k_own_ref,
    k_came_ref,
    v_own_ref,
    v_came_ref,
    out_ref,
    turned_ref,
    logsum_ref,
    mask_ref,
    *,
    head_size,
):
    fill_mask(query_ref, key_ref, mask_ref)
    half = k_own_ref.shape[0]
    outs = []
    for head in range(q_ref.shape[1] // head_size):
        lanes = slice(head * head_size, (head + 1) * head_size)
        q = q_ref[:, lanes]
        keys = jnp.concatenate([k_own_ref[:, lanes], k_came_ref[:, lanes]], 0)
        scores = jnp.where(mask_ref[...] != 0.0, dot(keys, q, RIGHT_T), MASKED_SCORE)
        top = jnp.max(scores, 0, keepdims=True)
        terms = jnp.exp(scores - top)
        total = jnp.sum(terms, 0, keepdims=True)
        probs = (terms * (1.0 / total)).astype(jnp.bfloat16)
        outs.append(
            dot(v_own_ref[:, lanes], probs[:half], LEFT_T)
            + dot(v_came_ref[:, lanes], probs[half:], LEFT_T)
        )
        logsum_ref[0, head : head + 1, :] = top + jnp.log(total)
    out = jnp.concatenate(outs, 0)
    turned_ref[...] = out.astype(jnp.bfloat16)
    out_ref[...] = out.T.astype(jnp.bfloat16)


def attention_back_kernel(
    query_ref,
    key_ref,
    q_ref,
    k_own_ref,
    k_came_ref,
    v_own_ref,
    v_came_ref,
    grad_ref,
    logsum_ref,
    grad_q_ref,
    own_ref,
    other_ref,
    mask_ref,
    *,
    head_size,
):
    fill_mask(query_ref, key_ref, mask_ref)
    half = k_own_ref.shape[0]
    q_parts, k_parts, v_parts = [], [], []
    for head in range(q_ref.shape[1] // head_size):
        lanes = slice(head * head_size, (head + 1) * head_size)
        q, grad = q_ref[:, lanes], grad_ref[:, lanes]
        keys = jnp.concatenate([k_own_ref[:, lanes], k_came_ref[:, lanes]], 0)
        values = jnp.concatenate([v_own_ref[:, lanes], v_came_ref[:, lanes]], 0)
        scores = jnp.where(mask_ref[...] != 0.0, dot(keys, q, RIGHT_T), MASKED_SCORE)
        probs = jnp.exp(scores - logsum_ref[0, head : head + 1, :])
        grad_probs = dot(values, grad, RIGHT_T)
        shift = jnp.sum(grad_probs * probs, 0, keepdims=True)
        grad_scores = (probs * (grad_probs - shift)).astype(jnp.bfloat16)
        v_parts.append(dot(probs.astype(jnp.bfloat16), grad, NORMAL))
        k_parts.append(dot(grad_scores, q, NORMAL))
        q_parts.append(dot(keys, grad_scores, LEFT_T))
    grad_q_ref[...] = jnp.concatenate(q_parts, 0).T.astype(jnp.bfloat16) * jnp.bfloat16(0.125)
    for at, parts in enumerate((k_parts, v_parts)):
        grad_pair = jnp.concatenate(parts, 1)
        own_ref[at] = grad_pair[:half]
        other_ref[at] = grad_pair[half:]


def attention_call(kernel, results, marks, head_count, products, queries, pairs, extra=()):
    query_rows, width = queries.shape
    own, came = pairs
    key_rows = own.shape[0]
    head_size = width // head_count
    per_step = max(1, 128 // head_size)
    steps = head_count // per_step
    lanes = per_step * head_size
    heads = pl.BlockSpec((query_rows, lanes), lambda i: (0, i))
    keys = pl.BlockSpec((key_rows, lanes), lambda i: (0, i))
    values = pl.BlockSpec((key_rows, lanes), lambda i: (0, i + steps))
    sums = pl.BlockSpec((1, per_step, query_rows), lambda i: (i, 0, 0))
    kinds = {
        "q": (heads, (query_rows, width), jnp.bfloat16),
        "t": (pl.BlockSpec((lanes, query_rows), lambda i: (i, 0)), (width, query_rows), jnp.bfloat16),
        "s": (sums, (steps, per_step, query_rows), jnp.float32),
        "p": (
            pl.BlockSpec((2, key_rows, lanes), lambda i: (0, 0, i)),
            (2, key_rows, width),
            jnp.float32,
        ),
    }
    count = 2 * query_rows * key_rows
    return pl.pallas_call(
        functools.partial(kernel, head_size=head_size),
        grid=(steps,),
        in_specs=[pl.BlockSpec(part.shape, lambda i: (0, 0)) for part in marks]
        + [heads, keys, keys, values, values]
        + [heads, sums][: len(extra)],
        out_specs=[kinds[kind][0] for kind in results],
        out_shape=[jax.ShapeDtypeStruct(*kinds[kind][1:]) for kind in results],
        scratch_shapes=[pltpu.VMEM((2 * key_rows, query_rows), jnp.float32)],
        compiler_params=pltpu.CompilerParams(vmem_limit_bytes=KERNEL_BYTES),
        cost_estimate=pl.CostEstimate(
            flops=2 * products * count * width,
            bytes_accessed=2 * width * (query_rows + 2 * key_rows) * products,
            transcendentals=count * head_count,
        ),
    )(*marks, queries, own, came, own, came, *extra)


def branch_forward(queries, pairs, marks, weight_o, bias_o, head_count):
    mixed_b, mixed_t, logsum = attention_call(
        attention_kernel, "qts", marks, head_count, 2, queries, pairs
    )
    return (product(mixed_b, weight_o) + bias_o, mixed_t, logsum)


def branch_backward(grad_branch, queries, pairs, marks, logsum, weight_o, head_count):
    branch_grad = grad_branch.astype(jnp.bfloat16)
    grad_mixed = product_t(branch_grad, weight_o).astype(jnp.bfloat16)
    query_grad, own, other = attention_call(
        attention_back_kernel, "qpp", marks, head_count, 5, queries, pairs, (grad_mixed, logsum)
    )
    return (query_grad, (own, other), branch_grad, column_sums(branch_grad))


ALL = ("q", "p", "z", "x", "c")
SWAP = [(0, 1), (1, 0)]
SLOTS = 40


def swapped(part, axis):
    return lax.ppermute(part, axis, SWAP)


def one_hot(places, count):
    return (places[:, None] == jnp.arange(count, dtype=places.dtype)[None, :]).astype(jnp.bfloat16)


def shifted(part, axis, step):
    count = lax.axis_size(axis)
    return lax.ppermute(part, axis, [(i, (i + step) % count) for i in range(count)])


def line_in(part, axis):
    count = lax.axis_size(axis)
    return jnp.stack([part] + [shifted(part, axis, count - k) for k in range(1, count)])


def pair_in(part, axis, at):
    return jnp.stack([part, swapped(part, axis)], at)


def group_in(part, first):
    part = line_in(line_in(part, "p"), "z")
    if first == "q":
        part = pair_in(pair_in(part, "q", 0), "x", 0)
    else:
        part = pair_in(pair_in(part, "x", 0), "q", 1)
    return part


def group_rows(rows):
    half = rows.shape[1] // 2
    both = [group_in(rows[:, :half], "q"), group_in(rows[:, half:], "x")]
    return jnp.concatenate(both, -1).reshape(-1, rows.shape[1])


def send_half(part, axis, at):
    own = lax.index_in_dim(part, 0, at, keepdims=False)
    other = lax.index_in_dim(part, 1, at, keepdims=False)
    return own + swapped(other.astype(jnp.bfloat16), axis).astype(jnp.float32)


def send_line(part, axis):
    total = part[0]
    for k in range(1, lax.axis_size(axis)):
        total = total + shifted(part[k].astype(jnp.bfloat16), axis, k).astype(jnp.float32)
    return total


def group_sum(rows):
    ways = (2, 2, lax.axis_size("z"), lax.axis_size("p"))
    rows = rows.reshape(ways + (-1, rows.shape[-1]))
    half = rows.shape[-1] // 2
    first, second = rows[..., :half], rows[..., half:]
    first = send_half(send_half(first, "x", 0), "q", 0)
    second = send_half(send_half(second, "q", 1), "x", 0)
    return jnp.concatenate([send_line(send_line(part, "z"), "p") for part in (first, second)], -1)


def merge_stats(stats):

    def merge(first, second):
        return jnp.stack(combine_partial(first, second))

    ways = (2, 2, lax.axis_size("z"), lax.axis_size("p"))
    stats = stats.reshape((3,) + ways + (-1,))
    stats = merge(stats[:, 0], swapped(stats[:, 1], "x"))
    stats = merge(stats[:, 0], swapped(stats[:, 1], "q"))
    for axis in ("z", "p"):
        total = stats[:, 0]
        for k in range(1, lax.axis_size(axis)):
            total = merge(total, shifted(stats[:, k], axis, k))
        stats = total
    return stats


def unpack_kernel(pack_ref, out_ref, *, columns):
    sides, owners, rows, total = pack_ref.shape
    for side in range(sides):
        for owner in range(owners):
            for at in range(total // columns):
                row = (owner * (total // columns) + at) * rows
                out_ref[row : row + rows, side * columns : (side + 1) * columns] = pack_ref[
                    side, owner, :, at * columns : (at + 1) * columns
                ]


def unpack_rows(pack, columns):
    sides, owners, rows, total = pack.shape
    each = rows * total // columns
    step = math.gcd(owners, 4)
    if rows % 16:
        pack = pack.reshape(sides, owners, rows, -1, columns)
        return jnp.transpose(pack, (1, 3, 2, 0, 4)).reshape(owners * each, sides * columns)
    return pl.pallas_call(
        functools.partial(unpack_kernel, columns=columns),
        grid=(owners // step,),
        in_specs=[pl.BlockSpec((sides, step, rows, total), lambda i: (0, i, 0, 0))],
        out_specs=pl.BlockSpec((step * each, sides * columns), lambda i: (i, 0)),
        out_shape=jax.ShapeDtypeStruct((owners * each, sides * columns), pack.dtype),
        cost_estimate=pl.CostEstimate(flops=0, bytes_accessed=4 * pack.size, transcendentals=0),
    )(pack)


def hold(*trees):
    return lax.optimization_barrier(trees)


def all_pairs(part, combine, whole):
    for axis in ALL:
        count = lax.axis_size(axis)
        if count & (count - 1):
            part = whole(part, axis)
            continue
        step = 1
        while step < count:
            part = combine(part, lax.ppermute(part, axis, [(i, i ^ step) for i in range(count)]))
            step *= 2
    return part


def all_sum(part):
    return all_pairs(part, jnp.add, lax.psum)


def pick(part, axis, index):
    return lax.dynamic_index_in_dim(part, index, axis, keepdims=False)


def own_first(part, axis):
    half = part.shape[axis] // 2
    first = lax.slice_in_dim(part, 0, half, axis=axis)
    second = lax.slice_in_dim(part, half, 2 * half, axis=axis)
    here = lax.axis_index("q") == 0
    return jnp.where(here, first, second), jnp.where(here, second, first)


def line_kernel(place_ref, *refs, unit):
    count = (len(refs) - 2) // 2
    kept_ref, sent_ref = refs[-2:]
    blocks = []
    for own, other in zip(refs[:count], refs[count : 2 * count]):
        total = own[0] + other[0].astype(jnp.float32)
        blocks += [total[at : at + unit] for at in range(0, total.shape[0], unit)]

    @pl.when(pl.program_id(0) == 0)
    def _():
        at = 0
        for block in blocks:
            kept_ref[:, at : at + block.shape[1]] = block
            at += block.shape[1]

    @pl.when(pl.program_id(0) > 0)
    def _():
        at = 0
        for block in blocks:
            sent_ref[0, :, at : at + block.shape[1]] = block.astype(jnp.bfloat16)
            at += block.shape[1]


def line_parts(owns, others, unit):
    lines = owns[0].shape[0]
    columns = sum(own.shape[1] // unit * own.shape[2] for own in owns)
    specs = [
        pl.BlockSpec((1,) + own.shape[1:], lambda k, place: ((place[0] + k) % lines, 0, 0))
        for own in owns
    ]
    return pl.pallas_call(
        functools.partial(line_kernel, unit=unit),
        grid_spec=pltpu.PrefetchScalarGridSpec(
            num_scalar_prefetch=1,
            grid=(lines,),
            in_specs=specs * 2,
            out_specs=[
                pl.BlockSpec((unit, columns), lambda k, place: (0, 0)),
                pl.BlockSpec((1, unit, columns), lambda k, place: (jnp.maximum(k - 1, 0), 0, 0)),
            ],
        ),
        out_shape=[
            jax.ShapeDtypeStruct((unit, columns), jnp.float32),
            jax.ShapeDtypeStruct((lines - 1, unit, columns), jnp.bfloat16),
        ],
        compiler_params=pltpu.CompilerParams(vmem_limit_bytes=KERNEL_BYTES),
        cost_estimate=pl.CostEstimate(
            flops=lines * unit * columns, bytes_accessed=8 * lines * unit * columns, transcendentals=0
        ),
    )(lax.axis_index("z").astype(jnp.int32).reshape(1), *owns, *others)


def factor_kernel(place_ref, *refs, turned, halves):
    (near, near_came, far, far_came), rights = refs[:4], refs[4:-2]
    kept_ref, sent_ref = refs[-2:]
    dims = RIGHT_T if turned else NORMAL

    def rows(ref):
        block = ref[...]
        return block.reshape(-1, block.shape[-1])

    def side(own, came, at):
        right, right_came = (ref[...].reshape(ref.shape[-2:]) for ref in rights[2 * at : 2 * at + 2])
        return dot(rows(own), right, dims) + dot(rows(came), right_came, dims)

    if halves:
        kept_ref[0], kept_ref[1] = side(near, near_came, 0), side(far, far_came, 0)
        sent_ref[0] = side(near, near_came, 1).astype(jnp.bfloat16)
        sent_ref[1] = side(far, far_came, 1).astype(jnp.bfloat16)
    else:
        kept_ref[...] = side(near, near_came, 0)
        sent_ref[...] = side(far, far_came, 0).astype(jnp.bfloat16)


def factor_parts(left, right, names, halves):
    own, came = left
    right, right_came = right
    _, lines, _, rows, tokens = own.shape
    turned = right.ndim == 2
    width = right.shape[0] if turned else right.shape[2]
    step = width // 2 if halves or width < 3072 else 384
    blocks = width // step
    place = [lax.axis_index("x"), lax.axis_index("q")]
    place += [left_at for _, left_at, _ in names] + [right_at or 0 for _, _, right_at in names]
    place = jnp.stack([jnp.asarray(part, jnp.int32) for part in place])
    count, groups = lines * rows, len(names)
    inner = 1 if halves else blocks

    def left_spec(far):

        def at_place(j, at):
            return at[2 + j // inner], 0, 1 - at[0] if far else at[0], 0, 0

        return pl.BlockSpec((1, lines, 1, rows, tokens), at_place)

    def right_spec(other):

        def at_place(j, at):
            if turned:
                return j, 0
            part = (1 - at[1] if other else at[1]) if halves else j % inner
            return at[2 + groups + j // inner], 0, part

        return pl.BlockSpec((step, tokens) if turned else (1, tokens, step), at_place)

    steps = groups * inner
    shape = (2, count, steps * step) if halves else (count, steps * step)
    out_spec = (
        pl.BlockSpec((2, count, step), lambda j, at: (0, 0, j))
        if halves
        else pl.BlockSpec((count, step), lambda j, at: (0, j))
    )
    rights = [right, right_came] * (2 if halves else 1)
    return pl.pallas_call(
        functools.partial(factor_kernel, turned=turned, halves=halves),
        grid_spec=pltpu.PrefetchScalarGridSpec(
            num_scalar_prefetch=1,
            grid=(steps,),
            in_specs=[left_spec(False), left_spec(False), left_spec(True), left_spec(True)]
            + [right_spec(at >= 2) for at in range(len(rights))],
            out_specs=[out_spec, out_spec],
        ),
        out_shape=[
            jax.ShapeDtypeStruct(shape, jnp.float32),
            jax.ShapeDtypeStruct(shape, jnp.bfloat16),
        ],
        compiler_params=pltpu.CompilerParams(vmem_limit_bytes=KERNEL_BYTES),
        cost_estimate=pl.CostEstimate(
            flops=8 * count * tokens * width * groups,
            bytes_accessed=8 * count * tokens + (4 * tokens + 12 * count) * width * groups,
            transcendentals=0,
        ),
    )(place, own, came, own, came, *rights)


class Group:
    def __init__(self, *factors, ready=(), mixed=0):
        core, side = lax.axis_index("c"), lax.axis_index("x")
        self.names, self.kept, self.flight, self.ways, self.rows = [], [], [], [], []
        self.mixed = mixed
        self.stage = 0
        for way, left, right, names in factors:
            kept, sent = factor_parts(left, right, names, not way)
            self.take([name for name, _, _ in names], kept, sent, way)
        for name, grad in ready:
            grad = grad.reshape(lax.axis_size("z"), 2, 2, -1, grad.shape[1])
            grad = pick(grad, 2, core) + swapped(pick(grad, 2, 1 - core), "c")
            self.take([name], pick(grad, 1, side), pick(grad, 1, 1 - side), True)
        self.unit = min(self.rows)

    def take(self, names, kept, sent, way):
        self.names.append(names[:1] if way else names)
        kept, sent = (part.reshape(-1, part.shape[-1]) for part in (kept, sent))
        self.kept.append(kept)
        self.ways.append(way)
        self.rows.append(kept.shape[0] // lax.axis_size("z") // (1 if way else 2))
        self.flight.append(swapped(sent.astype(jnp.bfloat16), "x" if way else "q"))

    def advance(self):
        self.stage += 1
        lines = lax.axis_size("z")
        if self.stage == 1:
            for at, way in enumerate(self.ways):
                kept, came = self.kept[at], self.flight[at]
                total = kept + came.astype(jnp.float32)
                half = total.shape[0] // 2
                near, far = own_first(total, 1) if way else (total[:half], total[half:])
                self.kept[at] = near.reshape(lines, -1, near.shape[1])
                far = far.astype(jnp.bfloat16).reshape(lines, -1, far.shape[1])
                self.flight[at] = swapped(far, "q" if way else "x")
        elif self.stage == 2:
            self.shapes = [part.shape[1:] for part in self.kept]
            self.total, sent = line_parts(self.kept, self.flight, self.unit)
            self.flight = [shifted(sent[k], "z", k + 1) for k in range(sent.shape[0])]
        elif self.stage == 3:
            for part in self.flight:
                self.total = self.total + part.astype(jnp.float32)
            if lax.axis_size("p") > 1:
                self.total = lax.psum(self.total, "p")
                self.mixed = sum(len(names) for names in self.names)
            self.spans = []
            for names, (rows, columns) in zip(self.names, self.shapes):
                for name in names:
                    self.spans.append((name, rows // self.unit, columns // len(names)))
            width = sum(blocks * columns for _, blocks, columns in self.spans[: self.mixed])
            self.flight = swapped(self.total[:, :width], "q") if self.mixed else ()
        else:
            at, self.done = 0, {}
            for turn, (name, blocks, columns) in enumerate(self.spans):
                parts = []
                for _ in range(blocks):
                    near = self.total[:, at : at + columns]
                    if turn < self.mixed:
                        far = self.flight[:, at : at + columns]
                        near = jnp.where(
                            lax.axis_index("q") == 0,
                            jnp.concatenate([near, far], 1),
                            jnp.concatenate([far, near], 1),
                        )
                    parts.append(near)
                    at += columns
                self.done[name] = parts[0] if len(parts) == 1 else jnp.concatenate(parts, 0)


class Chain:
    def __init__(self, name, part):
        self.names = [name]
        self.part = part
        self.hops = []
        for axis in ALL:
            count = lax.axis_size(axis)
            self.hops += [(axis, 1 << bit) for bit in range((count - 1).bit_length())]
        self.stage = 4 - len(self.hops)
        self.launch()

    def launch(self):
        axis, step = self.hops.pop(0)
        count = lax.axis_size(axis)
        self.flight = lax.ppermute(self.part, axis, [(i, i ^ step) for i in range(count)])

    def advance(self):
        self.stage += 1
        self.part = self.part + self.flight
        if self.hops:
            self.launch()
        else:
            self.stage = 4
            self.done = {self.names[0]: self.part}


class Reducer:

    def __init__(self):
        self.moving = []
        self.done = {}

    def add(self, item):
        self.moving.append(item)

    def step(self, *live):
        live, flights = hold(live, [item.flight for item in self.moving])
        for item, flight in zip(self.moving, flights):
            item.flight = flight
        self.advance()
        return live

    def advance(self):
        for item in self.moving:
            item.advance()
            if item.stage == 4:
                self.done.update(item.done)
        self.moving = [item for item in self.moving if item.stage < 4]


def pairs_in(pairs):
    both = (pairs, swapped(pairs, "c"))
    if lax.axis_size("p") > 1:
        both = tuple(lax.all_gather(part, "p", axis=0, tiled=True) for part in both)
    return both


def pairs_back(grads):
    if lax.axis_size("p") > 1:
        grads = tuple(
            lax.psum_scatter(part, "p", scatter_dimension=1, tiled=True) for part in grads
        )
    own, other = grads
    return (own + swapped(other, "c")).astype(jnp.bfloat16)


def both_cores(part):
    return part, swapped(part, "c")


def turn_kernel(core_ref, *refs, rows):
    parts, (own_ref, other_ref) = refs[:-2], refs[-2:]
    lines = own_ref.shape[1]
    for at, ref in enumerate(parts):
        part = ref[...]
        if part.shape[0] != lines * 4 * rows:
            part = part.astype(jnp.float32).T.astype(jnp.bfloat16)
        blocks = [part[k * rows : (k + 1) * rows] for k in range(4 * lines)]
        for here in range(2):

            @pl.when(core_ref[0] == here)
            def _():
                for line in range(lines):
                    for side in range(2):
                        first = (line * 2 + side) * 2
                        own_ref[at, line, side] = blocks[first + here]
                        other_ref[at, line, side] = blocks[first + 1 - here]


def turn_rows(parts, turned, rows):
    tokens, width = parts[0].shape
    lines = width // (4 * rows)
    count = len(parts) + len(turned)
    shape = (count, lines, 2, rows, tokens)
    if rows % 16 or tokens == width:
        whole = jnp.stack([part.T for part in parts] + list(turned))
        whole = whole.reshape(count, lines, 2, 2, rows, tokens)
        core = lax.axis_index("c")
        return pick(whole, 3, core), pick(whole, 3, 1 - core)
    vmem = pl.BlockSpec(memory_space=pltpu.VMEM)
    return pl.pallas_call(
        functools.partial(turn_kernel, rows=rows),
        in_specs=[pl.BlockSpec(memory_space=pltpu.SMEM)] + [vmem] * count,
        out_specs=[vmem, vmem],
        out_shape=[jax.ShapeDtypeStruct(shape, jnp.bfloat16)] * 2,
        compiler_params=pltpu.CompilerParams(vmem_limit_bytes=KERNEL_BYTES),
        cost_estimate=pl.CostEstimate(
            flops=0, bytes_accessed=4 * count * tokens * width, transcendentals=0
        ),
    )(lax.axis_index("c").astype(jnp.int32).reshape(1), *parts, *turned)


def pack_kernel(*refs, width):
    out_ref = refs[-1]
    at = 0
    for ref in refs[:-1]:
        for column in range(0, ref.shape[1], width):
            out_ref[at : at + 1, :] = ref[0:1, column : column + width]
            at += 1


def pack_rows(parts, width):
    count = sum(part.shape[1] // width for part in parts)
    vmem = pl.BlockSpec(memory_space=pltpu.VMEM)
    return pl.pallas_call(
        functools.partial(pack_kernel, width=width),
        in_specs=[vmem] * len(parts),
        out_specs=vmem,
        out_shape=jax.ShapeDtypeStruct((count, width), jnp.float32),
    )(*parts)


def head_scores(table_ref, rows_ref, ids_ref):
    scores = dot(table_ref[...], rows_ref[...], RIGHT_T)
    return jnp.where(ids_ref[:, 0:1] < V, scores, MASKED_SCORE)


def head_kernel(table_ref, rows_ref, ids_ref, labels_ref, terms_ref, stats_ref):
    scores = head_scores(table_ref, rows_ref, ids_ref)
    top = jnp.max(scores, 0, keepdims=True)
    terms = jnp.exp(scores - top)
    stats_ref[0:1, :] = top
    stats_ref[1:2, :] = jnp.sum(terms, 0, keepdims=True)
    hit = ids_ref[:, 0:1] == labels_ref[0:1, :]
    stats_ref[2:3, :] = jnp.sum(jnp.where(hit, scores, 0.0), 0, keepdims=True)
    terms_ref[...] = terms.astype(jnp.bfloat16)


def head_forward(table, rows, ids, labels):
    columns, width = table.shape
    count = rows.shape[0]
    step = math.gcd(count, 256)
    return pl.pallas_call(
        head_kernel,
        grid=(count // step,),
        in_specs=[
            pl.BlockSpec((columns, width), lambda i: (0, 0)),
            pl.BlockSpec((step, width), lambda i: (i, 0)),
            pl.BlockSpec((columns, 1), lambda i: (0, 0)),
            pl.BlockSpec((1, step), lambda i: (0, i)),
        ],
        out_specs=[
            pl.BlockSpec((columns, step), lambda i: (0, i)),
            pl.BlockSpec((3, step), lambda i: (0, i)),
        ],
        out_shape=[
            jax.ShapeDtypeStruct((columns, count), jnp.bfloat16),
            jax.ShapeDtypeStruct((3, count), jnp.float32),
        ],
        compiler_params=pltpu.CompilerParams(vmem_limit_bytes=KERNEL_BYTES),
        cost_estimate=pl.CostEstimate(
            flops=2 * columns * width * count,
            bytes_accessed=2 * (columns * width + count * width + columns * count),
            transcendentals=columns * count,
        ),
    )(table, rows, ids, labels)


def table_kernel(table_ref, rows_ref, ids_ref, labels_ref, logsum_ref, grad_ref, *, scale):
    scores = head_scores(table_ref, rows_ref, ids_ref)
    hit = ids_ref[:, 0:1] == labels_ref[0:1, :]
    probs = jnp.exp(scores - logsum_ref[0:1, :])
    grad = ((probs - jnp.where(hit, 1.0, 0.0)) * scale).astype(jnp.bfloat16)
    grad_ref[...] = dot(grad, rows_ref[...], NORMAL)


def head_table(table, rows, ids, labels, logsum, scale):
    columns, width = table.shape
    count = rows.shape[0]
    steps = max(k for k in range(1, 13) if k == 1 or columns % (16 * k) == 0)
    step = columns // steps
    return pl.pallas_call(
        functools.partial(table_kernel, scale=scale),
        grid=(steps,),
        in_specs=[
            pl.BlockSpec((step, width), lambda i: (i, 0)),
            pl.BlockSpec((count, width), lambda i: (0, 0)),
            pl.BlockSpec((step, 1), lambda i: (i, 0)),
            pl.BlockSpec((1, count), lambda i: (0, 0)),
            pl.BlockSpec((1, count), lambda i: (0, 0)),
        ],
        out_specs=pl.BlockSpec((step, width), lambda i: (i, 0)),
        out_shape=jax.ShapeDtypeStruct((columns, width), jnp.float32),
        compiler_params=pltpu.CompilerParams(vmem_limit_bytes=KERNEL_BYTES),
        cost_estimate=pl.CostEstimate(
            flops=4 * columns * width * count,
            bytes_accessed=6 * columns * width + 2 * count * width,
            transcendentals=columns * count,
        ),
    )(table, rows, ids, labels, logsum)


class Lookup:
    def __init__(self, token_ids, own_rows):
        owners = 1
        for axis in ALL:
            owners *= lax.axis_size(axis)
        self.owners = owners
        self.own_rows = own_rows
        count = token_ids.shape[0]
        places = jnp.arange(count, dtype=jnp.int32)
        owner = token_ids // own_rows
        same = token_ids[:, None] == token_ids[None, :]
        first = jnp.min(jnp.where(same, places[None, :], count), 1)
        is_first = first == places
        ahead = (owner[:, None] == owner[None, :]) & is_first[None, :] & (places[None, :] < first[:, None])
        self.rank = jnp.sum(ahead.astype(jnp.int32), 1)
        self.owner = owner
        self.is_first = is_first
        self.local_id = token_ids - owner * own_rows
    def round_places(self, turn):
        rank = self.rank - turn * SLOTS
        inside = (rank >= 0) & (rank < SLOTS)
        slot = jnp.where(inside, self.owner * SLOTS + rank, -1)
        to_owner = jnp.where(
            (self.owner[:, None] == jnp.arange(self.owners)[None, :]) & self.is_first[:, None],
            (self.local_id + 1).astype(jnp.float32)[:, None],
            0.0,
        )
        to_slot = (rank[:, None] == jnp.arange(SLOTS)[None, :]).astype(jnp.float32)
        asked = lax.dot_general(to_owner, to_slot, (((0,), (0,)), ((), ())), precision=PRECISE)
        asked = jnp.round(asked).astype(jnp.int32) - 1
        last = jnp.broadcast_to(jnp.max(self.rank), (self.owners, 1))
        wanted = lax.all_to_all(jnp.concatenate([asked, last], 1), ALL, 0, 0, tiled=True)
        self.rounds = jnp.max(wanted[:, SLOTS:]) // SLOTS + 1
        wanted = wanted[:, :SLOTS].reshape(-1)
        return one_hot(slot, self.owners * SLOTS), one_hot(wanted, self.own_rows)

    def fetch_round(self, turn, table_low):
        to_slot, to_row = self.round_places(turn)
        sent = product(to_row, table_low).astype(jnp.bfloat16)
        rows = lax.all_to_all(sent, ALL, 0, 0, tiled=True)
        return product(to_slot, rows), (to_slot, to_row)

    def fetch(self, table_low):
        rows, self.kept = self.fetch_round(0, table_low)
        rounds = self.rounds
        rows = lax.fori_loop(
            1, rounds, lambda turn, total: total + self.fetch_round(turn, table_low)[0], rows
        )
        self.rounds = rounds
        return rows

    def give_round(self, places, grads_b):
        to_slot, to_row = places
        sent = row_contract(to_slot, grads_b).astype(jnp.bfloat16)
        back = lax.all_to_all(sent, ALL, 0, 0, tiled=True)
        return row_contract(to_row, back)

    def give(self, grads_b):
        grad = self.give_round(self.kept, grads_b)
        rounds = self.rounds
        return lax.fori_loop(
            1,
            rounds,
            lambda turn, total: total + self.give_round(self.round_places(turn), grads_b),
            grad,
        )


def local(
    table_weight,
    table_moment,
    table_square,
    position_weight,
    position_moment,
    position_square,
    wide_weight,
    wide_moment,
    wide_square,
    down_weight,
    down_moment,
    down_square,
    vector_weight,
    vector_moment,
    vector_square,
    source_ids,
    target_ids,
    target_labels,
    source_segments,
    target_segments,
    completion_idx,
):
    cuts = lax.axis_size("p")
    ctx_count = 2 * cuts
    shard_count = lax.axis_size("z") * 4
    core = lax.axis_index("c")
    block = lax.axis_index("p") * 2 + core
    ctx_index = lax.axis_index("q") * cuts + lax.axis_index("p")
    tokens = source_ids.shape[1]
    comp_count = completion_idx.shape[1]
    width = vector_weight.shape[1]
    hidden = down_weight.shape[1] * shard_count
    head_count = H
    own_rows = table_weight.shape[0]
    table_low = table_weight.astype(jnp.bfloat16)

    small = jnp.concatenate(
        [source_ids, target_ids, target_labels, source_segments, target_segments, completion_idx], 1
    )
    small = lax.all_gather(small[0], ("q", "p", "c"))
    small = small.reshape(ctx_count, 2, -1)
    small = lax.dynamic_index_in_dim(small, lax.axis_index("q"), 1, keepdims=False)
    src_ids, tgt_ids, tgt_labels, src_seg, tgt_seg = (
        small[:, k * tokens : (k + 1) * tokens] for k in range(5)
    )

    def own_block(blocks):
        return lax.dynamic_index_in_dim(blocks, block, 0, keepdims=False)

    def key_order(blocks):
        pairs = blocks.reshape(cuts, 2, -1)
        pairs = jnp.where(core == 0, pairs, pairs[:, ::-1])
        return jnp.moveaxis(pairs, 1, 0).reshape(-1)

    comp_places = own_block(small[:, 5 * tokens :])
    comp_hit = one_hot(comp_places, tokens)
    own_labels = jnp.take(own_block(tgt_labels), comp_places)

    lookup = Lookup(jnp.concatenate([own_block(src_ids), own_block(tgt_ids)]), own_rows)
    token_rows = lookup.fetch(table_low)

    wide_low = wide_weight.astype(jnp.bfloat16)
    down_low = down_weight.astype(jnp.bfloat16)
    shard_rows, span = wide_low.shape
    bounds = [0, span * 2 // 5, span * 4 // 5, span]
    place_pack = position_weight.astype(jnp.bfloat16).reshape(shard_rows, -1)

    def gathered(parts):
        part = parts[0] if len(parts) == 1 else jnp.concatenate(parts, 1)
        return lax.all_gather(part, ALL).reshape(ctx_count, width, part.shape[1])

    def flat_down(part):
        part = part.reshape(-1, shard_rows, part.shape[1])
        return jnp.moveaxis(part, 0, 1).reshape(shard_rows, -1)

    def tall_down(pack):
        return unpack_rows(pack.reshape(ctx_count, shard_count, shard_rows, -1), width // ctx_count)

    early = gathered([wide_low[:, : bounds[1]], wide_low[:, bounds[2] :], place_pack])
    middle = gathered([wide_low[:, bounds[1] : bounds[2]], flat_down(down_low[0])])
    late = gathered([flat_down(down_low[1])])
    position_full = early[:, :, span - bounds[2] + bounds[1] :].reshape(
        (ctx_count, shard_count) + position_weight.shape
    )
    position_full = jnp.moveaxis(position_full, 0, 2).reshape(-1, width)

    def columns(name, size=None):
        start = starts[name]
        size = size or (hidden if name in FIRSTS else width)
        pieces = []
        while size:
            side, inner = divmod(start, span)
            turn = max(k for k in range(3) if bounds[k] <= inner)
            take = min(size, bounds[turn + 1] - inner)
            source = middle if turn == 1 else early
            at = inner - (0, bounds[1], bounds[2] - bounds[1])[turn]
            pieces.append(source[side, :, at : at + take])
            start, size = start + take, size - take
        return pieces[0] if len(pieces) == 1 else jnp.concatenate(pieces, 1)

    def vector_row(name):
        return vector_weight[name]

    blocks = hidden // width
    base_row = Row.dec_norm3_bias + 1
    enc_first_bias = vector_weight[base_row : base_row + blocks].reshape(-1)
    dec_first_bias = vector_weight[base_row + blocks : base_row + 2 * blocks].reshape(-1)
    names = range(Part.dec_first + 1)
    starts, offset = {}, 0
    for name in names:
        starts[name] = offset
        offset += hidden if name in FIRSTS else width


    table_count = position_full.shape[0]
    src_pos = own_block(doc_positions(src_seg.reshape(-1), table_count).reshape(ctx_count, -1))
    tgt_pos = own_block(doc_positions(tgt_seg.reshape(-1), table_count).reshape(ctx_count, -1))
    src_onehot = one_hot(src_pos, table_count)
    tgt_onehot = one_hot(tgt_pos, table_count)
    src_input = token_rows[:tokens] + product(src_onehot, position_full)
    tgt_input = token_rows[tokens:] + product(tgt_onehot, position_full)

    query_places = block * tokens + jnp.arange(tokens)
    key_places = key_order(jnp.arange(ctx_count * tokens).reshape(ctx_count, tokens))
    src_keys_seg = key_order(src_seg)
    tgt_keys_seg = key_order(tgt_seg)
    own_src_seg = own_block(src_seg)
    own_tgt_seg = own_block(tgt_seg)
    last_place = jnp.full((tokens,), ctx_count * tokens, jnp.int32)

    def marks(query_seg, query_last, key_seg):
        return (
            jnp.pad(jnp.stack([query_seg, query_last]), ((0, 6), (0, 0))),
            jnp.pad(jnp.stack([key_seg, key_places], 1), ((0, 0), (0, 126))),
        )

    enc_marks = marks(own_src_seg, last_place, src_keys_seg)
    self_marks = marks(own_tgt_seg, query_places, tgt_keys_seg)
    cross_marks = marks(own_tgt_seg, last_place, src_keys_seg)

    def norm(values, gain, bias):
        return norm_forward(values, vector_row(gain), vector_row(bias))

    enc_norm0, enc_saved0 = norm(src_input, Row.enc_norm0_gain, Row.enc_norm0_bias)
    enc_in_b = enc_norm0.astype(jnp.bfloat16)
    enc_queries = project_queries(enc_in_b, columns(Part.enc_wq), vector_row(Row.enc_query_bias))
    enc_pairs = project_pairs(
        enc_in_b, columns(Part.enc_wk, 2 * width), vector_row(Row.enc_value_bias)
    )
    enc_pairs_all = pairs_in(enc_pairs)
    dec_norm0, dec_saved0 = norm(tgt_input, Row.dec_norm0_gain, Row.dec_norm0_bias)
    dec_in_b = dec_norm0.astype(jnp.bfloat16)
    dec_queries = project_queries(dec_in_b, columns(Part.dec_wq), vector_row(Row.dec_query_bias))
    dec_pairs = project_pairs(
        dec_in_b, columns(Part.dec_wk, 2 * width), vector_row(Row.dec_value_bias)
    )
    dec_pairs_all = pairs_in(dec_pairs)
    enc_branch, enc_mixed_t, enc_logsum = branch_forward(
        enc_queries,
        enc_pairs_all,
        enc_marks,
        columns(Part.enc_out),
        vector_row(Row.enc_out_bias),
        head_count,
    )
    enc_norm1, enc_saved1 = norm(enc_norm0 + enc_branch, Row.enc_norm1_gain, Row.enc_norm1_bias)
    self_branch, self_mixed_t, self_logsum = branch_forward(
        dec_queries,
        dec_pairs_all,
        self_marks,
        columns(Part.dec_out),
        vector_row(Row.dec_out_bias),
        head_count,
    )
    dec_norm1, dec_saved1 = norm(dec_norm0 + self_branch, Row.dec_norm1_gain, Row.dec_norm1_bias)
    cross_in_b = dec_norm1.astype(jnp.bfloat16)
    cross_queries = project_queries(
        cross_in_b, columns(Part.cross_wq), vector_row(Row.cross_query_bias)
    )

    enc_norm1, cross_queries, middle, own_labels = hold(
        enc_norm1, cross_queries, middle, own_labels
    )
    head_labels = group_in(own_labels, "q").reshape(-1)
    enc_first, enc_second = (
        columns(Part.enc_first),
        tall_down(middle[:, :, bounds[2] - bounds[1] :]),
    )
    enc_mid_b = enc_norm1.astype(jnp.bfloat16)
    enc_ffn, enc_slope, enc_act_t = feed_forward(
        enc_mid_b, enc_first, enc_first_bias, enc_second, vector_row(Row.enc_ffn_bias)
    )
    encoded, enc_saved2 = norm(enc_norm1 + enc_ffn, Row.enc_norm2_gain, Row.enc_norm2_bias)
    encoded_b = encoded.astype(jnp.bfloat16)
    cross_pair_weights = columns(Part.cross_wk, 2 * width)
    cross_pairs = project_pairs(encoded_b, cross_pair_weights, vector_row(Row.cross_value_bias))
    cross_pairs_all = pairs_in(cross_pairs)
    cross_branch, cross_mixed_t, cross_logsum = branch_forward(
        cross_queries,
        cross_pairs_all,
        cross_marks,
        columns(Part.cross_out),
        vector_row(Row.cross_out_bias),
        head_count,
    )
    dec_norm2, dec_saved2 = norm(dec_norm1 + cross_branch, Row.dec_norm2_gain, Row.dec_norm2_bias)
    dec_norm2, late, head_labels = hold(dec_norm2, late, head_labels)
    dec_first, dec_second = columns(Part.dec_first), tall_down(late)
    dec_mid_b = dec_norm2.astype(jnp.bfloat16)
    dec_ffn, dec_slope, dec_act_t = feed_forward(
        dec_mid_b, dec_first, dec_first_bias, dec_second, vector_row(Row.dec_ffn_bias)
    )
    final, dec_saved3 = norm(dec_norm2 + dec_ffn, Row.dec_norm3_gain, Row.dec_norm3_bias)
    final_b = final.astype(jnp.bfloat16)
    head_rows = group_rows(product(comp_hit, final_b).astype(jnp.bfloat16))

    own_left, other_left = turn_rows(
        (enc_in_b, dec_in_b, cross_in_b, enc_mid_b, encoded_b, dec_mid_b),
        (enc_mixed_t, self_mixed_t, cross_mixed_t),
        shard_rows,
    )
    left = (own_left, swapped(other_left, "c"))

    def act_left(act_t):
        act_t = act_t.reshape(lax.axis_size("z"), 2, 2, -1, act_t.shape[1])
        own, other = pick(act_t, 2, core), pick(act_t, 2, 1 - core)
        return own[None], swapped(other, "c")[None]

    enc_act, dec_act = act_left(enc_act_t), act_left(dec_act_t)
    head_rows, left, enc_act, dec_act = hold(head_rows, left, enc_act, dec_act)
    table_pair = jnp.concatenate([table_low, swapped(table_low, "c")], 0)
    group_start = 0
    for axis in ("q", "p", "z", "x"):
        group_start = group_start * lax.axis_size(axis) + lax.axis_index(axis)
    own_ids = jnp.arange(own_rows, dtype=jnp.int32)
    column_ids = jnp.concatenate(
        [(group_start * 2 + core) * own_rows + own_ids, (group_start * 2 + 1 - core) * own_rows + own_ids]
    )
    column_marks, label_marks = column_ids[:, None], head_labels[None, :]
    terms, stats = head_forward(table_pair, head_rows, column_marks, label_marks)
    merged_top, merged_sum, merged_label = merge_stats(stats)
    own_logsum = merged_top + jnp.log(merged_sum)
    loss_local = jnp.sum(own_logsum - merged_label)
    logsum_rows = group_in(own_logsum, "q").reshape(-1)
    loss_scale = 1.0 / (comp_count * ctx_count * shard_count)
    mixed_rows = dot(terms, table_pair, LEFT_T)
    label_hit = (column_marks == label_marks).astype(jnp.bfloat16)
    label_rows = dot(label_hit, table_pair, LEFT_T)
    mixed_rows, label_rows, logsum_rows = hold(mixed_rows, label_rows, logsum_rows)
    row_scale = jnp.exp(stats[0] - logsum_rows)[:, None]
    grad_picked = group_sum((mixed_rows * row_scale - label_rows) * loss_scale)
    marks = (label_marks, logsum_rows[None, :], loss_scale)
    other_grad = head_table(table_pair[own_rows:], head_rows, column_marks[own_rows:], *marks)
    table_grad = head_table(table_low, head_rows, column_marks[:own_rows], *marks)
    table_grad, grad_picked = hold(table_grad, grad_picked)
    table_grad = table_grad + swapped(other_grad, "c")
    grad_final = lax.dot_general(
        comp_hit.astype(jnp.float32), grad_picked, (((0,), (0,)), ((), ())), precision=PRECISE
    )

    vector_grads = {}
    reducer = Reducer()

    def norm_back(grad, saved, gain):
        grad, vector_grads[gain], vector_grads[gain + 1] = norm_backward(
            grad, saved, vector_row(gain)
        )
        return grad

    grad_sum3 = norm_back(grad_final, dec_saved3, Row.dec_norm3_gain)
    grad_mid, dec_pre_grad, dec_first_bias_g, dec_ffn_grad, vector_grads[Row.dec_ffn_bias] = (
        feed_backward(grad_sum3, dec_slope, dec_first, dec_second)
    )
    grad_sum2 = norm_back(grad_sum3 + grad_mid, dec_saved2, Row.dec_norm2_gain)
    reducer.add(
        Group(
            (True, left, both_cores(dec_pre_grad), ((Part.dec_first, 5, None),)),
            (False, dec_act, both_cores(dec_ffn_grad[None]), ((Part.dec_second, 0, 0),)),
            mixed=1,
        )
    )
    cross_query_grad, cross_grad_pairs, cross_branch_grad, vector_grads[Row.cross_out_bias] = (
        branch_backward(
            grad_sum2,
            cross_queries,
            cross_pairs_all,
            cross_marks,
            cross_logsum,
            columns(Part.cross_out),
            head_count,
        )
    )
    cross_query_grad, cross_grad_pairs = reducer.step(cross_query_grad, cross_grad_pairs)
    cross_pairs_grad = pairs_back(cross_grad_pairs)
    vector_grads[Row.cross_query_bias], grad_cross_in = query_backward(
        columns(Part.cross_wq), cross_query_grad
    )
    grad_sum1 = norm_back(grad_sum2 + grad_cross_in, dec_saved1, Row.dec_norm1_gain)
    vector_grads[Row.cross_value_bias], grad_encoded = pairs_backward(
        cross_pair_weights, cross_pairs_grad
    )
    right = both_cores(
        jnp.concatenate([cross_pairs_grad, cross_query_grad[None], cross_branch_grad[None]], 0)
    )
    reducer.add(
        Group(
            (True, left, right, ((Part.cross_wk, 4, 0), (Part.cross_wv, 4, 1))),
            (False, left, right, ((Part.cross_wq, 2, 2), (Part.cross_out, 8, 3))),
            mixed=4,
        )
    )
    dec_query_grad, dec_grad_pairs, dec_branch_grad, vector_grads[Row.dec_out_bias] = (
        branch_backward(
            grad_sum1,
            dec_queries,
            dec_pairs_all,
            self_marks,
            self_logsum,
            columns(Part.dec_out),
            head_count,
        )
    )
    grad_encoded, dec_query_grad, dec_grad_pairs = reducer.step(
        grad_encoded, dec_query_grad, dec_grad_pairs
    )
    dec_pairs_grad = pairs_back(dec_grad_pairs)
    vector_grads[Row.dec_query_bias], grad_dec_q_in = query_backward(
        columns(Part.dec_wq), dec_query_grad
    )
    vector_grads[Row.dec_value_bias], grad_dec_kv_in = pairs_backward(
        columns(Part.dec_wk, 2 * width), dec_pairs_grad
    )
    right = both_cores(
        jnp.concatenate([dec_pairs_grad, dec_query_grad[None], dec_branch_grad[None]], 0)
    )
    reducer.add(
        Group(
            (True, left, right, ((Part.dec_wk, 1, 0), (Part.dec_wv, 1, 1))),
            (False, left, right, ((Part.dec_wq, 1, 2), (Part.dec_out, 7, 3))),
            mixed=4,
        )
    )
    grad_enc2 = norm_back(grad_encoded, enc_saved2, Row.enc_norm2_gain)
    grad_tgt_input = norm_back(
        grad_sum1 + grad_dec_q_in + grad_dec_kv_in, dec_saved0, Row.dec_norm0_gain
    )
    grad_enc2, grad_tgt_input = reducer.step(grad_enc2, grad_tgt_input)
    grad_enc_mid, enc_pre_grad, enc_first_bias_g, enc_ffn_grad, vector_grads[Row.enc_ffn_bias] = (
        feed_backward(grad_enc2, enc_slope, enc_first, enc_second)
    )
    grad_enc1 = norm_back(grad_enc2 + grad_enc_mid, enc_saved1, Row.enc_norm1_gain)
    grad_enc1, enc_pre_grad, enc_ffn_grad = reducer.step(grad_enc1, enc_pre_grad, enc_ffn_grad)
    reducer.add(
        Group(
            (True, left, both_cores(enc_pre_grad), ((Part.enc_first, 3, None),)),
            (False, enc_act, both_cores(enc_ffn_grad[None]), ((Part.enc_second, 0, 0),)),
            mixed=1,
        )
    )
    enc_query_grad, enc_grad_pairs, enc_branch_grad, vector_grads[Row.enc_out_bias] = (
        branch_backward(
            grad_enc1,
            enc_queries,
            enc_pairs_all,
            enc_marks,
            enc_logsum,
            columns(Part.enc_out),
            head_count,
        )
    )
    enc_query_grad, enc_grad_pairs = reducer.step(enc_query_grad, enc_grad_pairs)
    enc_pairs_grad = pairs_back(enc_grad_pairs)
    vector_grads[Row.enc_query_bias], grad_enc_q_in = query_backward(
        columns(Part.enc_wq), enc_query_grad
    )
    vector_grads[Row.enc_value_bias], grad_enc_kv_in = pairs_backward(
        columns(Part.enc_wk, 2 * width), enc_pairs_grad
    )
    grad_src_input = norm_back(
        grad_enc1 + grad_enc_q_in + grad_enc_kv_in, enc_saved0, Row.enc_norm0_gain
    )
    right = both_cores(
        jnp.concatenate([enc_pairs_grad, enc_query_grad[None], enc_branch_grad[None]], 0)
    )
    reducer.add(
        Group(
            (True, left, right, ((Part.enc_wk, 0, 0), (Part.enc_wv, 0, 1))),
            (False, left, right, ((Part.enc_wq, 0, 2), (Part.enc_out, 6, 3))),
            mixed=4,
        )
    )
    table_grad = table_grad + lookup.give(
        jnp.concatenate(
            [grad_src_input.astype(jnp.bfloat16), grad_tgt_input.astype(jnp.bfloat16)], 0
        )
    )
    position_grad = lax.dot_general(
        src_onehot.astype(jnp.float32), grad_src_input, LEFT_T, precision=PRECISE
    ) + lax.dot_general(
        tgt_onehot.astype(jnp.float32), grad_tgt_input, LEFT_T, precision=PRECISE
    )
    reducer.add(Group(ready=[(Part.position, position_grad)]))
    vector_grad = pack_rows(
        [vector_grads[name] for name in range(base_row)] + [enc_first_bias_g, dec_first_bias_g],
        width,
    )
    reducer.add(Chain(None, vector_grad))
    while reducer.moving:
        reducer.advance()
    summed = reducer.done
    vector_grad = summed[None]

    def own_columns(part):
        part = part.reshape(part.shape[0], ctx_count, -1)
        return lax.dynamic_index_in_dim(part, ctx_index, 1, keepdims=False)

    wide_grad = own_columns(
        jnp.concatenate(
            [
                summed[name]
                for name in (
                    Part.enc_wq,
                    Part.enc_wk,
                    Part.enc_out,
                    Part.enc_first,
                    Part.dec_wq,
                    Part.dec_wk,
                    Part.dec_out,
                    Part.cross_wq,
                    Part.cross_wk,
                    Part.cross_out,
                    Part.dec_first,
                )
            ],
            1,
        )
    )
    deep = [summed[name] for name in (Part.enc_second, Part.dec_second, Part.position)]
    if cuts > 1:
        deep = [own_columns(part) for part in deep]
    down_grad, position_grad = jnp.stack(deep[:2]), deep[2]
    owned_squares = (
        jnp.sum(wide_grad * wide_grad)
        + jnp.sum(down_grad * down_grad)
        + jnp.sum(position_grad * position_grad)
        + jnp.sum(table_grad * table_grad)
    )
    sums = all_sum(jnp.stack([owned_squares, loss_local]))
    square_total, loss_sum = sums[0], sums[1]
    grad_norm = jnp.sqrt(square_total + jnp.sum(vector_grad * vector_grad))
    clip_factor = jnp.minimum(1.0, CLIP_LIMIT / (grad_norm + 1e-06))
    outs = [loss_sum, grad_norm]
    for weight, moment, square, grad, decay, rate in (
        (table_weight, table_moment, table_square, table_grad, WEIGHT_DECAY, LEARN_RATE),
        (position_weight, position_moment, position_square, position_grad, WEIGHT_DECAY, LEARN_RATE),
        (wide_weight, wide_moment, wide_square, wide_grad, WEIGHT_DECAY, LEARN_RATE),
        (down_weight, down_moment, down_square, down_grad, WEIGHT_DECAY, LEARN_RATE),
        (vector_weight, vector_moment, vector_square, vector_grad, 0.0, VECTOR_RATE),
    ):
        outs.extend(adam_step(weight, moment, square, grad * clip_factor, decay, rate))
    return tuple(outs)


def solution(mesh):
    ctx_count, shard_count = mesh.devices.shape
    fine = Mesh(mesh.devices.reshape(2, ctx_count // 2, shard_count // 4, 2, 2), ALL)
    ctx, shard = ("q", "p"), ("z", "x", "c")
    table, plane, deep, whole = P(ALL, None), P(shard, ctx), P(None, shard, ctx), P()
    states = (table,) * 3 + (plane,) * 6 + (deep,) * 3 + (whole,) * 3
    return jax.shard_map(
        local,
        mesh=fine,
        in_specs=states + (plane,) * 6,
        out_specs=(whole, whole) + states,
        check_vma=False,
    )
```

```python
import functools
import math

import jax
import jax.numpy as jnp
from jax import lax
from jax.experimental import pallas as pl
from jax.experimental.pallas import tpu as pltpu
from jax.sharding import Mesh
from jax.sharding import PartitionSpec as P

H = 12
V = 50265
STEP = 10


PRECISE = lax.Precision.HIGHEST
NORM_EPS = 1e-05
LEARN_RATE = 0.03
VECTOR_RATE = 0.3
BETA_ONE = 0.9
BETA_TWO = 0.999
ADAM_EPS = 1e-08
WEIGHT_DECAY = 0.01
CLIP_LIMIT = 0.05
MASKED_SCORE = -1e30

class Row:
    (
        enc_norm0_gain,
        enc_norm0_bias,
        enc_query_bias,
        enc_value_bias,
        enc_out_bias,
        enc_norm1_gain,
        enc_norm1_bias,
        enc_ffn_bias,
        enc_norm2_gain,
        enc_norm2_bias,
        dec_norm0_gain,
        dec_norm0_bias,
        dec_query_bias,
        dec_value_bias,
        dec_out_bias,
        dec_norm1_gain,
        dec_norm1_bias,
        cross_query_bias,
        cross_value_bias,
        cross_out_bias,
        dec_norm2_gain,
        dec_norm2_bias,
        dec_ffn_bias,
        dec_norm3_gain,
        dec_norm3_bias,
    ) = range(25)


class Part:
    (
        enc_wq,
        enc_wk,
        enc_wv,
        enc_out,
        enc_first,
        dec_wq,
        dec_wk,
        dec_wv,
        dec_out,
        cross_wq,
        cross_wk,
        cross_wv,
        cross_out,
        dec_first,
        enc_second,
        dec_second,
        position,
    ) = range(17)


FIRSTS = (Part.enc_first, Part.dec_first)


def product(left, right):
    return jnp.dot(left, right, preferred_element_type=jnp.float32)


def product_t(left, right):
    return lax.dot_general(
        left, right, (((1,), (1,)), ((), ())), preferred_element_type=jnp.float32
    )


def row_contract(left, right):
    return lax.dot_general(
        left, right, (((0,), (0,)), ((), ())), preferred_element_type=jnp.float32
    )


NORMAL = (((1,), (0,)), ((), ()))
RIGHT_T = (((1,), (1,)), ((), ()))
LEFT_T = (((0,), (0,)), ((), ()))
KERNEL_BYTES = 48 * 2**20


def dot(left, right, dims):
    return lax.dot_general(left, right, dims, preferred_element_type=jnp.float32)


def norm_forward(values, gain, bias):
    center = values - jnp.mean(values, -1, keepdims=True)
    scale = lax.rsqrt(jnp.mean(center * center, -1, keepdims=True) + NORM_EPS)
    unit = center * scale
    return unit * gain + bias, (unit, scale)


def norm_backward(grad, saved, gain):
    unit, scale = saved
    grad_unit = grad * gain
    shift = jnp.mean(grad_unit, -1, keepdims=True)
    slope = jnp.mean(grad_unit * unit, -1, keepdims=True)
    return (
        scale * (grad_unit - shift - unit * slope),
        jnp.sum(grad * unit, 0, keepdims=True),
        jnp.sum(grad, 0, keepdims=True),
    )


def column_sums(part, dims=NORMAL):
    count = part.shape[dims[0][1][0]]
    return dot(jnp.ones((8, count), jnp.bfloat16), part, dims)[:1]


def doc_positions(segment, limit):
    length = segment.shape[0]
    places = jnp.arange(length, dtype=jnp.int32)
    change = jnp.concatenate([jnp.ones((1,), bool), segment[1:] != segment[:-1]])
    starts = lax.cummax(jnp.where(change, places, 0), axis=0)
    return jnp.minimum(places - starts, limit - 1)


def combine_partial(first, second):
    top_value = jnp.maximum(first[0], second[0])
    sum_value = first[1] * jnp.exp(first[0] - top_value) + second[1] * jnp.exp(
        second[0] - top_value
    )
    return (top_value, sum_value, first[2] + second[2])


def project_queries(inputs_b, weight_q, bias_q):
    return ((product(inputs_b, weight_q) + bias_q) * 0.125).astype(jnp.bfloat16)


def project_pairs(inputs_b, weight_pair, bias_v):
    bias = jnp.concatenate([jnp.zeros_like(bias_v), bias_v])
    return (product(inputs_b, weight_pair) + bias).astype(jnp.bfloat16)


def query_backward(weight_q, grad_query):
    return (column_sums(grad_query), product_t(grad_query, weight_q))


def pairs_backward(weight_pair, pairs_grad):
    width = pairs_grad.shape[2]
    return (
        column_sums(pairs_grad[1]),
        product_t(pairs_grad[0], weight_pair[:, :width])
        + product_t(pairs_grad[1], weight_pair[:, width:]),
    )


def feed_forward(inputs_b, first_weight, first_bias, second_weight, second_bias):
    pre_act = dot(first_weight, inputs_b, (((0,), (1,)), ((), ()))) + first_bias[:, None]
    share = 0.5 + 0.5 * lax.erf(pre_act * 0.5**0.5)
    act_b = (pre_act * share).astype(jnp.bfloat16)
    slope = share + pre_act * jnp.exp(-0.5 * pre_act * pre_act) * (0.5 / math.pi) ** 0.5
    return (dot(act_b, second_weight, LEFT_T) + second_bias, slope, act_b)


def feed_backward(grad_branch, slope, first_weight, second_weight):
    branch_grad = grad_branch.astype(jnp.bfloat16)
    grad_pre = (dot(second_weight, branch_grad, RIGHT_T) * slope).astype(jnp.bfloat16)
    return (
        dot(grad_pre, first_weight, (((0,), (1,)), ((), ()))),
        grad_pre,
        column_sums(grad_pre, RIGHT_T),
        branch_grad,
        column_sums(branch_grad),
    )


def adam_step(weight, moment, square, grad, decay, rate):
    new_moment = BETA_ONE * moment + (1.0 - BETA_ONE) * grad
    new_square = BETA_TWO * square + (1.0 - BETA_TWO) * grad * grad
    direction = (
        new_moment
        / (1.0 - BETA_ONE**STEP)
        / (jnp.sqrt(new_square / (1.0 - BETA_TWO**STEP)) + ADAM_EPS)
    )
    return (new_moment, new_square, weight - rate * (direction + decay * weight))


def fill_mask(query_ref, key_ref, mask_ref):

    @pl.when(pl.program_id(0) == 0)
    def _():
        allowed = (key_ref[:, 0:1] == query_ref[0:1, :]) & (key_ref[:, 1:2] <= query_ref[1:2, :])
        mask_ref[...] = jnp.where(allowed, 1.0, 0.0)


def attention_kernel(
    query_ref,
    key_ref,
    q_ref,
    k_own_ref,
    k_came_ref,
    v_own_ref,
    v_came_ref,
    out_ref,
    turned_ref,
    logsum_ref,
    mask_ref,
    *,
    head_size,
):
    fill_mask(query_ref, key_ref, mask_ref)
    half = k_own_ref.shape[0]
    outs = []
    for head in range(q_ref.shape[1] // head_size):
        lanes = slice(head * head_size, (head + 1) * head_size)
        q = q_ref[:, lanes]
        keys = jnp.concatenate([k_own_ref[:, lanes], k_came_ref[:, lanes]], 0)
        scores = jnp.where(mask_ref[...] != 0.0, dot(keys, q, RIGHT_T), MASKED_SCORE)
        top = jnp.max(scores, 0, keepdims=True)
        terms = jnp.exp(scores - top)
        total = jnp.sum(terms, 0, keepdims=True)
        probs = (terms * (1.0 / total)).astype(jnp.bfloat16)
        outs.append(
            dot(v_own_ref[:, lanes], probs[:half], LEFT_T)
            + dot(v_came_ref[:, lanes], probs[half:], LEFT_T)
        )
        logsum_ref[0, head : head + 1, :] = top + jnp.log(total)
    out = jnp.concatenate(outs, 0)
    turned_ref[...] = out.astype(jnp.bfloat16)
    out_ref[...] = out.T.astype(jnp.bfloat16)


def attention_back_kernel(
    query_ref,
    key_ref,
    q_ref,
    k_own_ref,
    k_came_ref,
    v_own_ref,
    v_came_ref,
    grad_ref,
    logsum_ref,
    grad_q_ref,
    own_ref,
    other_ref,
    mask_ref,
    *,
    head_size,
):
    fill_mask(query_ref, key_ref, mask_ref)
    half = k_own_ref.shape[0]
    q_parts, k_parts, v_parts = [], [], []
    for head in range(q_ref.shape[1] // head_size):
        lanes = slice(head * head_size, (head + 1) * head_size)
        q, grad = q_ref[:, lanes], grad_ref[:, lanes]
        keys = jnp.concatenate([k_own_ref[:, lanes], k_came_ref[:, lanes]], 0)
        values = jnp.concatenate([v_own_ref[:, lanes], v_came_ref[:, lanes]], 0)
        scores = jnp.where(mask_ref[...] != 0.0, dot(keys, q, RIGHT_T), MASKED_SCORE)
        probs = jnp.exp(scores - logsum_ref[0, head : head + 1, :])
        grad_probs = dot(values, grad, RIGHT_T)
        shift = jnp.sum(grad_probs * probs, 0, keepdims=True)
        grad_scores = (probs * (grad_probs - shift)).astype(jnp.bfloat16)
        v_parts.append(dot(probs.astype(jnp.bfloat16), grad, NORMAL))
        k_parts.append(dot(grad_scores, q, NORMAL))
        q_parts.append(dot(keys, grad_scores, LEFT_T))
    grad_q_ref[...] = jnp.concatenate(q_parts, 0).T.astype(jnp.bfloat16) * jnp.bfloat16(0.125)
    for at, parts in enumerate((k_parts, v_parts)):
        grad_pair = jnp.concatenate(parts, 1)
        own_ref[at] = grad_pair[:half]
        other_ref[at] = grad_pair[half:]


def attention_call(kernel, results, marks, head_count, products, queries, pairs, extra=()):
    query_rows, width = queries.shape
    own, came = pairs
    key_rows = own.shape[0]
    head_size = width // head_count
    per_step = max(1, 128 // head_size)
    steps = head_count // per_step
    lanes = per_step * head_size
    heads = pl.BlockSpec((query_rows, lanes), lambda i: (0, i))
    keys = pl.BlockSpec((key_rows, lanes), lambda i: (0, i))
    values = pl.BlockSpec((key_rows, lanes), lambda i: (0, i + steps))
    sums = pl.BlockSpec((1, per_step, query_rows), lambda i: (i, 0, 0))
    kinds = {
        "q": (heads, (query_rows, width), jnp.bfloat16),
        "t": (pl.BlockSpec((lanes, query_rows), lambda i: (i, 0)), (width, query_rows), jnp.bfloat16),
        "s": (sums, (steps, per_step, query_rows), jnp.float32),
        "p": (
            pl.BlockSpec((2, key_rows, lanes), lambda i: (0, 0, i)),
            (2, key_rows, width),
            jnp.float32,
        ),
    }
    count = 2 * query_rows * key_rows
    return pl.pallas_call(
        functools.partial(kernel, head_size=head_size),
        grid=(steps,),
        in_specs=[pl.BlockSpec(part.shape, lambda i: (0, 0)) for part in marks]
        + [heads, keys, keys, values, values]
        + [heads, sums][: len(extra)],
        out_specs=[kinds[kind][0] for kind in results],
        out_shape=[jax.ShapeDtypeStruct(*kinds[kind][1:]) for kind in results],
        scratch_shapes=[pltpu.VMEM((2 * key_rows, query_rows), jnp.float32)],
        compiler_params=pltpu.CompilerParams(vmem_limit_bytes=KERNEL_BYTES),
        cost_estimate=pl.CostEstimate(
            flops=2 * products * count * width,
            bytes_accessed=2 * width * (query_rows + 2 * key_rows) * products,
            transcendentals=count * head_count,
        ),
    )(*marks, queries, own, came, own, came, *extra)


def branch_forward(queries, pairs, marks, weight_o, bias_o, head_count):
    mixed_b, mixed_t, logsum = attention_call(
        attention_kernel, "qts", marks, head_count, 2, queries, pairs
    )
    return (product(mixed_b, weight_o) + bias_o, mixed_t, logsum)


def branch_backward(grad_branch, queries, pairs, marks, logsum, weight_o, head_count):
    branch_grad = grad_branch.astype(jnp.bfloat16)
    grad_mixed = product_t(branch_grad, weight_o).astype(jnp.bfloat16)
    query_grad, own, other = attention_call(
        attention_back_kernel, "qpp", marks, head_count, 5, queries, pairs, (grad_mixed, logsum)
    )
    return (query_grad, (own, other), branch_grad, column_sums(branch_grad))


ALL = ("q", "p", "z", "x", "c")
SWAP = [(0, 1), (1, 0)]
SLOTS = 40


def swapped(part, axis):
    return lax.ppermute(part, axis, SWAP)


def one_hot(places, count):
    return (places[:, None] == jnp.arange(count, dtype=places.dtype)[None, :]).astype(jnp.bfloat16)


def shifted(part, axis, step):
    count = lax.axis_size(axis)
    return lax.ppermute(part, axis, [(i, (i + step) % count) for i in range(count)])


def line_in(part, axis):
    count = lax.axis_size(axis)
    return jnp.stack([part] + [shifted(part, axis, count - k) for k in range(1, count)])


def pair_in(part, axis, at):
    return jnp.stack([part, swapped(part, axis)], at)


def group_in(part, first):
    part = line_in(line_in(part, "p"), "z")
    if first == "q":
        part = pair_in(pair_in(part, "q", 0), "x", 0)
    else:
        part = pair_in(pair_in(part, "x", 0), "q", 1)
    return part


def group_rows(rows):
    half = rows.shape[1] // 2
    both = [group_in(rows[:, :half], "q"), group_in(rows[:, half:], "x")]
    return jnp.concatenate(both, -1).reshape(-1, rows.shape[1])


def send_half(part, axis, at):
    own = lax.index_in_dim(part, 0, at, keepdims=False)
    other = lax.index_in_dim(part, 1, at, keepdims=False)
    return own + swapped(other.astype(jnp.bfloat16), axis).astype(jnp.float32)


def send_line(part, axis):
    total = part[0]
    for k in range(1, lax.axis_size(axis)):
        total = total + shifted(part[k].astype(jnp.bfloat16), axis, k).astype(jnp.float32)
    return total


def group_sum(rows):
    ways = (2, 2, lax.axis_size("z"), lax.axis_size("p"))
    rows = rows.reshape(ways + (-1, rows.shape[-1]))
    half = rows.shape[-1] // 2
    first, second = rows[..., :half], rows[..., half:]
    first = send_half(send_half(first, "x", 0), "q", 0)
    second = send_half(send_half(second, "q", 1), "x", 0)
    return jnp.concatenate([send_line(send_line(part, "z"), "p") for part in (first, second)], -1)


def merge_stats(stats, beside):

    def merge(first, second):
        return jnp.stack(combine_partial(first, second))

    ways = (2, 2, lax.axis_size("z"), lax.axis_size("p"))
    stats = stats.reshape((3,) + ways + (-1,))
    stats = merge(stats[:, 0], beside(swapped(stats[:, 1], "x")))
    stats = merge(stats[:, 0], beside(swapped(stats[:, 1], "q")))
    for axis in ("z", "p"):
        total = stats[:, 0]
        came = [shifted(stats[:, k], axis, k) for k in range(1, lax.axis_size(axis))]
        if axis == "z":
            came = beside(came)
        for part in came:
            total = merge(total, part)
        stats = total
    return stats


def unpack_kernel(pack_ref, out_ref, *, columns):
    sides, owners, rows, total = pack_ref.shape
    for side in range(sides):
        for owner in range(owners):
            for at in range(total // columns):
                row = (owner * (total // columns) + at) * rows
                out_ref[row : row + rows, side * columns : (side + 1) * columns] = pack_ref[
                    side, owner, :, at * columns : (at + 1) * columns
                ]


def unpack_rows(pack, columns):
    sides, owners, rows, total = pack.shape
    each = rows * total // columns
    step = math.gcd(owners, 4)
    if rows % 16:
        pack = pack.reshape(sides, owners, rows, -1, columns)
        return jnp.transpose(pack, (1, 3, 2, 0, 4)).reshape(owners * each, sides * columns)
    return pl.pallas_call(
        functools.partial(unpack_kernel, columns=columns),
        grid=(owners // step,),
        in_specs=[pl.BlockSpec((sides, step, rows, total), lambda i: (0, i, 0, 0))],
        out_specs=pl.BlockSpec((step * each, sides * columns), lambda i: (i, 0)),
        out_shape=jax.ShapeDtypeStruct((owners * each, sides * columns), pack.dtype),
        cost_estimate=pl.CostEstimate(flops=0, bytes_accessed=4 * pack.size, transcendentals=0),
    )(pack)


def places_kernel(pack_ref, out_ref):
    sides, owners, _, _ = pack_ref.shape
    rows, columns = out_ref.shape[0] // owners, out_ref.shape[1] // sides
    across = columns // 128
    for side in range(sides):
        for owner in range(owners):
            for tile in range(rows // 16 * across):
                row, lane = tile // 4 * 16, tile % 4 * 128
                to_row = owner * rows + tile // across * 16
                to_lane = side * columns + tile % across * 128
                out_ref[to_row : to_row + 16, to_lane : to_lane + 128] = pack_ref[
                    side, owner, row : row + 16, lane : lane + 128
                ]


def unpack_places(pack, at, rows, columns):
    sides, owners, height, _ = pack.shape
    step = math.gcd(owners, 8)
    return pl.pallas_call(
        places_kernel,
        grid=(owners // step,),
        in_specs=[pl.BlockSpec((sides, step, height, 512), lambda i: (0, i, 0, at // 512))],
        out_specs=pl.BlockSpec((step * rows, sides * columns), lambda i: (i, 0)),
        out_shape=jax.ShapeDtypeStruct((owners * rows, sides * columns), pack.dtype),
        cost_estimate=pl.CostEstimate(
            flops=0, bytes_accessed=4 * owners * rows * sides * columns, transcendentals=0
        ),
    )(pack)


def hold(*trees):
    return lax.optimization_barrier(trees)


def all_pairs(part, combine, whole):
    for axis in ALL:
        count = lax.axis_size(axis)
        if count & (count - 1):
            part = whole(part, axis)
            continue
        step = 1
        while step < count:
            part = combine(part, lax.ppermute(part, axis, [(i, i ^ step) for i in range(count)]))
            step *= 2
    return part


def all_sum(part):
    return all_pairs(part, jnp.add, lax.psum)


def pick(part, axis, index):
    return lax.dynamic_index_in_dim(part, index, axis, keepdims=False)


def own_first(part, axis):
    half = part.shape[axis] // 2
    first = lax.slice_in_dim(part, 0, half, axis=axis)
    second = lax.slice_in_dim(part, half, 2 * half, axis=axis)
    here = lax.axis_index("q") == 0
    return jnp.where(here, first, second), jnp.where(here, second, first)


def line_kernel(place_ref, *refs, unit):
    count = (len(refs) - 2) // 2
    kept_ref, sent_ref = refs[-2:]
    blocks = []
    for own, other in zip(refs[:count], refs[count : 2 * count]):
        total = own[0] + other[0].astype(jnp.float32)
        blocks += [total[at : at + unit] for at in range(0, total.shape[0], unit)]

    @pl.when(pl.program_id(0) == 0)
    def _():
        at = 0
        for block in blocks:
            kept_ref[:, at : at + block.shape[1]] = block
            at += block.shape[1]

    @pl.when(pl.program_id(0) > 0)
    def _():
        at = 0
        for block in blocks:
            sent_ref[0, :, at : at + block.shape[1]] = block.astype(jnp.bfloat16)
            at += block.shape[1]


def line_parts(owns, others, unit):
    lines = owns[0].shape[0]
    columns = sum(own.shape[1] // unit * own.shape[2] for own in owns)
    specs = [
        pl.BlockSpec((1,) + own.shape[1:], lambda k, place: ((place[0] + k) % lines, 0, 0))
        for own in owns
    ]
    return pl.pallas_call(
        functools.partial(line_kernel, unit=unit),
        grid_spec=pltpu.PrefetchScalarGridSpec(
            num_scalar_prefetch=1,
            grid=(lines,),
            in_specs=specs * 2,
            out_specs=[
                pl.BlockSpec((unit, columns), lambda k, place: (0, 0)),
                pl.BlockSpec((1, unit, columns), lambda k, place: (jnp.maximum(k - 1, 0), 0, 0)),
            ],
        ),
        out_shape=[
            jax.ShapeDtypeStruct((unit, columns), jnp.float32),
            jax.ShapeDtypeStruct((lines - 1, unit, columns), jnp.bfloat16),
        ],
        compiler_params=pltpu.CompilerParams(vmem_limit_bytes=KERNEL_BYTES),
        cost_estimate=pl.CostEstimate(
            flops=lines * unit * columns, bytes_accessed=8 * lines * unit * columns, transcendentals=0
        ),
    )(lax.axis_index("z").astype(jnp.int32).reshape(1), *owns, *others)


def factor_kernel(place_ref, *refs, turned, halves):
    (near, near_came, far, far_came), rights = refs[:4], refs[4:-2]
    kept_ref, sent_ref = refs[-2:]
    dims = RIGHT_T if turned else NORMAL

    def rows(ref):
        block = ref[...]
        return block.reshape(-1, block.shape[-1])

    def side(own, came, at):
        right, right_came = (ref[...].reshape(ref.shape[-2:]) for ref in rights[2 * at : 2 * at + 2])
        return dot(rows(own), right, dims) + dot(rows(came), right_came, dims)

    if halves:
        kept_ref[0], kept_ref[1] = side(near, near_came, 0), side(far, far_came, 0)
        sent_ref[0] = side(near, near_came, 1).astype(jnp.bfloat16)
        sent_ref[1] = side(far, far_came, 1).astype(jnp.bfloat16)
    else:
        kept_ref[...] = side(near, near_came, 0)
        sent_ref[...] = side(far, far_came, 0).astype(jnp.bfloat16)


def factor_parts(left, right, names, halves):
    own, came = left
    right, right_came = right
    _, lines, _, rows, tokens = own.shape
    turned = right.ndim == 2
    width = right.shape[0] if turned else right.shape[2]
    step = width // 2 if halves or width < 3072 else 384
    blocks = width // step
    place = [lax.axis_index("x"), lax.axis_index("q")]
    place += [left_at for _, left_at, _ in names] + [right_at or 0 for _, _, right_at in names]
    place = jnp.stack([jnp.asarray(part, jnp.int32) for part in place])
    count, groups = lines * rows, len(names)
    inner = 1 if halves else blocks

    def left_spec(far):

        def at_place(j, at):
            return at[2 + j // inner], 0, 1 - at[0] if far else at[0], 0, 0

        return pl.BlockSpec((1, lines, 1, rows, tokens), at_place)

    def right_spec(other):

        def at_place(j, at):
            if turned:
                return j, 0
            part = (1 - at[1] if other else at[1]) if halves else j % inner
            return at[2 + groups + j // inner], 0, part

        return pl.BlockSpec((step, tokens) if turned else (1, tokens, step), at_place)

    steps = groups * inner
    shape = (2, count, steps * step) if halves else (count, steps * step)
    out_spec = (
        pl.BlockSpec((2, count, step), lambda j, at: (0, 0, j))
        if halves
        else pl.BlockSpec((count, step), lambda j, at: (0, j))
    )
    rights = [right, right_came] * (2 if halves else 1)
    return pl.pallas_call(
        functools.partial(factor_kernel, turned=turned, halves=halves),
        grid_spec=pltpu.PrefetchScalarGridSpec(
            num_scalar_prefetch=1,
            grid=(steps,),
            in_specs=[left_spec(False), left_spec(False), left_spec(True), left_spec(True)]
            + [right_spec(at >= 2) for at in range(len(rights))],
            out_specs=[out_spec, out_spec],
        ),
        out_shape=[
            jax.ShapeDtypeStruct(shape, jnp.float32),
            jax.ShapeDtypeStruct(shape, jnp.bfloat16),
        ],
        compiler_params=pltpu.CompilerParams(vmem_limit_bytes=KERNEL_BYTES),
        cost_estimate=pl.CostEstimate(
            flops=8 * count * tokens * width * groups,
            bytes_accessed=8 * count * tokens + (4 * tokens + 12 * count) * width * groups,
            transcendentals=0,
        ),
    )(place, own, came, own, came, *rights)


class Group:
    def __init__(self, *factors, ready=(), mixed=0):
        core, side = lax.axis_index("c"), lax.axis_index("x")
        self.names, self.kept, self.flight, self.ways, self.rows = [], [], [], [], []
        self.mixed = mixed
        self.stage = 0
        for way, left, right, names in factors:
            kept, sent = factor_parts(left, right, names, not way)
            self.take([name for name, _, _ in names], kept, sent, way)
        for name, grad in ready:
            grad = grad.reshape(lax.axis_size("z"), 2, 2, -1, grad.shape[1])
            grad = pick(grad, 2, core) + swapped(pick(grad, 2, 1 - core), "c")
            self.take([name], pick(grad, 1, side), pick(grad, 1, 1 - side), True)
        self.unit = min(self.rows)

    def before(self, *live):
        self.kept, live = hold(self.kept, live)
        return live if len(live) > 1 else live[0]

    def take(self, names, kept, sent, way):
        self.names.append(names[:1] if way else names)
        kept, sent = (part.reshape(-1, part.shape[-1]) for part in (kept, sent))
        self.kept.append(kept)
        self.ways.append(way)
        self.rows.append(kept.shape[0] // lax.axis_size("z") // (1 if way else 2))
        self.flight.append(swapped(sent.astype(jnp.bfloat16), "x" if way else "q"))

    def advance(self):
        self.stage += 1
        lines = lax.axis_size("z")
        if self.stage == 1:
            for at, way in enumerate(self.ways):
                kept, came = self.kept[at], self.flight[at]
                total = kept + came.astype(jnp.float32)
                half = total.shape[0] // 2
                near, far = own_first(total, 1) if way else (total[:half], total[half:])
                self.kept[at] = near.reshape(lines, -1, near.shape[1])
                far = far.astype(jnp.bfloat16).reshape(lines, -1, far.shape[1])
                self.flight[at] = swapped(far, "q" if way else "x")
        elif self.stage == 2:
            self.shapes = [part.shape[1:] for part in self.kept]
            self.total, sent = line_parts(self.kept, self.flight, self.unit)
            self.flight = [shifted(sent[k], "z", k + 1) for k in range(sent.shape[0])]
        elif self.stage == 3:
            for part in self.flight:
                self.total = self.total + part.astype(jnp.float32)
            if lax.axis_size("p") > 1:
                self.total = lax.psum(self.total, "p")
                self.mixed = sum(len(names) for names in self.names)
            self.spans = []
            for names, (rows, columns) in zip(self.names, self.shapes):
                for name in names:
                    self.spans.append((name, rows // self.unit, columns // len(names)))
            width = sum(blocks * columns for _, blocks, columns in self.spans[: self.mixed])
            self.flight = swapped(self.total[:, :width], "q") if self.mixed else ()
        else:
            at, self.done = 0, {}
            for turn, (name, blocks, columns) in enumerate(self.spans):
                parts = []
                for _ in range(blocks):
                    near = self.total[:, at : at + columns]
                    if turn < self.mixed:
                        far = self.flight[:, at : at + columns]
                        near = jnp.where(
                            lax.axis_index("q") == 0,
                            jnp.concatenate([near, far], 1),
                            jnp.concatenate([far, near], 1),
                        )
                    parts.append(near)
                    at += columns
                self.done[name] = parts[0] if len(parts) == 1 else jnp.concatenate(parts, 0)


class Reducer:

    def __init__(self):
        self.moving = []
        self.done = {}

    def add(self, item):
        self.moving.append(item)
        return item

    def step(self, *live):
        live, flights = hold(live, [item.flight for item in self.moving])
        for item, flight in zip(self.moving, flights):
            item.flight = flight
        self.advance()
        return live

    def advance(self):
        for item in self.moving:
            item.advance()
            if item.stage == 4:
                self.done.update(item.done)
        self.moving = [item for item in self.moving if item.stage < 4]


def pairs_in(pairs):
    both = (pairs, swapped(pairs, "c"))
    if lax.axis_size("p") > 1:
        both = tuple(lax.all_gather(part, "p", axis=0, tiled=True) for part in both)
    return both


def pairs_back(grads):
    if lax.axis_size("p") > 1:
        grads = tuple(
            lax.psum_scatter(part, "p", scatter_dimension=1, tiled=True) for part in grads
        )
    own, other = grads
    return (own + swapped(other, "c")).astype(jnp.bfloat16)


def both_cores(part):
    return part, swapped(part, "c")


def turn_kernel(core_ref, *refs, rows):
    parts, (own_ref, other_ref) = refs[:-2], refs[-2:]
    lines = own_ref.shape[1]
    for at, ref in enumerate(parts):
        part = ref[...]
        if part.shape[0] != lines * 4 * rows:
            part = part.astype(jnp.float32).T.astype(jnp.bfloat16)
        blocks = [part[k * rows : (k + 1) * rows] for k in range(4 * lines)]
        for here in range(2):

            @pl.when(core_ref[0] == here)
            def _():
                for line in range(lines):
                    for side in range(2):
                        first = (line * 2 + side) * 2
                        own_ref[at, line, side] = blocks[first + here]
                        other_ref[at, line, side] = blocks[first + 1 - here]


def turn_rows(parts, turned, rows):
    tokens, width = parts[0].shape
    lines = width // (4 * rows)
    count = len(parts) + len(turned)
    shape = (count, lines, 2, rows, tokens)
    if rows % 16 or tokens == width:
        whole = jnp.stack([part.T for part in parts] + list(turned))
        whole = whole.reshape(count, lines, 2, 2, rows, tokens)
        core = lax.axis_index("c")
        return pick(whole, 3, core), pick(whole, 3, 1 - core)
    vmem = pl.BlockSpec(memory_space=pltpu.VMEM)
    return pl.pallas_call(
        functools.partial(turn_kernel, rows=rows),
        in_specs=[pl.BlockSpec(memory_space=pltpu.SMEM)] + [vmem] * count,
        out_specs=[vmem, vmem],
        out_shape=[jax.ShapeDtypeStruct(shape, jnp.bfloat16)] * 2,
        compiler_params=pltpu.CompilerParams(vmem_limit_bytes=KERNEL_BYTES),
        cost_estimate=pl.CostEstimate(
            flops=0, bytes_accessed=4 * count * tokens * width, transcendentals=0
        ),
    )(lax.axis_index("c").astype(jnp.int32).reshape(1), *parts, *turned)


def pack_kernel(*refs, width):
    out_ref = refs[-1]
    at = 0
    for ref in refs[:-1]:
        for column in range(0, ref.shape[1], width):
            out_ref[at : at + 1, :] = ref[0:1, column : column + width]
            at += 1


def pack_rows(parts, width):
    count = sum(part.shape[1] // width for part in parts)
    vmem = pl.BlockSpec(memory_space=pltpu.VMEM)
    return pl.pallas_call(
        functools.partial(pack_kernel, width=width),
        in_specs=[vmem] * len(parts),
        out_specs=vmem,
        out_shape=jax.ShapeDtypeStruct((count, width), jnp.float32),
    )(*parts)


def head_kernel(table_ref, rows_ref, ids_ref, labels_ref, terms_ref, label_rows_ref, stats_ref):
    scores = dot(rows_ref[...], table_ref[...], RIGHT_T)
    ids = ids_ref[0:1, :]
    scores = jnp.where(ids < V, scores, MASKED_SCORE)
    top = jnp.max(scores, 1, keepdims=True)
    terms = jnp.exp(scores - top)
    total = jnp.sum(terms, 1, keepdims=True)
    terms_ref[...] = terms.astype(jnp.bfloat16)
    hit = ids == labels_ref[:, 0:1]
    label = jnp.sum(jnp.where(hit, scores, 0.0), 1, keepdims=True)
    chosen = jnp.where(hit, 1.0, 0.0).astype(jnp.bfloat16)
    label_rows_ref[...] = dot(chosen, table_ref[...], NORMAL).astype(jnp.bfloat16)
    lane = lax.broadcasted_iota(jnp.int32, (scores.shape[0], 128), 1)
    stats = jnp.where(lane == 0, top, jnp.where(lane == 1, total, label))
    stats_ref[...] = stats.T[:8]


def head_forward(table, rows, ids, labels):
    columns, width = table.shape
    count = rows.shape[0]
    step = math.gcd(count, 256)
    return pl.pallas_call(
        head_kernel,
        grid=(count // step,),
        in_specs=[
            pl.BlockSpec((columns, width), lambda i: (0, 0)),
            pl.BlockSpec((step, width), lambda i: (i, 0)),
            pl.BlockSpec((1, columns), lambda i: (0, 0)),
            pl.BlockSpec((step, 1), lambda i: (i, 0)),
        ],
        out_specs=[
            pl.BlockSpec((step, columns), lambda i: (i, 0)),
            pl.BlockSpec((step, width), lambda i: (i, 0)),
            pl.BlockSpec((8, step), lambda i: (0, i)),
        ],
        out_shape=[
            jax.ShapeDtypeStruct((count, columns), jnp.bfloat16),
            jax.ShapeDtypeStruct((count, width), jnp.bfloat16),
            jax.ShapeDtypeStruct((8, count), jnp.float32),
        ],
        compiler_params=pltpu.CompilerParams(vmem_limit_bytes=KERNEL_BYTES),
        cost_estimate=pl.CostEstimate(
            flops=4 * columns * width * count,
            bytes_accessed=2 * (columns * width + 2 * count * width + columns * count),
            transcendentals=columns * count,
        ),
    )(table, rows, ids[None, :], labels[:, None])


def table_kernel(terms_ref, rows_ref, ids_ref, marks_ref, labels_ref, own_ref, other_ref, total_ref, *, scale):
    probs = terms_ref[...].astype(jnp.float32) * marks_ref[:, 0:1]
    hit = ids_ref[0:1, :] == labels_ref[:, 0:1]
    grad = ((probs - jnp.where(hit, 1.0, 0.0)) * scale).astype(jnp.bfloat16)
    part = dot(grad, rows_ref[...], LEFT_T)

    @pl.when(pl.program_id(0) == 0)
    def _():
        total_ref[...] = part

    @pl.when(pl.program_id(0) > 0)
    def _():
        total_ref[...] += part

    @pl.when(pl.program_id(0) == pl.num_programs(0) - 1)
    def _():
        own_ref[...] = total_ref[: own_ref.shape[0]]
        other_ref[...] = total_ref[own_ref.shape[0] :]


def head_table(terms, rows, ids, row_scale, labels, scale):
    count, columns = terms.shape
    width = rows.shape[1]
    step = math.gcd(count, 256)
    half = pl.BlockSpec((columns // 2, width), lambda i: (0, 0))
    return pl.pallas_call(
        functools.partial(table_kernel, scale=scale),
        grid=(count // step,),
        in_specs=[
            pl.BlockSpec((step, columns), lambda i: (i, 0)),
            pl.BlockSpec((step, width), lambda i: (i, 0)),
            pl.BlockSpec((1, columns), lambda i: (0, 0)),
            pl.BlockSpec((step, 1), lambda i: (i, 0)),
            pl.BlockSpec((step, 1), lambda i: (i, 0)),
        ],
        out_specs=[half, half],
        out_shape=[jax.ShapeDtypeStruct((columns // 2, width), jnp.float32)] * 2,
        scratch_shapes=[pltpu.VMEM((columns, width), jnp.float32)],
        compiler_params=pltpu.CompilerParams(vmem_limit_bytes=KERNEL_BYTES),
        cost_estimate=pl.CostEstimate(
            flops=2 * columns * width * count,
            bytes_accessed=4 * columns * width + 2 * count * (width + columns),
            transcendentals=0,
        ),
    )(terms, rows, ids[None, :], row_scale, labels[:, None])


class Lookup:
    def __init__(self, token_ids, own_rows):
        owners = 1
        for axis in ALL:
            owners *= lax.axis_size(axis)
        self.owners = owners
        self.own_rows = own_rows
        count = token_ids.shape[0]
        places = jnp.arange(count, dtype=jnp.int32)
        owner = token_ids // own_rows
        same = token_ids[:, None] == token_ids[None, :]
        first = jnp.min(jnp.where(same, places[None, :], count), 1)
        is_first = first == places
        ahead = (owner[:, None] == owner[None, :]) & is_first[None, :] & (places[None, :] < first[:, None])
        self.rank = jnp.sum(ahead.astype(jnp.int32), 1)
        self.owner = owner
        self.is_first = is_first
        self.local_id = token_ids - owner * own_rows
    def round_places(self, turn):
        rank = self.rank - turn * SLOTS
        inside = (rank >= 0) & (rank < SLOTS)
        slot = jnp.where(inside, self.owner * SLOTS + rank, -1)
        to_owner = jnp.where(
            (self.owner[:, None] == jnp.arange(self.owners)[None, :]) & self.is_first[:, None],
            (self.local_id + 1).astype(jnp.float32)[:, None],
            0.0,
        )
        to_slot = (rank[:, None] == jnp.arange(SLOTS)[None, :]).astype(jnp.float32)
        asked = lax.dot_general(to_owner, to_slot, (((0,), (0,)), ((), ())), precision=PRECISE)
        asked = jnp.round(asked).astype(jnp.int32) - 1
        last = jnp.broadcast_to(jnp.max(self.rank), (self.owners, 1))
        wanted = lax.all_to_all(jnp.concatenate([asked, last], 1), ALL, 0, 0, tiled=True)
        self.rounds = jnp.max(wanted[:, SLOTS:]) // SLOTS + 1
        wanted = wanted[:, :SLOTS].reshape(-1)
        return one_hot(slot, self.owners * SLOTS), one_hot(wanted, self.own_rows)

    def fetch_round(self, turn, table_low):
        to_slot, to_row = self.round_places(turn)
        sent = product(to_row, table_low).astype(jnp.bfloat16)
        rows = lax.all_to_all(sent, ALL, 0, 0, tiled=True)
        return product(to_slot, rows), (to_slot, to_row)

    def fetch(self, table_low):
        rows, self.kept = self.fetch_round(0, table_low)
        rounds = self.rounds
        rows = lax.cond(
            rounds > 1,
            lambda: lax.fori_loop(
                1, rounds, lambda turn, total: total + self.fetch_round(turn, table_low)[0], rows
            ),
            lambda: rows,
        )
        self.rounds = rounds
        return rows

    def give_round(self, places, grads_b):
        to_slot, to_row = places
        sent = row_contract(to_slot, grads_b).astype(jnp.bfloat16)
        back = lax.all_to_all(sent, ALL, 0, 0, tiled=True)
        return row_contract(to_row, back)

    def give(self, total, grads_b):
        total = total + self.give_round(self.kept, grads_b)
        rounds = self.rounds
        return lax.cond(
            rounds > 1,
            lambda: lax.fori_loop(
                1,
                rounds,
                lambda turn, sums: sums + self.give_round(self.round_places(turn), grads_b),
                total,
            ),
            lambda: total,
        )


def local(
    table_weight,
    table_moment,
    table_square,
    position_weight,
    position_moment,
    position_square,
    wide_weight,
    wide_moment,
    wide_square,
    down_weight,
    down_moment,
    down_square,
    vector_weight,
    vector_moment,
    vector_square,
    source_ids,
    target_ids,
    target_labels,
    source_segments,
    target_segments,
    completion_idx,
):
    cuts = lax.axis_size("p")
    ctx_count = 2 * cuts
    shard_count = lax.axis_size("z") * 4
    core = lax.axis_index("c")
    block = lax.axis_index("p") * 2 + core
    ctx_index = lax.axis_index("q") * cuts + lax.axis_index("p")
    tokens = source_ids.shape[1]
    comp_count = completion_idx.shape[1]
    width = vector_weight.shape[1]
    hidden = down_weight.shape[1] * shard_count
    head_count = H
    own_rows = table_weight.shape[0]
    table_low = table_weight.astype(jnp.bfloat16)

    small = jnp.concatenate(
        [source_ids, target_ids, target_labels, source_segments, target_segments, completion_idx], 1
    )
    small = lax.all_gather(small[0], ("q", "p", "c"))
    small = small.reshape(ctx_count, 2, -1)
    small = lax.dynamic_index_in_dim(small, lax.axis_index("q"), 1, keepdims=False)
    src_ids, tgt_ids, tgt_labels, src_seg, tgt_seg = (
        small[:, k * tokens : (k + 1) * tokens] for k in range(5)
    )

    def own_block(blocks):
        return lax.dynamic_index_in_dim(blocks, block, 0, keepdims=False)

    def key_order(blocks):
        pairs = blocks.reshape(cuts, 2, -1)
        pairs = jnp.where(core == 0, pairs, pairs[:, ::-1])
        return jnp.moveaxis(pairs, 1, 0).reshape(-1)

    comp_places = own_block(small[:, 5 * tokens :])
    comp_hit = one_hot(comp_places, tokens)
    own_labels = jnp.take(own_block(tgt_labels), comp_places)

    lookup = Lookup(jnp.concatenate([own_block(src_ids), own_block(tgt_ids)]), own_rows)
    token_rows = lookup.fetch(table_low)

    wide_low = wide_weight.astype(jnp.bfloat16)
    down_low = down_weight.astype(jnp.bfloat16)
    shard_rows, span = wide_low.shape
    bounds = [0, span * 2 // 5, span * 4 // 5, span]
    place_low = position_weight.astype(jnp.bfloat16)
    place_rows, place_columns = place_low.shape
    early_width = span - bounds[2] + bounds[1]
    by_tiles = (
        place_rows * place_columns == shard_rows * 512
        and place_columns % 128 == 0
        and shard_rows % 16 == 0
        and early_width % 512 == 0
    )
    if by_tiles:
        tiles = place_low.reshape(place_rows // 16, 16, place_columns // 128, 128)
        tiles = jnp.moveaxis(tiles, 1, 2).reshape(shard_rows // 16, 4, 16, 128)
        place_pack = jnp.moveaxis(tiles, 1, 2).reshape(shard_rows, 512)
    else:
        place_pack = place_low.reshape(shard_rows, -1)

    def gathered(parts):
        part = parts[0] if len(parts) == 1 else jnp.concatenate(parts, 1)
        return lax.all_gather(part, ALL).reshape(ctx_count, width, part.shape[1])

    def flat_down(part):
        part = part.reshape(-1, shard_rows, part.shape[1])
        return jnp.moveaxis(part, 0, 1).reshape(shard_rows, -1)

    def tall_down(pack):
        return unpack_rows(pack.reshape(ctx_count, shard_count, shard_rows, -1), width // ctx_count)

    early = gathered([wide_low[:, : bounds[1]], wide_low[:, bounds[2] :], place_pack])
    middle = gathered([wide_low[:, bounds[1] : bounds[2]], flat_down(down_low[0])])
    late = gathered([flat_down(down_low[1])])
    if by_tiles:
        position_full = unpack_places(
            early.reshape(ctx_count, shard_count, shard_rows, -1),
            early_width,
            place_rows,
            place_columns,
        )
    else:
        position_full = early[:, :, early_width:].reshape(
            (ctx_count, shard_count) + position_weight.shape
        )
        position_full = jnp.moveaxis(position_full, 0, 2).reshape(-1, width)

    def columns(name, size=None):
        start = starts[name]
        size = size or (hidden if name in FIRSTS else width)
        pieces = []
        while size:
            side, inner = divmod(start, span)
            turn = max(k for k in range(3) if bounds[k] <= inner)
            take = min(size, bounds[turn + 1] - inner)
            source = middle if turn == 1 else early
            at = inner - (0, bounds[1], bounds[2] - bounds[1])[turn]
            pieces.append(source[side, :, at : at + take])
            start, size = start + take, size - take
        return pieces[0] if len(pieces) == 1 else jnp.concatenate(pieces, 1)

    def vector_row(name):
        return vector_weight[name]

    blocks = hidden // width
    base_row = Row.dec_norm3_bias + 1
    enc_first_bias = vector_weight[base_row : base_row + blocks].reshape(-1)
    dec_first_bias = vector_weight[base_row + blocks : base_row + 2 * blocks].reshape(-1)
    names = range(Part.dec_first + 1)
    starts, offset = {}, 0
    for name in names:
        starts[name] = offset
        offset += hidden if name in FIRSTS else width


    table_count = position_full.shape[0]
    src_pos = own_block(doc_positions(src_seg.reshape(-1), table_count).reshape(ctx_count, -1))
    tgt_pos = own_block(doc_positions(tgt_seg.reshape(-1), table_count).reshape(ctx_count, -1))
    src_onehot = one_hot(src_pos, table_count)
    tgt_onehot = one_hot(tgt_pos, table_count)
    src_input = token_rows[:tokens] + product(src_onehot, position_full)
    tgt_input = token_rows[tokens:] + product(tgt_onehot, position_full)

    key_places = key_order(jnp.arange(ctx_count * tokens).reshape(ctx_count, tokens))
    src_keys_seg = key_order(src_seg)
    tgt_keys_seg = key_order(tgt_seg)
    own_src_seg = own_block(src_seg)
    own_tgt_seg = own_block(tgt_seg)
    def no_limit(seg):
        return jnp.full_like(seg, ctx_count * tokens)

    comp_seg = jnp.take(own_tgt_seg, comp_places)

    def marks(query_seg, query_last, key_seg):
        return (
            jnp.pad(jnp.stack([query_seg, query_last]), ((0, 6), (0, 0))),
            jnp.pad(jnp.stack([key_seg, key_places], 1), ((0, 0), (0, 126))),
        )

    enc_marks = marks(own_src_seg, no_limit(own_src_seg), src_keys_seg)
    self_marks = marks(comp_seg, block * tokens + comp_places, tgt_keys_seg)
    cross_marks = marks(comp_seg, no_limit(comp_seg), src_keys_seg)

    def norm(values, gain, bias):
        return norm_forward(values, vector_row(gain), vector_row(bias))

    enc_norm0, enc_saved0 = norm(src_input, Row.enc_norm0_gain, Row.enc_norm0_bias)
    enc_in_b = enc_norm0.astype(jnp.bfloat16)
    enc_queries = project_queries(enc_in_b, columns(Part.enc_wq), vector_row(Row.enc_query_bias))
    enc_pairs = project_pairs(
        enc_in_b, columns(Part.enc_wk, 2 * width), vector_row(Row.enc_value_bias)
    )
    enc_pairs_all = pairs_in(enc_pairs)
    dec_norm0, dec_saved0 = norm(tgt_input, Row.dec_norm0_gain, Row.dec_norm0_bias)
    dec_in_b = dec_norm0.astype(jnp.bfloat16)
    comp_exact = comp_hit.astype(jnp.float32)
    comp_norm0 = jnp.dot(comp_exact, dec_norm0, precision=PRECISE)
    comp_in_b = product(comp_hit, dec_in_b).astype(jnp.bfloat16)
    dec_queries = project_queries(comp_in_b, columns(Part.dec_wq), vector_row(Row.dec_query_bias))
    dec_pairs = project_pairs(
        dec_in_b, columns(Part.dec_wk, 2 * width), vector_row(Row.dec_value_bias)
    )
    dec_pairs_all = pairs_in(dec_pairs)
    enc_branch, enc_mixed_t, enc_logsum = branch_forward(
        enc_queries,
        enc_pairs_all,
        enc_marks,
        columns(Part.enc_out),
        vector_row(Row.enc_out_bias),
        head_count,
    )
    enc_norm1, enc_saved1 = norm(enc_norm0 + enc_branch, Row.enc_norm1_gain, Row.enc_norm1_bias)
    self_branch, self_mixed_t, self_logsum = branch_forward(
        dec_queries,
        dec_pairs_all,
        self_marks,
        columns(Part.dec_out),
        vector_row(Row.dec_out_bias),
        head_count,
    )
    dec_norm1, dec_saved1 = norm(comp_norm0 + self_branch, Row.dec_norm1_gain, Row.dec_norm1_bias)
    cross_in_b = dec_norm1.astype(jnp.bfloat16)
    cross_queries = project_queries(
        cross_in_b, columns(Part.cross_wq), vector_row(Row.cross_query_bias)
    )

    enc_norm1, cross_queries, middle, own_labels = hold(
        enc_norm1, cross_queries, middle, own_labels
    )
    head_labels = group_in(own_labels, "q").reshape(-1)
    enc_first, enc_second = (
        columns(Part.enc_first),
        tall_down(middle[:, :, bounds[2] - bounds[1] :]),
    )
    enc_mid_b = enc_norm1.astype(jnp.bfloat16)
    enc_ffn, enc_slope, enc_act_t = feed_forward(
        enc_mid_b, enc_first, enc_first_bias, enc_second, vector_row(Row.enc_ffn_bias)
    )
    encoded, enc_saved2 = norm(enc_norm1 + enc_ffn, Row.enc_norm2_gain, Row.enc_norm2_bias)
    encoded_b = encoded.astype(jnp.bfloat16)
    cross_pair_weights = columns(Part.cross_wk, 2 * width)
    cross_pairs = project_pairs(encoded_b, cross_pair_weights, vector_row(Row.cross_value_bias))
    cross_pairs_all = pairs_in(cross_pairs)
    cross_branch, cross_mixed_t, cross_logsum = branch_forward(
        cross_queries,
        cross_pairs_all,
        cross_marks,
        columns(Part.cross_out),
        vector_row(Row.cross_out_bias),
        head_count,
    )
    dec_norm2, dec_saved2 = norm(dec_norm1 + cross_branch, Row.dec_norm2_gain, Row.dec_norm2_bias)
    dec_norm2, late, head_labels = hold(dec_norm2, late, head_labels)
    dec_first, dec_second = columns(Part.dec_first), tall_down(late)
    dec_mid_b = dec_norm2.astype(jnp.bfloat16)
    dec_ffn, dec_slope, dec_act_t = feed_forward(
        dec_mid_b, dec_first, dec_first_bias, dec_second, vector_row(Row.dec_ffn_bias)
    )
    final, dec_saved3 = norm(dec_norm2 + dec_ffn, Row.dec_norm3_gain, Row.dec_norm3_bias)
    final_b = final.astype(jnp.bfloat16)
    head_rows = group_rows(final_b)

    to_turn = (
        (enc_in_b, dec_in_b, enc_mid_b, encoded_b),
        (comp_in_b, cross_in_b, dec_mid_b),
    )
    to_turn, head_labels, _ = hold(to_turn, head_labels, final_b)

    def both_lefts(parts, turned):
        own, other = turn_rows(parts, turned, shard_rows)
        return own, swapped(other, "c")

    left = both_lefts(to_turn[0], (enc_mixed_t,))
    comp_left = both_lefts(to_turn[1], (self_mixed_t, cross_mixed_t))
    group_start = 0
    for axis in ("q", "p", "z", "x"):
        group_start = group_start * lax.axis_size(axis) + lax.axis_index(axis)
    own_ids = jnp.arange(own_rows, dtype=jnp.int32)
    column_ids = jnp.concatenate(
        [(group_start * 2 + core) * own_rows + own_ids, (group_start * 2 + 1 - core) * own_rows + own_ids]
    )
    table_pair = jnp.concatenate([table_low, swapped(table_low, "c")], 0)

    def act_left(act_t):
        act_t = act_t.reshape(lax.axis_size("z"), 2, 2, -1, act_t.shape[1])
        own, other = pick(act_t, 2, core), pick(act_t, 2, 1 - core)
        return own[None], swapped(other, "c")[None]

    enc_act, dec_act = act_left(enc_act_t), act_left(dec_act_t)
    head_rows, left, comp_left, enc_act, dec_act, table_pair = hold(
        head_rows, left, comp_left, enc_act, dec_act, table_pair
    )
    terms, label_rows, stats = head_forward(table_pair, head_rows, column_ids, head_labels)
    quarter = terms.shape[0] // 4
    mixed = []

    def beside(part):
        at = len(mixed) * quarter
        rows = product(terms[at : at + quarter], table_pair)
        part, rows = hold(part, rows)
        mixed.append(rows)
        return part

    merged_top, merged_sum, merged_label = merge_stats(stats[:3], beside)
    own_logsum = merged_top + jnp.log(merged_sum)
    loss_local = jnp.sum(own_logsum - merged_label)
    logsum_rows = beside(line_in(line_in(own_logsum, "p"), "z"))
    logsum_rows = pair_in(pair_in(logsum_rows, "q", 0), "x", 0).reshape(-1)
    loss_scale = 1.0 / (comp_count * ctx_count * shard_count)
    row_scale = jnp.exp(stats[0] - logsum_rows)[:, None]
    mixed_rows = jnp.concatenate(mixed, 0) * row_scale - label_rows.astype(jnp.float32)
    grad_picked = group_sum(mixed_rows * loss_scale)
    table_grad, other_grad = head_table(
        terms, head_rows, column_ids, row_scale, head_labels, loss_scale
    )
    table_grad, other_grad, grad_picked = hold(table_grad, other_grad, grad_picked)
    table_grad = table_grad + swapped(other_grad, "c")
    vector_grads = {}
    reducer = Reducer()

    def norm_back(grad, saved, gain):
        grad, vector_grads[gain], vector_grads[gain + 1] = norm_backward(
            grad, saved, vector_row(gain)
        )
        return grad

    grad_sum3 = norm_back(grad_picked, dec_saved3, Row.dec_norm3_gain)
    grad_mid, dec_pre_grad, dec_first_bias_g, dec_ffn_grad, vector_grads[Row.dec_ffn_bias] = (
        feed_backward(grad_sum3, dec_slope, dec_first, dec_second)
    )
    grad_sum2 = norm_back(grad_sum3 + grad_mid, dec_saved2, Row.dec_norm2_gain)
    reducer.add(
        Group(
            (True, comp_left, both_cores(dec_pre_grad), ((Part.dec_first, 2, None),)),
            (False, dec_act, both_cores(dec_ffn_grad[None]), ((Part.dec_second, 0, 0),)),
            mixed=1,
        )
    )
    cross_query_grad, cross_grad_pairs, cross_branch_grad, vector_grads[Row.cross_out_bias] = (
        branch_backward(
            grad_sum2,
            cross_queries,
            cross_pairs_all,
            cross_marks,
            cross_logsum,
            columns(Part.cross_out),
            head_count,
        )
    )
    cross_query_grad, cross_grad_pairs = reducer.step(cross_query_grad, cross_grad_pairs)
    cross_pairs_grad = pairs_back(cross_grad_pairs)
    vector_grads[Row.cross_query_bias], grad_cross_in = query_backward(
        columns(Part.cross_wq), cross_query_grad
    )
    grad_sum1 = norm_back(grad_sum2 + grad_cross_in, dec_saved1, Row.dec_norm1_gain)
    vector_grads[Row.cross_value_bias], grad_encoded = pairs_backward(
        cross_pair_weights, cross_pairs_grad
    )
    comp_right = both_cores(jnp.stack([cross_query_grad, cross_branch_grad]))
    group = reducer.add(
        Group(
            (True, left, both_cores(cross_pairs_grad), ((Part.cross_wk, 3, 0), (Part.cross_wv, 3, 1))),
            (False, comp_left, comp_right, ((Part.cross_wq, 1, 0), (Part.cross_out, 4, 1))),
            mixed=4,
        )
    )
    grad_sum1 = group.before(grad_sum1)
    dec_query_grad, dec_grad_pairs, dec_branch_grad, vector_grads[Row.dec_out_bias] = (
        branch_backward(
            grad_sum1,
            dec_queries,
            dec_pairs_all,
            self_marks,
            self_logsum,
            columns(Part.dec_out),
            head_count,
        )
    )
    grad_encoded, dec_query_grad, dec_grad_pairs, table_grad = reducer.step(
        grad_encoded, dec_query_grad, dec_grad_pairs, table_grad
    )
    dec_pairs_grad = pairs_back(dec_grad_pairs)
    vector_grads[Row.dec_query_bias], grad_dec_q_in = query_backward(
        columns(Part.dec_wq), dec_query_grad
    )
    vector_grads[Row.dec_value_bias], grad_dec_kv_in = pairs_backward(
        columns(Part.dec_wk, 2 * width), dec_pairs_grad
    )
    comp_right = both_cores(jnp.stack([dec_query_grad, dec_branch_grad]))
    reducer.add(
        Group(
            (True, left, both_cores(dec_pairs_grad), ((Part.dec_wk, 1, 0), (Part.dec_wv, 1, 1))),
            (False, comp_left, comp_right, ((Part.dec_wq, 0, 0), (Part.dec_out, 3, 1))),
            mixed=4,
        )
    )
    grad_enc2 = norm_back(grad_encoded, enc_saved2, Row.enc_norm2_gain)
    grad_comp0 = lax.dot_general(
        comp_exact, grad_sum1 + grad_dec_q_in, LEFT_T, precision=PRECISE
    )
    grad_tgt_input = norm_back(grad_comp0 + grad_dec_kv_in, dec_saved0, Row.dec_norm0_gain)
    grad_enc2, grad_tgt_input = reducer.step(grad_enc2, grad_tgt_input)
    grad_enc_mid, enc_pre_grad, enc_first_bias_g, enc_ffn_grad, vector_grads[Row.enc_ffn_bias] = (
        feed_backward(grad_enc2, enc_slope, enc_first, enc_second)
    )
    grad_enc1 = norm_back(grad_enc2 + grad_enc_mid, enc_saved1, Row.enc_norm1_gain)
    grad_enc1, enc_pre_grad, enc_ffn_grad = reducer.step(grad_enc1, enc_pre_grad, enc_ffn_grad)
    reducer.add(
        Group(
            (True, left, both_cores(enc_pre_grad), ((Part.enc_first, 2, None),)),
            (False, enc_act, both_cores(enc_ffn_grad[None]), ((Part.enc_second, 0, 0),)),
            mixed=1,
        )
    )
    enc_query_grad, enc_grad_pairs, enc_branch_grad, vector_grads[Row.enc_out_bias] = (
        branch_backward(
            grad_enc1,
            enc_queries,
            enc_pairs_all,
            enc_marks,
            enc_logsum,
            columns(Part.enc_out),
            head_count,
        )
    )
    enc_query_grad, enc_grad_pairs = reducer.step(enc_query_grad, enc_grad_pairs)
    enc_pairs_grad = pairs_back(enc_grad_pairs)
    vector_grads[Row.enc_query_bias], grad_enc_q_in = query_backward(
        columns(Part.enc_wq), enc_query_grad
    )
    vector_grads[Row.enc_value_bias], grad_enc_kv_in = pairs_backward(
        columns(Part.enc_wk, 2 * width), enc_pairs_grad
    )
    grad_src_input = norm_back(
        grad_enc1 + grad_enc_q_in + grad_enc_kv_in, enc_saved0, Row.enc_norm0_gain
    )
    right = both_cores(
        jnp.concatenate([enc_pairs_grad, enc_query_grad[None], enc_branch_grad[None]], 0)
    )
    group = reducer.add(
        Group(
            (True, left, right, ((Part.enc_wk, 0, 0), (Part.enc_wv, 0, 1))),
            (False, left, right, ((Part.enc_wq, 0, 2), (Part.enc_out, 4, 3))),
            mixed=4,
        )
    )
    table_grad = lookup.give(
        table_grad,
        jnp.concatenate(
            [grad_src_input.astype(jnp.bfloat16), grad_tgt_input.astype(jnp.bfloat16)], 0
        ),
    )
    grad_src_input, grad_tgt_input = group.before(grad_src_input, grad_tgt_input)
    position_grad = lax.dot_general(
        src_onehot.astype(jnp.float32), grad_src_input, LEFT_T, precision=PRECISE
    ) + lax.dot_general(
        tgt_onehot.astype(jnp.float32), grad_tgt_input, LEFT_T, precision=PRECISE
    )
    reducer.add(Group(ready=[(Part.position, position_grad)]))
    vector_grad = pack_rows(
        [vector_grads[name] for name in range(base_row)] + [enc_first_bias_g, dec_first_bias_g],
        width,
    )
    while reducer.moving:
        reducer.advance()
    summed = reducer.done

    def own_columns(part):
        if cuts == 1:
            return own_first(part, 1)[0]
        part = part.reshape(part.shape[0], ctx_count, -1)
        return lax.dynamic_index_in_dim(part, ctx_index, 1, keepdims=False)

    wide_grad = own_columns(
        jnp.concatenate(
            [
                summed[name]
                for name in (
                    Part.enc_wq,
                    Part.enc_wk,
                    Part.enc_out,
                    Part.enc_first,
                    Part.dec_wq,
                    Part.dec_wk,
                    Part.dec_out,
                    Part.cross_wq,
                    Part.cross_wk,
                    Part.cross_out,
                    Part.dec_first,
                )
            ],
            1,
        )
    )
    deep = [summed[name] for name in (Part.enc_second, Part.dec_second, Part.position)]
    if cuts > 1:
        deep = [own_columns(part) for part in deep]
    down_grad, position_grad = jnp.stack(deep[:2]), deep[2]
    owned_squares = (
        jnp.sum(wide_grad * wide_grad)
        + jnp.sum(down_grad * down_grad)
        + jnp.sum(position_grad * position_grad)
        + jnp.sum(table_grad * table_grad)
    )
    scalars = jnp.pad(jnp.stack([owned_squares, loss_local])[None, :], ((0, 0), (0, width - 2)))
    sums = all_sum(jnp.concatenate([vector_grad, scalars], 0))
    vector_grad, square_total, loss_sum = sums[:-1], sums[-1, 0], sums[-1, 1]
    grad_norm = jnp.sqrt(square_total + jnp.sum(vector_grad * vector_grad))
    clip_factor = jnp.minimum(1.0, CLIP_LIMIT / (grad_norm + 1e-06))
    outs = [loss_sum, grad_norm]
    for weight, moment, square, grad, decay, rate in (
        (table_weight, table_moment, table_square, table_grad, WEIGHT_DECAY, LEARN_RATE),
        (position_weight, position_moment, position_square, position_grad, WEIGHT_DECAY, LEARN_RATE),
        (wide_weight, wide_moment, wide_square, wide_grad, WEIGHT_DECAY, LEARN_RATE),
        (down_weight, down_moment, down_square, down_grad, WEIGHT_DECAY, LEARN_RATE),
        (vector_weight, vector_moment, vector_square, vector_grad, 0.0, VECTOR_RATE),
    ):
        outs.extend(adam_step(weight, moment, square, grad * clip_factor, decay, rate))
    return tuple(outs)


def solution(mesh):
    ctx_count, shard_count = mesh.devices.shape
    fine = Mesh(mesh.devices.reshape(2, ctx_count // 2, shard_count // 4, 2, 2), ALL)
    ctx, shard = ("q", "p"), ("z", "x", "c")
    table, plane, deep, whole = P(ALL, None), P(shard, ctx), P(None, shard, ctx), P()
    states = (table,) * 3 + (plane,) * 6 + (deep,) * 3 + (whole,) * 3
    return jax.shard_map(
        local,
        mesh=fine,
        in_specs=states + (plane,) * 6,
        out_specs=(whole, whole) + states,
        check_vma=False,
    )
```

```python
import functools
import math

import jax
import jax.numpy as jnp
from jax import lax
from jax.experimental import pallas as pl
from jax.experimental.pallas import tpu as pltpu
from jax.sharding import Mesh
from jax.sharding import PartitionSpec as P

H = 12
V = 50265
STEP = 10


PRECISE = lax.Precision.HIGHEST
NORM_EPS = 1e-05
LEARN_RATE = 0.03
VECTOR_RATE = 0.3
BETA_ONE = 0.9
BETA_TWO = 0.999
ADAM_EPS = 1e-08
WEIGHT_DECAY = 0.01
CLIP_LIMIT = 0.05
MASKED_SCORE = -1e30

class Row:
    (
        enc_norm0_gain,
        enc_norm0_bias,
        enc_query_bias,
        enc_value_bias,
        enc_out_bias,
        enc_norm1_gain,
        enc_norm1_bias,
        enc_ffn_bias,
        enc_norm2_gain,
        enc_norm2_bias,
        dec_norm0_gain,
        dec_norm0_bias,
        dec_query_bias,
        dec_value_bias,
        dec_out_bias,
        dec_norm1_gain,
        dec_norm1_bias,
        cross_query_bias,
        cross_value_bias,
        cross_out_bias,
        dec_norm2_gain,
        dec_norm2_bias,
        dec_ffn_bias,
        dec_norm3_gain,
        dec_norm3_bias,
    ) = range(25)


class Part:
    (
        enc_wq,
        enc_wk,
        enc_wv,
        enc_out,
        enc_first,
        dec_wq,
        dec_wk,
        dec_wv,
        dec_out,
        cross_wq,
        cross_wk,
        cross_wv,
        cross_out,
        dec_first,
        enc_second,
        dec_second,
        position,
    ) = range(17)


FIRSTS = (Part.enc_first, Part.dec_first)


def product(left, right):
    return jnp.dot(left, right, preferred_element_type=jnp.float32)


def product_t(left, right):
    return lax.dot_general(
        left, right, (((1,), (1,)), ((), ())), preferred_element_type=jnp.float32
    )


def row_contract(left, right):
    return lax.dot_general(
        left, right, (((0,), (0,)), ((), ())), preferred_element_type=jnp.float32
    )


NORMAL = (((1,), (0,)), ((), ()))
RIGHT_T = (((1,), (1,)), ((), ()))
LEFT_T = (((0,), (0,)), ((), ()))
KERNEL_BYTES = 48 * 2**20


def dot(left, right, dims):
    return lax.dot_general(left, right, dims, preferred_element_type=jnp.float32)


def norm_forward(values, gain, bias):
    center = values - jnp.mean(values, -1, keepdims=True)
    scale = lax.rsqrt(jnp.mean(center * center, -1, keepdims=True) + NORM_EPS)
    unit = center * scale
    return unit * gain + bias, (unit, scale)


def norm_backward(grad, saved, gain):
    unit, scale = saved
    grad_unit = grad * gain
    shift = jnp.mean(grad_unit, -1, keepdims=True)
    slope = jnp.mean(grad_unit * unit, -1, keepdims=True)
    return (
        scale * (grad_unit - shift - unit * slope),
        jnp.sum(grad * unit, 0, keepdims=True),
        jnp.sum(grad, 0, keepdims=True),
    )


def column_sums(part, dims=NORMAL):
    count = part.shape[dims[0][1][0]]
    return dot(jnp.ones((8, count), jnp.bfloat16), part, dims)[:1]


def doc_positions(segment, limit):
    length = segment.shape[0]
    places = jnp.arange(length, dtype=jnp.int32)
    change = jnp.concatenate([jnp.ones((1,), bool), segment[1:] != segment[:-1]])
    starts = lax.cummax(jnp.where(change, places, 0), axis=0)
    return jnp.minimum(places - starts, limit - 1)


def combine_partial(first, second):
    top_value = jnp.maximum(first[0], second[0])
    sum_value = first[1] * jnp.exp(first[0] - top_value) + second[1] * jnp.exp(
        second[0] - top_value
    )
    return (top_value, sum_value, first[2] + second[2])


def project_queries(inputs_b, weight_q, bias_q):
    return ((product(inputs_b, weight_q) + bias_q) * 0.125).astype(jnp.bfloat16)


def project_pairs(inputs_b, weight_pair, bias_v):
    bias = jnp.concatenate([jnp.zeros_like(bias_v), bias_v])
    return (product(inputs_b, weight_pair) + bias).astype(jnp.bfloat16)


def query_backward(weight_q, grad_query):
    return (column_sums(grad_query), product_t(grad_query, weight_q))


def pairs_backward(weight_pair, pairs_grad):
    width = pairs_grad.shape[2]
    return (
        column_sums(pairs_grad[1]),
        product_t(pairs_grad[0], weight_pair[:, :width])
        + product_t(pairs_grad[1], weight_pair[:, width:]),
    )


def feed_forward(inputs_b, first_weight, first_bias, second_weight, second_bias):
    pre_act = dot(first_weight, inputs_b, (((0,), (1,)), ((), ()))) + first_bias[:, None]
    share = 0.5 + 0.5 * lax.erf(pre_act * 0.5**0.5)
    act_b = (pre_act * share).astype(jnp.bfloat16)
    slope = share + pre_act * jnp.exp(-0.5 * pre_act * pre_act) * (0.5 / math.pi) ** 0.5
    return (dot(act_b, second_weight, LEFT_T) + second_bias, slope, act_b)


def feed_backward(grad_branch, slope, first_weight, second_weight):
    branch_grad = grad_branch.astype(jnp.bfloat16)
    grad_pre = (dot(second_weight, branch_grad, RIGHT_T) * slope).astype(jnp.bfloat16)
    return (
        dot(grad_pre, first_weight, (((0,), (1,)), ((), ()))),
        grad_pre,
        column_sums(grad_pre, RIGHT_T),
        branch_grad,
        column_sums(branch_grad),
    )


def adam_step(weight, moment, square, grad, decay, rate):
    new_moment = BETA_ONE * moment + (1.0 - BETA_ONE) * grad
    new_square = BETA_TWO * square + (1.0 - BETA_TWO) * grad * grad
    direction = (
        new_moment
        / (1.0 - BETA_ONE**STEP)
        / (jnp.sqrt(new_square / (1.0 - BETA_TWO**STEP)) + ADAM_EPS)
    )
    return (new_moment, new_square, weight - rate * (direction + decay * weight))


def fill_mask(query_ref, key_ref, mask_ref):

    @pl.when(pl.program_id(0) == 0)
    def _():
        allowed = (key_ref[:, 0:1] == query_ref[0:1, :]) & (key_ref[:, 1:2] <= query_ref[1:2, :])
        mask_ref[...] = jnp.where(allowed, 1.0, 0.0)


def attention_kernel(
    query_ref,
    key_ref,
    q_ref,
    k_own_ref,
    k_came_ref,
    v_own_ref,
    v_came_ref,
    out_ref,
    turned_ref,
    logsum_ref,
    mask_ref,
    *,
    head_size,
):
    fill_mask(query_ref, key_ref, mask_ref)
    half = k_own_ref.shape[0]
    outs = []
    for head in range(q_ref.shape[1] // head_size):
        lanes = slice(head * head_size, (head + 1) * head_size)
        q = q_ref[:, lanes]
        keys = jnp.concatenate([k_own_ref[:, lanes], k_came_ref[:, lanes]], 0)
        scores = jnp.where(mask_ref[...] != 0.0, dot(keys, q, RIGHT_T), MASKED_SCORE)
        top = jnp.max(scores, 0, keepdims=True)
        terms = jnp.exp(scores - top)
        total = jnp.sum(terms, 0, keepdims=True)
        probs = (terms * (1.0 / total)).astype(jnp.bfloat16)
        outs.append(
            dot(v_own_ref[:, lanes], probs[:half], LEFT_T)
            + dot(v_came_ref[:, lanes], probs[half:], LEFT_T)
        )
        logsum_ref[0, head : head + 1, :] = top + jnp.log(total)
    out = jnp.concatenate(outs, 0)
    turned_ref[...] = out.astype(jnp.bfloat16)
    out_ref[...] = out.T.astype(jnp.bfloat16)


def attention_back_kernel(
    query_ref,
    key_ref,
    q_ref,
    k_own_ref,
    k_came_ref,
    v_own_ref,
    v_came_ref,
    grad_ref,
    logsum_ref,
    grad_q_ref,
    own_ref,
    other_ref,
    mask_ref,
    *,
    head_size,
):
    fill_mask(query_ref, key_ref, mask_ref)
    half = k_own_ref.shape[0]
    q_parts, k_parts, v_parts = [], [], []
    for head in range(q_ref.shape[1] // head_size):
        lanes = slice(head * head_size, (head + 1) * head_size)
        q, grad = q_ref[:, lanes], grad_ref[:, lanes]
        keys = jnp.concatenate([k_own_ref[:, lanes], k_came_ref[:, lanes]], 0)
        values = jnp.concatenate([v_own_ref[:, lanes], v_came_ref[:, lanes]], 0)
        scores = jnp.where(mask_ref[...] != 0.0, dot(keys, q, RIGHT_T), MASKED_SCORE)
        probs = jnp.exp(scores - logsum_ref[0, head : head + 1, :])
        grad_probs = dot(values, grad, RIGHT_T)
        shift = jnp.sum(grad_probs * probs, 0, keepdims=True)
        grad_scores = (probs * (grad_probs - shift)).astype(jnp.bfloat16)
        v_parts.append(dot(probs.astype(jnp.bfloat16), grad, NORMAL))
        k_parts.append(dot(grad_scores, q, NORMAL))
        q_parts.append(dot(keys, grad_scores, LEFT_T))
    grad_q_ref[...] = jnp.concatenate(q_parts, 0).T.astype(jnp.bfloat16) * jnp.bfloat16(0.125)
    for at, parts in enumerate((k_parts, v_parts)):
        grad_pair = jnp.concatenate(parts, 1)
        own_ref[at] = grad_pair[:half]
        other_ref[at] = grad_pair[half:]


def attention_call(kernel, results, marks, head_count, products, queries, pairs, extra=()):
    query_rows, width = queries.shape
    own, came = pairs
    key_rows = own.shape[0]
    head_size = width // head_count
    per_step = max(1, 128 // head_size)
    steps = head_count // per_step
    lanes = per_step * head_size
    heads = pl.BlockSpec((query_rows, lanes), lambda i: (0, i))
    keys = pl.BlockSpec((key_rows, lanes), lambda i: (0, i))
    values = pl.BlockSpec((key_rows, lanes), lambda i: (0, i + steps))
    sums = pl.BlockSpec((1, per_step, query_rows), lambda i: (i, 0, 0))
    kinds = {
        "q": (heads, (query_rows, width), jnp.bfloat16),
        "t": (pl.BlockSpec((lanes, query_rows), lambda i: (i, 0)), (width, query_rows), jnp.bfloat16),
        "s": (sums, (steps, per_step, query_rows), jnp.float32),
        "p": (
            pl.BlockSpec((2, key_rows, lanes), lambda i: (0, 0, i)),
            (2, key_rows, width),
            jnp.float32,
        ),
    }
    count = 2 * query_rows * key_rows
    return pl.pallas_call(
        functools.partial(kernel, head_size=head_size),
        grid=(steps,),
        in_specs=[pl.BlockSpec(part.shape, lambda i: (0, 0)) for part in marks]
        + [heads, keys, keys, values, values]
        + [heads, sums][: len(extra)],
        out_specs=[kinds[kind][0] for kind in results],
        out_shape=[jax.ShapeDtypeStruct(*kinds[kind][1:]) for kind in results],
        scratch_shapes=[pltpu.VMEM((2 * key_rows, query_rows), jnp.float32)],
        compiler_params=pltpu.CompilerParams(vmem_limit_bytes=KERNEL_BYTES),
        cost_estimate=pl.CostEstimate(
            flops=2 * products * count * width,
            bytes_accessed=2 * width * (query_rows + 2 * key_rows) * products,
            transcendentals=count * head_count,
        ),
    )(*marks, queries, own, came, own, came, *extra)


def branch_forward(queries, pairs, marks, weight_o, bias_o, head_count):
    mixed_b, mixed_t, logsum = attention_call(
        attention_kernel, "qts", marks, head_count, 2, queries, pairs
    )
    return (product(mixed_b, weight_o) + bias_o, mixed_t, logsum)


def branch_backward(grad_branch, queries, pairs, marks, logsum, weight_o, head_count):
    branch_grad = grad_branch.astype(jnp.bfloat16)
    grad_mixed = product_t(branch_grad, weight_o).astype(jnp.bfloat16)
    query_grad, own, other = attention_call(
        attention_back_kernel, "qpp", marks, head_count, 5, queries, pairs, (grad_mixed, logsum)
    )
    return (query_grad, (own, other), branch_grad, column_sums(branch_grad))


ALL = ("q", "p", "z", "x", "c")
SWAP = [(0, 1), (1, 0)]
SLOTS = 40


def swapped(part, axis):
    return lax.ppermute(part, axis, SWAP)


def one_hot(places, count):
    return (places[:, None] == jnp.arange(count, dtype=places.dtype)[None, :]).astype(jnp.bfloat16)


def shifted(part, axis, step):
    count = lax.axis_size(axis)
    return lax.ppermute(part, axis, [(i, (i + step) % count) for i in range(count)])


def line_in(part, axis):
    count = lax.axis_size(axis)
    return jnp.stack([part] + [shifted(part, axis, count - k) for k in range(1, count)])


def pair_in(part, axis, at):
    return jnp.stack([part, swapped(part, axis)], at)


def group_in(part, first):
    part = line_in(line_in(part, "p"), "z")
    if first == "q":
        part = pair_in(pair_in(part, "q", 0), "x", 0)
    else:
        part = pair_in(pair_in(part, "x", 0), "q", 1)
    return part


def group_rows(rows):
    half = rows.shape[1] // 2
    both = [group_in(rows[:, :half], "q"), group_in(rows[:, half:], "x")]
    return jnp.concatenate(both, -1).reshape(-1, rows.shape[1])


def send_half(part, axis, at):
    own = lax.index_in_dim(part, 0, at, keepdims=False)
    other = lax.index_in_dim(part, 1, at, keepdims=False)
    return own + swapped(other.astype(jnp.bfloat16), axis).astype(jnp.float32)


def send_line(part, axis):
    total = part[0]
    for k in range(1, lax.axis_size(axis)):
        total = total + shifted(part[k].astype(jnp.bfloat16), axis, k).astype(jnp.float32)
    return total


def group_sum(rows):
    ways = (2, 2, lax.axis_size("z"), lax.axis_size("p"))
    rows = rows.reshape(ways + (-1, rows.shape[-1]))
    half = rows.shape[-1] // 2
    first, second = rows[..., :half], rows[..., half:]
    first = send_half(send_half(first, "x", 0), "q", 0)
    second = send_half(send_half(second, "q", 1), "x", 0)
    return jnp.concatenate([send_line(send_line(part, "z"), "p") for part in (first, second)], -1)


def from_others(parts, axes):
    return [
        lax.ppermute(part, axes, [(i, i ^ (k + 1)) for i in range(4)])
        for k, part in enumerate(parts)
    ]


def merge_stats(stats):

    def merge(first, second):
        return jnp.stack(combine_partial(first, second))

    ways = (2, 2, lax.axis_size("z"), lax.axis_size("p"))
    stats = stats.reshape((3,) + ways + (-1,))
    came = from_others([stats[:, 1, 0], stats[:, 0, 1], stats[:, 1, 1]], ("q", "x"))
    stats = merge(merge(stats[:, 0, 0], came[0]), merge(came[1], came[2]))
    for axis in ("z", "p"):
        total = stats[:, 0]
        came = [shifted(stats[:, k], axis, k) for k in range(1, lax.axis_size(axis))]
        for part in came:
            total = merge(total, part)
        stats = total
    return stats


def unpack_kernel(pack_ref, out_ref, *, columns):
    sides, owners, rows, total = pack_ref.shape
    for side in range(sides):
        for owner in range(owners):
            for at in range(total // columns):
                row = (owner * (total // columns) + at) * rows
                out_ref[row : row + rows, side * columns : (side + 1) * columns] = pack_ref[
                    side, owner, :, at * columns : (at + 1) * columns
                ]


def unpack_rows(pack, columns):
    sides, owners, rows, total = pack.shape
    each = rows * total // columns
    step = math.gcd(owners, 4)
    if rows % 16:
        pack = pack.reshape(sides, owners, rows, -1, columns)
        return jnp.transpose(pack, (1, 3, 2, 0, 4)).reshape(owners * each, sides * columns)
    return pl.pallas_call(
        functools.partial(unpack_kernel, columns=columns),
        grid=(owners // step,),
        in_specs=[pl.BlockSpec((sides, step, rows, total), lambda i: (0, i, 0, 0))],
        out_specs=pl.BlockSpec((step * each, sides * columns), lambda i: (i, 0)),
        out_shape=jax.ShapeDtypeStruct((owners * each, sides * columns), pack.dtype),
        cost_estimate=pl.CostEstimate(flops=0, bytes_accessed=4 * pack.size, transcendentals=0),
    )(pack)


def places_kernel(pack_ref, out_ref):
    sides, owners, _, _ = pack_ref.shape
    rows, columns = out_ref.shape[0] // owners, out_ref.shape[1] // sides
    across = columns // 128
    for side in range(sides):
        for owner in range(owners):
            for tile in range(rows // 16 * across):
                row, lane = tile // 4 * 16, tile % 4 * 128
                to_row = owner * rows + tile // across * 16
                to_lane = side * columns + tile % across * 128
                out_ref[to_row : to_row + 16, to_lane : to_lane + 128] = pack_ref[
                    side, owner, row : row + 16, lane : lane + 128
                ]


def unpack_places(pack, at, rows, columns):
    sides, owners, height, _ = pack.shape
    step = math.gcd(owners, 8)
    return pl.pallas_call(
        places_kernel,
        grid=(owners // step,),
        in_specs=[pl.BlockSpec((sides, step, height, 512), lambda i: (0, i, 0, at // 512))],
        out_specs=pl.BlockSpec((step * rows, sides * columns), lambda i: (i, 0)),
        out_shape=jax.ShapeDtypeStruct((owners * rows, sides * columns), pack.dtype),
        cost_estimate=pl.CostEstimate(
            flops=0, bytes_accessed=4 * owners * rows * sides * columns, transcendentals=0
        ),
    )(pack)


def hold(*trees):
    return lax.optimization_barrier(trees)


def all_sum(part):
    part = part + swapped(part, "c")
    for axes in (("q", "x"), ("z",)):
        if axes == ("q", "x") or lax.axis_size("z") == 4:
            first, second, third = from_others([part] * 3, axes)
            part = (part + first) + (second + third)
        else:
            part = lax.psum(part, axes)
    return lax.psum(part, "p") if lax.axis_size("p") > 1 else part


def pick(part, axis, index):
    return lax.dynamic_index_in_dim(part, index, axis, keepdims=False)


def own_first(part, axis):
    half = part.shape[axis] // 2
    first = lax.slice_in_dim(part, 0, half, axis=axis)
    second = lax.slice_in_dim(part, half, 2 * half, axis=axis)
    here = lax.axis_index("q") == 0
    return jnp.where(here, first, second), jnp.where(here, second, first)


def line_kernel(place_ref, *refs, unit):
    count = (len(refs) - 2) // 2
    kept_ref, sent_ref = refs[-2:]
    blocks = []
    for own, other in zip(refs[:count], refs[count : 2 * count]):
        total = own[0] + other[0].astype(jnp.float32)
        blocks += [total[at : at + unit] for at in range(0, total.shape[0], unit)]

    @pl.when(pl.program_id(0) == 0)
    def _():
        at = 0
        for block in blocks:
            kept_ref[:, at : at + block.shape[1]] = block
            at += block.shape[1]

    @pl.when(pl.program_id(0) > 0)
    def _():
        at = 0
        for block in blocks:
            sent_ref[0, :, at : at + block.shape[1]] = block.astype(jnp.bfloat16)
            at += block.shape[1]


def line_parts(owns, others, unit):
    lines = owns[0].shape[0]
    columns = sum(own.shape[1] // unit * own.shape[2] for own in owns)
    specs = [
        pl.BlockSpec((1,) + own.shape[1:], lambda k, place: ((place[0] + k) % lines, 0, 0))
        for own in owns
    ]
    return pl.pallas_call(
        functools.partial(line_kernel, unit=unit),
        grid_spec=pltpu.PrefetchScalarGridSpec(
            num_scalar_prefetch=1,
            grid=(lines,),
            in_specs=specs * 2,
            out_specs=[
                pl.BlockSpec((unit, columns), lambda k, place: (0, 0)),
                pl.BlockSpec((1, unit, columns), lambda k, place: (jnp.maximum(k - 1, 0), 0, 0)),
            ],
        ),
        out_shape=[
            jax.ShapeDtypeStruct((unit, columns), jnp.float32),
            jax.ShapeDtypeStruct((lines - 1, unit, columns), jnp.bfloat16),
        ],
        compiler_params=pltpu.CompilerParams(vmem_limit_bytes=KERNEL_BYTES),
        cost_estimate=pl.CostEstimate(
            flops=lines * unit * columns, bytes_accessed=8 * lines * unit * columns, transcendentals=0
        ),
    )(lax.axis_index("z").astype(jnp.int32).reshape(1), *owns, *others)


def factor_kernel(place_ref, *refs, turned, halves):
    (near, near_came, far, far_came), rights = refs[:4], refs[4:-2]
    kept_ref, sent_ref = refs[-2:]
    dims = RIGHT_T if turned else NORMAL

    def rows(ref):
        block = ref[...]
        return block.reshape(-1, block.shape[-1])

    def side(own, came, at):
        right, right_came = (ref[...].reshape(ref.shape[-2:]) for ref in rights[2 * at : 2 * at + 2])
        return dot(rows(own), right, dims) + dot(rows(came), right_came, dims)

    if halves:
        kept_ref[0], kept_ref[1] = side(near, near_came, 0), side(far, far_came, 0)
        sent_ref[0] = side(near, near_came, 1).astype(jnp.bfloat16)
        sent_ref[1] = side(far, far_came, 1).astype(jnp.bfloat16)
    else:
        kept_ref[...] = side(near, near_came, 0)
        sent_ref[...] = side(far, far_came, 0).astype(jnp.bfloat16)


def factor_parts(left, right, names, halves):
    own, came = left
    right, right_came = right
    _, lines, _, rows, tokens = own.shape
    turned = right.ndim == 2
    width = right.shape[0] if turned else right.shape[2]
    step = width // 2 if halves or width < 3072 else 384
    blocks = width // step
    place = [lax.axis_index("x"), lax.axis_index("q")]
    place += [left_at for _, left_at, _ in names] + [right_at or 0 for _, _, right_at in names]
    place = jnp.stack([jnp.asarray(part, jnp.int32) for part in place])
    count, groups = lines * rows, len(names)
    inner = 1 if halves else blocks

    def left_spec(far):

        def at_place(j, at):
            return at[2 + j // inner], 0, 1 - at[0] if far else at[0], 0, 0

        return pl.BlockSpec((1, lines, 1, rows, tokens), at_place)

    def right_spec(other):

        def at_place(j, at):
            if turned:
                return j, 0
            part = (1 - at[1] if other else at[1]) if halves else j % inner
            return at[2 + groups + j // inner], 0, part

        return pl.BlockSpec((step, tokens) if turned else (1, tokens, step), at_place)

    steps = groups * inner
    shape = (2, count, steps * step) if halves else (count, steps * step)
    out_spec = (
        pl.BlockSpec((2, count, step), lambda j, at: (0, 0, j))
        if halves
        else pl.BlockSpec((count, step), lambda j, at: (0, j))
    )
    rights = [right, right_came] * (2 if halves else 1)
    return pl.pallas_call(
        functools.partial(factor_kernel, turned=turned, halves=halves),
        grid_spec=pltpu.PrefetchScalarGridSpec(
            num_scalar_prefetch=1,
            grid=(steps,),
            in_specs=[left_spec(False), left_spec(False), left_spec(True), left_spec(True)]
            + [right_spec(at >= 2) for at in range(len(rights))],
            out_specs=[out_spec, out_spec],
        ),
        out_shape=[
            jax.ShapeDtypeStruct(shape, jnp.float32),
            jax.ShapeDtypeStruct(shape, jnp.bfloat16),
        ],
        compiler_params=pltpu.CompilerParams(vmem_limit_bytes=KERNEL_BYTES),
        cost_estimate=pl.CostEstimate(
            flops=8 * count * tokens * width * groups,
            bytes_accessed=8 * count * tokens + (4 * tokens + 12 * count) * width * groups,
            transcendentals=0,
        ),
    )(place, own, came, own, came, *rights)


class Group:
    def __init__(self, *factors, ready=(), mixed=0):
        core, side = lax.axis_index("c"), lax.axis_index("x")
        self.names, self.kept, self.flight, self.ways, self.rows = [], [], [], [], []
        self.mixed = mixed
        self.stage = 0
        for way, left, right, names in factors:
            kept, sent = factor_parts(left, right, names, not way)
            self.take([name for name, _, _ in names], kept, sent, way)
        for name, grad in ready:
            grad = grad.reshape(lax.axis_size("z"), 2, 2, -1, grad.shape[1])
            grad = pick(grad, 2, core) + swapped(pick(grad, 2, 1 - core), "c")
            self.take([name], pick(grad, 1, side), pick(grad, 1, 1 - side), True)
        self.unit = min(self.rows)

    def before(self, *live):
        self.kept, live = hold(self.kept, live)
        return live if len(live) > 1 else live[0]

    def take(self, names, kept, sent, way):
        self.names.append(names[:1] if way else names)
        kept, sent = (part.reshape(-1, part.shape[-1]) for part in (kept, sent))
        self.kept.append(kept)
        self.ways.append(way)
        self.rows.append(kept.shape[0] // lax.axis_size("z") // (1 if way else 2))
        self.flight.append(swapped(sent.astype(jnp.bfloat16), "x" if way else "q"))

    def advance(self):
        self.stage += 1
        lines = lax.axis_size("z")
        if self.stage == 1:
            for at, way in enumerate(self.ways):
                kept, came = self.kept[at], self.flight[at]
                total = kept + came.astype(jnp.float32)
                half = total.shape[0] // 2
                near, far = own_first(total, 1) if way else (total[:half], total[half:])
                self.kept[at] = near.reshape(lines, -1, near.shape[1])
                far = far.astype(jnp.bfloat16).reshape(lines, -1, far.shape[1])
                self.flight[at] = swapped(far, "q" if way else "x")
        elif self.stage == 2:
            self.shapes = [part.shape[1:] for part in self.kept]
            self.total, sent = line_parts(self.kept, self.flight, self.unit)
            self.flight = [shifted(sent[k], "z", k + 1) for k in range(sent.shape[0])]
        elif self.stage == 3:
            for part in self.flight:
                self.total = self.total + part.astype(jnp.float32)
            if lax.axis_size("p") > 1:
                self.total = lax.psum(self.total, "p")
                self.mixed = sum(len(names) for names in self.names)
            self.spans = []
            for names, (rows, columns) in zip(self.names, self.shapes):
                for name in names:
                    self.spans.append((name, rows // self.unit, columns // len(names)))
            width = sum(blocks * columns for _, blocks, columns in self.spans[: self.mixed])
            self.flight = swapped(self.total[:, :width], "q") if self.mixed else ()
        else:
            at, self.done = 0, {}
            for turn, (name, blocks, columns) in enumerate(self.spans):
                parts = []
                for _ in range(blocks):
                    near = self.total[:, at : at + columns]
                    if turn < self.mixed:
                        far = self.flight[:, at : at + columns]
                        near = jnp.where(
                            lax.axis_index("q") == 0,
                            jnp.concatenate([near, far], 1),
                            jnp.concatenate([far, near], 1),
                        )
                    parts.append(near)
                    at += columns
                self.done[name] = parts[0] if len(parts) == 1 else jnp.concatenate(parts, 0)


class Reducer:

    def __init__(self):
        self.moving = []
        self.done = {}

    def add(self, item):
        self.moving.append(item)
        return item

    def step(self, *live, only=()):
        items = [item for item in self.moving if not only or item in only]
        live, flights = hold(live, [item.flight for item in items])
        for item, flight in zip(items, flights):
            item.flight = flight
        self.advance(items)
        return live if len(live) > 1 else live[0]

    def advance(self, items=None):
        for item in list(self.moving) if items is None else items:
            item.advance()
            if item.stage == 4:
                self.done.update(item.done)
        self.moving = [item for item in self.moving if item.stage < 4]


def pairs_in(pairs):
    both = (pairs, swapped(pairs, "c"))
    if lax.axis_size("p") > 1:
        both = tuple(lax.all_gather(part, "p", axis=0, tiled=True) for part in both)
    return both


def pairs_back(grads):
    if lax.axis_size("p") > 1:
        grads = tuple(
            lax.psum_scatter(part, "p", scatter_dimension=1, tiled=True) for part in grads
        )
    own, other = grads
    return (own + swapped(other, "c")).astype(jnp.bfloat16)


def both_cores(part):
    return part, swapped(part, "c")


def turn_kernel(core_ref, *refs, rows):
    parts, (own_ref, other_ref) = refs[:-2], refs[-2:]
    lines = own_ref.shape[1]
    for at, ref in enumerate(parts):
        part = ref[...]
        if part.shape[0] != lines * 4 * rows:
            part = part.astype(jnp.float32).T.astype(jnp.bfloat16)
        blocks = [part[k * rows : (k + 1) * rows] for k in range(4 * lines)]
        for here in range(2):

            @pl.when(core_ref[0] == here)
            def _():
                for line in range(lines):
                    for side in range(2):
                        first = (line * 2 + side) * 2
                        own_ref[at, line, side] = blocks[first + here]
                        other_ref[at, line, side] = blocks[first + 1 - here]


def turn_rows(parts, turned, rows):
    tokens, width = parts[0].shape
    lines = width // (4 * rows)
    count = len(parts) + len(turned)
    shape = (count, lines, 2, rows, tokens)
    if rows % 16 or tokens == width:
        whole = jnp.stack([part.T for part in parts] + list(turned))
        whole = whole.reshape(count, lines, 2, 2, rows, tokens)
        core = lax.axis_index("c")
        return pick(whole, 3, core), pick(whole, 3, 1 - core)
    vmem = pl.BlockSpec(memory_space=pltpu.VMEM)
    return pl.pallas_call(
        functools.partial(turn_kernel, rows=rows),
        in_specs=[pl.BlockSpec(memory_space=pltpu.SMEM)] + [vmem] * count,
        out_specs=[vmem, vmem],
        out_shape=[jax.ShapeDtypeStruct(shape, jnp.bfloat16)] * 2,
        compiler_params=pltpu.CompilerParams(vmem_limit_bytes=KERNEL_BYTES),
        cost_estimate=pl.CostEstimate(
            flops=0, bytes_accessed=4 * count * tokens * width, transcendentals=0
        ),
    )(lax.axis_index("c").astype(jnp.int32).reshape(1), *parts, *turned)


def pack_kernel(*refs, width):
    out_ref = refs[-1]
    at = 0
    for ref in refs[:-1]:
        for column in range(0, ref.shape[1], width):
            out_ref[at : at + 1, :] = ref[0:1, column : column + width]
            at += 1


def pack_rows(parts, width):
    count = sum(part.shape[1] // width for part in parts)
    vmem = pl.BlockSpec(memory_space=pltpu.VMEM)
    return pl.pallas_call(
        functools.partial(pack_kernel, width=width),
        in_specs=[vmem] * len(parts),
        out_specs=vmem,
        out_shape=jax.ShapeDtypeStruct((count, width), jnp.float32),
    )(*parts)


def head_kernel(
    table_ref, rows_ref, ids_ref, labels_ref, terms_ref, mixed_ref, label_rows_ref, stats_ref
):
    scores = dot(rows_ref[...], table_ref[...], RIGHT_T)
    ids = ids_ref[0:1, :]
    scores = jnp.where(ids < V, scores, MASKED_SCORE)
    top = jnp.max(scores, 1, keepdims=True)
    terms = jnp.exp(scores - top)
    total = jnp.sum(terms, 1, keepdims=True)
    terms = terms.astype(jnp.bfloat16)
    terms_ref[...] = terms
    mixed_ref[...] = dot(terms, table_ref[...], NORMAL)
    hit = ids == labels_ref[:, 0:1]
    label = jnp.sum(jnp.where(hit, scores, 0.0), 1, keepdims=True)
    chosen = jnp.where(hit, 1.0, 0.0).astype(jnp.bfloat16)
    label_rows_ref[...] = dot(chosen, table_ref[...], NORMAL).astype(jnp.bfloat16)
    lane = lax.broadcasted_iota(jnp.int32, (scores.shape[0], 128), 1)
    stats = jnp.where(lane == 0, top, jnp.where(lane == 1, total, label))
    stats_ref[...] = stats.T[:8]


def head_forward(table, rows, ids, labels):
    columns, width = table.shape
    count = rows.shape[0]
    step = math.gcd(count, 256)
    return pl.pallas_call(
        head_kernel,
        grid=(count // step,),
        in_specs=[
            pl.BlockSpec((columns, width), lambda i: (0, 0)),
            pl.BlockSpec((step, width), lambda i: (i, 0)),
            pl.BlockSpec((1, columns), lambda i: (0, 0)),
            pl.BlockSpec((step, 1), lambda i: (i, 0)),
        ],
        out_specs=[
            pl.BlockSpec((step, columns), lambda i: (i, 0)),
            pl.BlockSpec((step, width), lambda i: (i, 0)),
            pl.BlockSpec((step, width), lambda i: (i, 0)),
            pl.BlockSpec((8, step), lambda i: (0, i)),
        ],
        out_shape=[
            jax.ShapeDtypeStruct((count, columns), jnp.bfloat16),
            jax.ShapeDtypeStruct((count, width), jnp.float32),
            jax.ShapeDtypeStruct((count, width), jnp.bfloat16),
            jax.ShapeDtypeStruct((8, count), jnp.float32),
        ],
        compiler_params=pltpu.CompilerParams(vmem_limit_bytes=KERNEL_BYTES),
        cost_estimate=pl.CostEstimate(
            flops=6 * columns * width * count,
            bytes_accessed=2 * (columns * width + 4 * count * width + columns * count),
            transcendentals=columns * count,
        ),
    )(table, rows, ids[None, :], labels[:, None])


def table_kernel(terms_ref, rows_ref, ids_ref, marks_ref, labels_ref, own_ref, other_ref, total_ref, *, scale):
    probs = terms_ref[...].astype(jnp.float32) * marks_ref[:, 0:1]
    hit = ids_ref[0:1, :] == labels_ref[:, 0:1]
    grad = ((probs - jnp.where(hit, 1.0, 0.0)) * scale).astype(jnp.bfloat16)
    part = dot(grad, rows_ref[...], LEFT_T)

    @pl.when(pl.program_id(0) == 0)
    def _():
        total_ref[...] = part

    @pl.when(pl.program_id(0) > 0)
    def _():
        total_ref[...] += part

    @pl.when(pl.program_id(0) == pl.num_programs(0) - 1)
    def _():
        own_ref[...] = total_ref[: own_ref.shape[0]]
        other_ref[...] = total_ref[own_ref.shape[0] :]


def head_table(terms, rows, ids, row_scale, labels, scale):
    count, columns = terms.shape
    width = rows.shape[1]
    step = math.gcd(count, 256)
    half = pl.BlockSpec((columns // 2, width), lambda i: (0, 0))
    return pl.pallas_call(
        functools.partial(table_kernel, scale=scale),
        grid=(count // step,),
        in_specs=[
            pl.BlockSpec((step, columns), lambda i: (i, 0)),
            pl.BlockSpec((step, width), lambda i: (i, 0)),
            pl.BlockSpec((1, columns), lambda i: (0, 0)),
            pl.BlockSpec((step, 1), lambda i: (i, 0)),
            pl.BlockSpec((step, 1), lambda i: (i, 0)),
        ],
        out_specs=[half, half],
        out_shape=[jax.ShapeDtypeStruct((columns // 2, width), jnp.float32)] * 2,
        scratch_shapes=[pltpu.VMEM((columns, width), jnp.float32)],
        compiler_params=pltpu.CompilerParams(vmem_limit_bytes=KERNEL_BYTES),
        cost_estimate=pl.CostEstimate(
            flops=2 * columns * width * count,
            bytes_accessed=4 * columns * width + 2 * count * (width + columns),
            transcendentals=0,
        ),
    )(terms, rows, ids[None, :], row_scale, labels[:, None])


class Lookup:
    def __init__(self, token_ids, own_rows):
        owners = 1
        for axis in ALL:
            owners *= lax.axis_size(axis)
        self.owners = owners
        self.own_rows = own_rows
        count = token_ids.shape[0]
        places = jnp.arange(count, dtype=jnp.int32)
        owner = token_ids // own_rows
        same = token_ids[:, None] == token_ids[None, :]
        first = jnp.min(jnp.where(same, places[None, :], count), 1)
        is_first = first == places
        ahead = (owner[:, None] == owner[None, :]) & is_first[None, :] & (places[None, :] < first[:, None])
        self.rank = jnp.sum(ahead.astype(jnp.int32), 1)
        self.owner = owner
        self.is_first = is_first
        self.local_id = token_ids - owner * own_rows
    def round_places(self, turn):
        rank = self.rank - turn * SLOTS
        inside = (rank >= 0) & (rank < SLOTS)
        slot = jnp.where(inside, self.owner * SLOTS + rank, -1)
        to_owner = jnp.where(
            (self.owner[:, None] == jnp.arange(self.owners)[None, :]) & self.is_first[:, None],
            (self.local_id + 1).astype(jnp.float32)[:, None],
            0.0,
        )
        to_slot = (rank[:, None] == jnp.arange(SLOTS)[None, :]).astype(jnp.float32)
        asked = lax.dot_general(to_owner, to_slot, (((0,), (0,)), ((), ())), precision=PRECISE)
        asked = jnp.round(asked).astype(jnp.int32) - 1
        last = jnp.broadcast_to(jnp.max(self.rank), (self.owners, 1))
        wanted = lax.all_to_all(jnp.concatenate([asked, last], 1), ALL, 0, 0, tiled=True)
        self.rounds = jnp.max(wanted[:, SLOTS:]) // SLOTS + 1
        wanted = wanted[:, :SLOTS].reshape(-1)
        return one_hot(slot, self.owners * SLOTS), one_hot(wanted, self.own_rows)

    def fetch_round(self, turn, table_low):
        to_slot, to_row = self.round_places(turn)
        sent = product(to_row, table_low).astype(jnp.bfloat16)
        rows = lax.all_to_all(sent, ALL, 0, 0, tiled=True)
        return product(to_slot, rows), (to_slot, to_row)

    def fetch(self, table_low):
        rows, self.kept = self.fetch_round(0, table_low)
        rounds = self.rounds
        rows = lax.cond(
            rounds > 1,
            lambda: lax.fori_loop(
                1, rounds, lambda turn, total: total + self.fetch_round(turn, table_low)[0], rows
            ),
            lambda: rows,
        )
        self.rounds = rounds
        return rows

    def give_round(self, places, grads_b):
        to_slot, to_row = places
        sent = row_contract(to_slot, grads_b).astype(jnp.bfloat16)
        back = lax.all_to_all(sent, ALL, 0, 0, tiled=True)
        return row_contract(to_row, back)

    def give(self, total, grads_b):
        total = total + self.give_round(self.kept, grads_b)
        rounds = self.rounds
        return lax.cond(
            rounds > 1,
            lambda: lax.fori_loop(
                1,
                rounds,
                lambda turn, sums: sums + self.give_round(self.round_places(turn), grads_b),
                total,
            ),
            lambda: total,
        )


def local(
    table_weight,
    table_moment,
    table_square,
    position_weight,
    position_moment,
    position_square,
    wide_weight,
    wide_moment,
    wide_square,
    down_weight,
    down_moment,
    down_square,
    vector_weight,
    vector_moment,
    vector_square,
    source_ids,
    target_ids,
    target_labels,
    source_segments,
    target_segments,
    completion_idx,
):
    cuts = lax.axis_size("p")
    ctx_count = 2 * cuts
    shard_count = lax.axis_size("z") * 4
    core = lax.axis_index("c")
    block = lax.axis_index("p") * 2 + core
    ctx_index = lax.axis_index("q") * cuts + lax.axis_index("p")
    tokens = source_ids.shape[1]
    comp_count = completion_idx.shape[1]
    width = vector_weight.shape[1]
    hidden = down_weight.shape[1] * shard_count
    head_count = H
    own_rows = table_weight.shape[0]
    table_low = table_weight.astype(jnp.bfloat16)

    small = jnp.concatenate(
        [source_ids, target_ids, target_labels, source_segments, target_segments, completion_idx], 1
    )
    small = lax.all_gather(small[0], ("q", "p", "c"))
    small = small.reshape(ctx_count, 2, -1)
    small = lax.dynamic_index_in_dim(small, lax.axis_index("q"), 1, keepdims=False)
    src_ids, tgt_ids, tgt_labels, src_seg, tgt_seg = (
        small[:, k * tokens : (k + 1) * tokens] for k in range(5)
    )

    def own_block(blocks):
        return lax.dynamic_index_in_dim(blocks, block, 0, keepdims=False)

    def key_order(blocks):
        pairs = blocks.reshape(cuts, 2, -1)
        pairs = jnp.where(core == 0, pairs, pairs[:, ::-1])
        return jnp.moveaxis(pairs, 1, 0).reshape(-1)

    comp_places = own_block(small[:, 5 * tokens :])
    comp_hit = one_hot(comp_places, tokens)
    own_labels = jnp.take(own_block(tgt_labels), comp_places)

    lookup = Lookup(jnp.concatenate([own_block(src_ids), own_block(tgt_ids)]), own_rows)
    token_rows = lookup.fetch(table_low)

    wide_low = wide_weight.astype(jnp.bfloat16)
    down_low = down_weight.astype(jnp.bfloat16)
    shard_rows, span = wide_low.shape
    bounds = [0, span * 2 // 5, span * 4 // 5, span]
    place_low = position_weight.astype(jnp.bfloat16)
    place_rows, place_columns = place_low.shape
    early_width = span - bounds[2] + bounds[1]
    by_tiles = (
        place_rows * place_columns == shard_rows * 512
        and place_columns % 128 == 0
        and shard_rows % 16 == 0
        and early_width % 512 == 0
    )
    if by_tiles:
        tiles = place_low.reshape(place_rows // 16, 16, place_columns // 128, 128)
        tiles = jnp.moveaxis(tiles, 1, 2).reshape(shard_rows // 16, 4, 16, 128)
        place_pack = jnp.moveaxis(tiles, 1, 2).reshape(shard_rows, 512)
    else:
        place_pack = place_low.reshape(shard_rows, -1)

    def gathered(parts):
        part = parts[0] if len(parts) == 1 else jnp.concatenate(parts, 1)
        return lax.all_gather(part, ALL).reshape(ctx_count, width, part.shape[1])

    def flat_down(part):
        part = part.reshape(-1, shard_rows, part.shape[1])
        return jnp.moveaxis(part, 0, 1).reshape(shard_rows, -1)

    def tall_down(pack):
        return unpack_rows(pack.reshape(ctx_count, shard_count, shard_rows, -1), width // ctx_count)

    early = gathered([wide_low[:, : bounds[1]], wide_low[:, bounds[2] :], place_pack])
    middle = gathered([wide_low[:, bounds[1] : bounds[2]], flat_down(down_low[0])])
    late = gathered([flat_down(down_low[1])])
    if by_tiles:
        position_full = unpack_places(
            early.reshape(ctx_count, shard_count, shard_rows, -1),
            early_width,
            place_rows,
            place_columns,
        )
    else:
        position_full = early[:, :, early_width:].reshape(
            (ctx_count, shard_count) + position_weight.shape
        )
        position_full = jnp.moveaxis(position_full, 0, 2).reshape(-1, width)

    def columns(name, size=None):
        start = starts[name]
        size = size or (hidden if name in FIRSTS else width)
        pieces = []
        while size:
            side, inner = divmod(start, span)
            turn = max(k for k in range(3) if bounds[k] <= inner)
            take = min(size, bounds[turn + 1] - inner)
            source = middle if turn == 1 else early
            at = inner - (0, bounds[1], bounds[2] - bounds[1])[turn]
            pieces.append(source[side, :, at : at + take])
            start, size = start + take, size - take
        return pieces[0] if len(pieces) == 1 else jnp.concatenate(pieces, 1)

    def vector_row(name):
        return vector_weight[name]

    blocks = hidden // width
    base_row = Row.dec_norm3_bias + 1
    enc_first_bias = vector_weight[base_row : base_row + blocks].reshape(-1)
    dec_first_bias = vector_weight[base_row + blocks : base_row + 2 * blocks].reshape(-1)
    names = range(Part.dec_first + 1)
    starts, offset = {}, 0
    for name in names:
        starts[name] = offset
        offset += hidden if name in FIRSTS else width


    table_count = position_full.shape[0]
    src_pos = own_block(doc_positions(src_seg.reshape(-1), table_count).reshape(ctx_count, -1))
    tgt_pos = own_block(doc_positions(tgt_seg.reshape(-1), table_count).reshape(ctx_count, -1))
    src_onehot = one_hot(src_pos, table_count)
    tgt_onehot = one_hot(tgt_pos, table_count)
    src_input = token_rows[:tokens] + product(src_onehot, position_full)
    tgt_input = token_rows[tokens:] + product(tgt_onehot, position_full)

    key_places = key_order(jnp.arange(ctx_count * tokens).reshape(ctx_count, tokens))
    src_keys_seg = key_order(src_seg)
    tgt_keys_seg = key_order(tgt_seg)
    own_src_seg = own_block(src_seg)
    own_tgt_seg = own_block(tgt_seg)
    def no_limit(seg):
        return jnp.full_like(seg, ctx_count * tokens)

    comp_seg = jnp.take(own_tgt_seg, comp_places)

    def marks(query_seg, query_last, key_seg):
        return (
            jnp.pad(jnp.stack([query_seg, query_last]), ((0, 6), (0, 0))),
            jnp.pad(jnp.stack([key_seg, key_places], 1), ((0, 0), (0, 126))),
        )

    enc_marks = marks(own_src_seg, no_limit(own_src_seg), src_keys_seg)
    self_marks = marks(comp_seg, block * tokens + comp_places, tgt_keys_seg)
    cross_marks = marks(comp_seg, no_limit(comp_seg), src_keys_seg)

    def norm(values, gain, bias):
        return norm_forward(values, vector_row(gain), vector_row(bias))

    enc_norm0, enc_saved0 = norm(src_input, Row.enc_norm0_gain, Row.enc_norm0_bias)
    enc_in_b = enc_norm0.astype(jnp.bfloat16)
    enc_queries = project_queries(enc_in_b, columns(Part.enc_wq), vector_row(Row.enc_query_bias))
    enc_pairs = project_pairs(
        enc_in_b, columns(Part.enc_wk, 2 * width), vector_row(Row.enc_value_bias)
    )
    enc_pairs_all = pairs_in(enc_pairs)
    dec_norm0, dec_saved0 = norm(tgt_input, Row.dec_norm0_gain, Row.dec_norm0_bias)
    dec_in_b = dec_norm0.astype(jnp.bfloat16)
    comp_exact = comp_hit.astype(jnp.float32)
    comp_norm0 = jnp.dot(comp_exact, dec_norm0, precision=PRECISE)
    comp_in_b = product(comp_hit, dec_in_b).astype(jnp.bfloat16)
    dec_queries = project_queries(comp_in_b, columns(Part.dec_wq), vector_row(Row.dec_query_bias))
    dec_pairs = project_pairs(
        dec_in_b, columns(Part.dec_wk, 2 * width), vector_row(Row.dec_value_bias)
    )
    dec_pairs_all = pairs_in(dec_pairs)
    enc_branch, enc_mixed_t, enc_logsum = branch_forward(
        enc_queries,
        enc_pairs_all,
        enc_marks,
        columns(Part.enc_out),
        vector_row(Row.enc_out_bias),
        head_count,
    )
    enc_norm1, enc_saved1 = norm(enc_norm0 + enc_branch, Row.enc_norm1_gain, Row.enc_norm1_bias)
    self_branch, self_mixed_t, self_logsum = branch_forward(
        dec_queries,
        dec_pairs_all,
        self_marks,
        columns(Part.dec_out),
        vector_row(Row.dec_out_bias),
        head_count,
    )
    dec_norm1, dec_saved1 = norm(comp_norm0 + self_branch, Row.dec_norm1_gain, Row.dec_norm1_bias)
    cross_in_b = dec_norm1.astype(jnp.bfloat16)
    cross_queries = project_queries(
        cross_in_b, columns(Part.cross_wq), vector_row(Row.cross_query_bias)
    )

    def both_lefts(parts, turned):
        own, other = turn_rows(parts, turned, shard_rows)
        return own, swapped(other, "c")

    left = both_lefts((enc_in_b, dec_in_b), (enc_mixed_t,))
    comp_left = both_lefts((comp_in_b,), (self_mixed_t,))
    table_pair = jnp.concatenate([table_low, swapped(table_low, "c")], 0)
    enc_norm1, cross_queries, middle, own_labels, left, comp_left, table_pair = hold(
        enc_norm1, cross_queries, middle, own_labels, left, comp_left, table_pair
    )
    head_labels = group_in(own_labels, "q").reshape(-1)
    enc_first, enc_second = (
        columns(Part.enc_first),
        tall_down(middle[:, :, bounds[2] - bounds[1] :]),
    )
    enc_mid_b = enc_norm1.astype(jnp.bfloat16)
    enc_ffn, enc_slope, enc_act_t = feed_forward(
        enc_mid_b, enc_first, enc_first_bias, enc_second, vector_row(Row.enc_ffn_bias)
    )
    encoded, enc_saved2 = norm(enc_norm1 + enc_ffn, Row.enc_norm2_gain, Row.enc_norm2_bias)
    encoded_b = encoded.astype(jnp.bfloat16)
    cross_pair_weights = columns(Part.cross_wk, 2 * width)
    cross_pairs = project_pairs(encoded_b, cross_pair_weights, vector_row(Row.cross_value_bias))
    cross_pairs_all = pairs_in(cross_pairs)
    cross_branch, cross_mixed_t, cross_logsum = branch_forward(
        cross_queries,
        cross_pairs_all,
        cross_marks,
        columns(Part.cross_out),
        vector_row(Row.cross_out_bias),
        head_count,
    )
    dec_norm2, dec_saved2 = norm(dec_norm1 + cross_branch, Row.dec_norm2_gain, Row.dec_norm2_bias)
    dec_norm2, late, head_labels = hold(dec_norm2, late, head_labels)
    dec_first, dec_second = columns(Part.dec_first), tall_down(late)
    dec_mid_b = dec_norm2.astype(jnp.bfloat16)
    dec_ffn, dec_slope, dec_act_t = feed_forward(
        dec_mid_b, dec_first, dec_first_bias, dec_second, vector_row(Row.dec_ffn_bias)
    )
    final, dec_saved3 = norm(dec_norm2 + dec_ffn, Row.dec_norm3_gain, Row.dec_norm3_bias)
    final_b = final.astype(jnp.bfloat16)
    head_rows = group_rows(final_b)

    to_turn = ((enc_mid_b, encoded_b), (cross_in_b, dec_mid_b))
    to_turn, head_labels, _ = hold(to_turn, head_labels, final_b)
    mid_left = both_lefts(to_turn[0], ())
    late_left = both_lefts(to_turn[1], (cross_mixed_t,))
    group_start = 0
    for axis in ("q", "p", "z", "x"):
        group_start = group_start * lax.axis_size(axis) + lax.axis_index(axis)
    own_ids = jnp.arange(own_rows, dtype=jnp.int32)
    column_ids = jnp.concatenate(
        [(group_start * 2 + core) * own_rows + own_ids, (group_start * 2 + 1 - core) * own_rows + own_ids]
    )

    def act_left(act_t):
        act_t = act_t.reshape(lax.axis_size("z"), 2, 2, -1, act_t.shape[1])
        own, other = pick(act_t, 2, core), pick(act_t, 2, 1 - core)
        return own[None], swapped(other, "c")[None]

    enc_act, dec_act = act_left(enc_act_t), act_left(dec_act_t)
    head_rows, mid_left, late_left, enc_act, dec_act = hold(
        head_rows, mid_left, late_left, enc_act, dec_act
    )
    terms, mixed_rows, label_rows, stats = head_forward(
        table_pair, head_rows, column_ids, head_labels
    )
    merged_top, merged_sum, merged_label = merge_stats(stats[:3])
    own_logsum = merged_top + jnp.log(merged_sum)
    loss_local = jnp.sum(own_logsum - merged_label)
    line = line_in(line_in(own_logsum, "p"), "z")
    came = from_others([line] * 3, ("q", "x"))
    logsum_rows = jnp.stack([line, came[1], came[0], came[2]]).reshape(-1)
    loss_scale = 1.0 / (comp_count * ctx_count * shard_count)
    row_scale = jnp.exp(stats[0] - logsum_rows)[:, None]
    mixed_rows = mixed_rows * row_scale - label_rows.astype(jnp.float32)
    grad_picked = group_sum(mixed_rows * loss_scale)
    table_grad, other_grad = head_table(
        terms, head_rows, column_ids, row_scale, head_labels, loss_scale
    )
    table_grad, other_grad, grad_picked = hold(table_grad, other_grad, grad_picked)
    table_grad = table_grad + swapped(other_grad, "c")
    vector_grads = {}
    reducer = Reducer()

    def norm_back(grad, saved, gain):
        grad, vector_grads[gain], vector_grads[gain + 1] = norm_backward(
            grad, saved, vector_row(gain)
        )
        return grad

    grad_sum3 = norm_back(grad_picked, dec_saved3, Row.dec_norm3_gain)
    grad_mid, dec_pre_grad, dec_first_bias_g, dec_ffn_grad, vector_grads[Row.dec_ffn_bias] = (
        feed_backward(grad_sum3, dec_slope, dec_first, dec_second)
    )
    grad_sum2 = norm_back(grad_sum3 + grad_mid, dec_saved2, Row.dec_norm2_gain)
    group1 = reducer.add(
        Group(
            (True, late_left, both_cores(dec_pre_grad), ((Part.dec_first, 1, None),)),
            (False, dec_act, both_cores(dec_ffn_grad[None]), ((Part.dec_second, 0, 0),)),
            mixed=1,
        )
    )
    cross_query_grad, cross_grad_pairs, cross_branch_grad, vector_grads[Row.cross_out_bias] = (
        branch_backward(
            grad_sum2,
            cross_queries,
            cross_pairs_all,
            cross_marks,
            cross_logsum,
            columns(Part.cross_out),
            head_count,
        )
    )
    cross_query_grad, cross_grad_pairs = reducer.step(cross_query_grad, cross_grad_pairs)
    cross_pairs_grad = pairs_back(cross_grad_pairs)
    vector_grads[Row.cross_query_bias], grad_cross_in = query_backward(
        columns(Part.cross_wq), cross_query_grad
    )
    grad_sum1 = norm_back(grad_sum2 + grad_cross_in, dec_saved1, Row.dec_norm1_gain)
    cross_pairs_grad, grad_sum1 = reducer.step(cross_pairs_grad, grad_sum1, only=(group1,))
    vector_grads[Row.cross_value_bias], grad_encoded = pairs_backward(
        cross_pair_weights, cross_pairs_grad
    )
    comp_right = both_cores(jnp.stack([cross_query_grad, cross_branch_grad]))
    group2 = group = reducer.add(
        Group(
            (True, mid_left, both_cores(cross_pairs_grad), ((Part.cross_wk, 1, 0), (Part.cross_wv, 1, 1))),
            (False, late_left, comp_right, ((Part.cross_wq, 0, 0), (Part.cross_out, 2, 1))),
            mixed=4,
        )
    )
    grad_sum1 = group.before(grad_sum1)
    dec_query_grad, dec_grad_pairs, dec_branch_grad, vector_grads[Row.dec_out_bias] = (
        branch_backward(
            grad_sum1,
            dec_queries,
            dec_pairs_all,
            self_marks,
            self_logsum,
            columns(Part.dec_out),
            head_count,
        )
    )
    grad_encoded, dec_query_grad, dec_grad_pairs, table_grad = reducer.step(
        grad_encoded, dec_query_grad, dec_grad_pairs, table_grad, only=(group2,)
    )
    dec_pairs_grad = pairs_back(dec_grad_pairs)
    vector_grads[Row.dec_query_bias], grad_dec_q_in = query_backward(
        columns(Part.dec_wq), dec_query_grad
    )
    vector_grads[Row.dec_value_bias], grad_dec_kv_in = pairs_backward(
        columns(Part.dec_wk, 2 * width), dec_pairs_grad
    )
    comp_right = both_cores(jnp.stack([dec_query_grad, dec_branch_grad]))
    group3 = reducer.add(
        Group(
            (True, left, both_cores(dec_pairs_grad), ((Part.dec_wk, 1, 0), (Part.dec_wv, 1, 1))),
            (False, comp_left, comp_right, ((Part.dec_wq, 0, 0), (Part.dec_out, 1, 1))),
            mixed=4,
        )
    )
    grad_enc2 = norm_back(grad_encoded, enc_saved2, Row.enc_norm2_gain)
    grad_comp0 = lax.dot_general(
        comp_exact, grad_sum1 + grad_dec_q_in, LEFT_T, precision=PRECISE
    )
    grad_tgt_input = norm_back(grad_comp0 + grad_dec_kv_in, dec_saved0, Row.dec_norm0_gain)
    grad_enc2, grad_tgt_input = reducer.step(grad_enc2, grad_tgt_input, only=(group1, group2))
    grad_enc_mid, enc_pre_grad, enc_first_bias_g, enc_ffn_grad, vector_grads[Row.enc_ffn_bias] = (
        feed_backward(grad_enc2, enc_slope, enc_first, enc_second)
    )
    grad_enc1 = norm_back(grad_enc2 + grad_enc_mid, enc_saved1, Row.enc_norm1_gain)
    grad_enc1, enc_pre_grad, enc_ffn_grad = reducer.step(grad_enc1, enc_pre_grad, enc_ffn_grad)
    group4 = reducer.add(
        Group(
            (True, mid_left, both_cores(enc_pre_grad), ((Part.enc_first, 0, None),)),
            (False, enc_act, both_cores(enc_ffn_grad[None]), ((Part.enc_second, 0, 0),)),
            mixed=1,
        )
    )
    enc_query_grad, enc_grad_pairs, enc_branch_grad, vector_grads[Row.enc_out_bias] = (
        branch_backward(
            grad_enc1,
            enc_queries,
            enc_pairs_all,
            enc_marks,
            enc_logsum,
            columns(Part.enc_out),
            head_count,
        )
    )
    enc_query_grad, enc_grad_pairs = reducer.step(enc_query_grad, enc_grad_pairs)
    enc_pairs_grad = pairs_back(enc_grad_pairs)
    vector_grads[Row.enc_query_bias], grad_enc_q_in = query_backward(
        columns(Part.enc_wq), enc_query_grad
    )
    vector_grads[Row.enc_value_bias], grad_enc_kv_in = pairs_backward(
        columns(Part.enc_wk, 2 * width), enc_pairs_grad
    )
    grad_src_input = norm_back(
        grad_enc1 + grad_enc_q_in + grad_enc_kv_in, enc_saved0, Row.enc_norm0_gain
    )
    right = both_cores(
        jnp.concatenate([enc_pairs_grad, enc_query_grad[None], enc_branch_grad[None]], 0)
    )
    group = reducer.add(
        Group(
            (True, left, right, ((Part.enc_wk, 0, 0), (Part.enc_wv, 0, 1))),
            (False, left, right, ((Part.enc_wq, 0, 2), (Part.enc_out, 2, 3))),
            mixed=4,
        )
    )
    table_grad = lookup.give(
        table_grad,
        jnp.concatenate(
            [grad_src_input.astype(jnp.bfloat16), grad_tgt_input.astype(jnp.bfloat16)], 0
        ),
    )
    grad_src_input, grad_tgt_input = group.before(grad_src_input, grad_tgt_input)
    position_grad = lax.dot_general(
        src_onehot.astype(jnp.float32), grad_src_input, LEFT_T, precision=PRECISE
    ) + lax.dot_general(
        tgt_onehot.astype(jnp.float32), grad_tgt_input, LEFT_T, precision=PRECISE
    )
    reducer.add(Group(ready=[(Part.position, position_grad)]))
    vector_grad = pack_rows(
        [vector_grads[name] for name in range(base_row)] + [enc_first_bias_g, dec_first_bias_g],
        width,
    )
    while reducer.moving:
        reducer.advance()
    summed = reducer.done

    def own_columns(part):
        if cuts == 1:
            return own_first(part, 1)[0]
        part = part.reshape(part.shape[0], ctx_count, -1)
        return lax.dynamic_index_in_dim(part, ctx_index, 1, keepdims=False)

    wide_grad = own_columns(
        jnp.concatenate(
            [
                summed[name]
                for name in (
                    Part.enc_wq,
                    Part.enc_wk,
                    Part.enc_out,
                    Part.enc_first,
                    Part.dec_wq,
                    Part.dec_wk,
                    Part.dec_out,
                    Part.cross_wq,
                    Part.cross_wk,
                    Part.cross_out,
                    Part.dec_first,
                )
            ],
            1,
        )
    )
    deep = [summed[name] for name in (Part.enc_second, Part.dec_second, Part.position)]
    if cuts > 1:
        deep = [own_columns(part) for part in deep]
    down_grad, position_grad = jnp.stack(deep[:2]), deep[2]
    owned_squares = (
        jnp.sum(wide_grad * wide_grad)
        + jnp.sum(down_grad * down_grad)
        + jnp.sum(position_grad * position_grad)
        + jnp.sum(table_grad * table_grad)
    )
    scalars = jnp.pad(jnp.stack([owned_squares, loss_local])[None, :], ((0, 0), (0, width - 2)))
    sums = all_sum(jnp.concatenate([vector_grad, scalars], 0))
    vector_grad, square_total, loss_sum = sums[:-1], sums[-1, 0], sums[-1, 1]
    grad_norm = jnp.sqrt(square_total + jnp.sum(vector_grad * vector_grad))
    clip_factor = jnp.minimum(1.0, CLIP_LIMIT / (grad_norm + 1e-06))
    outs = [loss_sum, grad_norm]
    for weight, moment, square, grad, decay, rate in (
        (table_weight, table_moment, table_square, table_grad, WEIGHT_DECAY, LEARN_RATE),
        (position_weight, position_moment, position_square, position_grad, WEIGHT_DECAY, LEARN_RATE),
        (wide_weight, wide_moment, wide_square, wide_grad, WEIGHT_DECAY, LEARN_RATE),
        (down_weight, down_moment, down_square, down_grad, WEIGHT_DECAY, LEARN_RATE),
        (vector_weight, vector_moment, vector_square, vector_grad, 0.0, VECTOR_RATE),
    ):
        outs.extend(adam_step(weight, moment, square, grad * clip_factor, decay, rate))
    return tuple(outs)


def solution(mesh):
    ctx_count, shard_count = mesh.devices.shape
    fine = Mesh(mesh.devices.reshape(2, ctx_count // 2, shard_count // 4, 2, 2), ALL)
    ctx, shard = ("q", "p"), ("z", "x", "c")
    table, plane, deep, whole = P(ALL, None), P(shard, ctx), P(None, shard, ctx), P()
    states = (table,) * 3 + (plane,) * 6 + (deep,) * 3 + (whole,) * 3
    return jax.shard_map(
        local,
        mesh=fine,
        in_specs=states + (plane,) * 6,
        out_specs=(whole, whole) + states,
        check_vma=False,
    )
```

```python
import functools
import math

import jax
import jax.numpy as jnp
from jax import lax
from jax.experimental import pallas as pl
from jax.experimental.pallas import tpu as pltpu
from jax.sharding import Mesh
from jax.sharding import PartitionSpec as P

H = 12
V = 50265
STEP = 10


PRECISE = lax.Precision.HIGHEST
NORM_EPS = 1e-05
LEARN_RATE = 0.03
VECTOR_RATE = 0.3
BETA_ONE = 0.9
BETA_TWO = 0.999
ADAM_EPS = 1e-08
WEIGHT_DECAY = 0.01
CLIP_LIMIT = 0.05
MASKED_SCORE = -1e30

class Row:
    (
        enc_norm0_gain,
        enc_norm0_bias,
        enc_query_bias,
        enc_value_bias,
        enc_out_bias,
        enc_norm1_gain,
        enc_norm1_bias,
        enc_ffn_bias,
        enc_norm2_gain,
        enc_norm2_bias,
        dec_norm0_gain,
        dec_norm0_bias,
        dec_query_bias,
        dec_value_bias,
        dec_out_bias,
        dec_norm1_gain,
        dec_norm1_bias,
        cross_query_bias,
        cross_value_bias,
        cross_out_bias,
        dec_norm2_gain,
        dec_norm2_bias,
        dec_ffn_bias,
        dec_norm3_gain,
        dec_norm3_bias,
    ) = range(25)


class Part:
    (
        enc_wq,
        enc_wk,
        enc_wv,
        enc_out,
        enc_first,
        dec_wq,
        dec_wk,
        dec_wv,
        dec_out,
        cross_wq,
        cross_wk,
        cross_wv,
        cross_out,
        dec_first,
        enc_second,
        dec_second,
        position,
    ) = range(17)


FIRSTS = (Part.enc_first, Part.dec_first)


def product(left, right):
    return jnp.dot(left, right, preferred_element_type=jnp.float32)


def product_t(left, right):
    return lax.dot_general(
        left, right, (((1,), (1,)), ((), ())), preferred_element_type=jnp.float32
    )


def row_contract(left, right):
    return lax.dot_general(
        left, right, (((0,), (0,)), ((), ())), preferred_element_type=jnp.float32
    )


NORMAL = (((1,), (0,)), ((), ()))
RIGHT_T = (((1,), (1,)), ((), ()))
LEFT_T = (((0,), (0,)), ((), ()))
KERNEL_BYTES = 48 * 2**20


def dot(left, right, dims):
    return lax.dot_general(left, right, dims, preferred_element_type=jnp.float32)


def norm_forward(values, gain, bias):
    center = values - jnp.mean(values, -1, keepdims=True)
    scale = lax.rsqrt(jnp.mean(center * center, -1, keepdims=True) + NORM_EPS)
    unit = center * scale
    return unit * gain + bias, (unit, scale)


def norm_backward(grad, saved, gain):
    unit, scale = saved
    grad_unit = grad * gain
    shift = jnp.mean(grad_unit, -1, keepdims=True)
    slope = jnp.mean(grad_unit * unit, -1, keepdims=True)
    return (
        scale * (grad_unit - shift - unit * slope),
        jnp.sum(grad * unit, 0, keepdims=True),
        jnp.sum(grad, 0, keepdims=True),
    )


def column_sums(part, dims=NORMAL):
    count = part.shape[dims[0][1][0]]
    return dot(jnp.ones((8, count), jnp.bfloat16), part, dims)[:1]


def doc_positions(segment, limit):
    length = segment.shape[0]
    places = jnp.arange(length, dtype=jnp.int32)
    change = jnp.concatenate([jnp.ones((1,), bool), segment[1:] != segment[:-1]])
    starts = lax.cummax(jnp.where(change, places, 0), axis=0)
    return jnp.minimum(places - starts, limit - 1)


def combine_partial(first, second):
    top_value = jnp.maximum(first[0], second[0])
    sum_value = first[1] * jnp.exp(first[0] - top_value) + second[1] * jnp.exp(
        second[0] - top_value
    )
    return (top_value, sum_value, first[2] + second[2])


def project_queries(inputs_b, weight_q, bias_q):
    return ((product(inputs_b, weight_q) + bias_q) * 0.125).astype(jnp.bfloat16)


def project_pairs(inputs_b, weight_pair, bias_v):
    bias = jnp.concatenate([jnp.zeros_like(bias_v), bias_v])
    return (product(inputs_b, weight_pair) + bias).astype(jnp.bfloat16)


def query_backward(weight_q, grad_query):
    return (column_sums(grad_query), product_t(grad_query, weight_q))


def pairs_backward(weight_pair, pairs_grad):
    width = pairs_grad.shape[2]
    return (
        column_sums(pairs_grad[1]),
        product_t(pairs_grad[0], weight_pair[:, :width])
        + product_t(pairs_grad[1], weight_pair[:, width:]),
    )


def feed_forward(inputs_b, first_weight, first_bias, second_weight, second_bias):
    pre_act = dot(first_weight, inputs_b, (((0,), (1,)), ((), ()))) + first_bias[:, None]
    share = 0.5 + 0.5 * lax.erf(pre_act * 0.5**0.5)
    act_b = (pre_act * share).astype(jnp.bfloat16)
    slope = share + pre_act * jnp.exp(-0.5 * pre_act * pre_act) * (0.5 / math.pi) ** 0.5
    return (dot(act_b, second_weight, LEFT_T) + second_bias, slope, act_b)


def feed_backward(grad_branch, slope, first_weight, second_weight):
    branch_grad = grad_branch.astype(jnp.bfloat16)
    grad_pre = (dot(second_weight, branch_grad, RIGHT_T) * slope).astype(jnp.bfloat16)
    return (
        dot(grad_pre, first_weight, (((0,), (1,)), ((), ()))),
        grad_pre,
        column_sums(grad_pre, RIGHT_T),
        branch_grad,
        column_sums(branch_grad),
    )


def adam_step(weight, moment, square, grad, decay, rate):
    new_moment = BETA_ONE * moment + (1.0 - BETA_ONE) * grad
    new_square = BETA_TWO * square + (1.0 - BETA_TWO) * grad * grad
    direction = (
        new_moment
        / (1.0 - BETA_ONE**STEP)
        / (jnp.sqrt(new_square / (1.0 - BETA_TWO**STEP)) + ADAM_EPS)
    )
    return (new_moment, new_square, weight - rate * (direction + decay * weight))


def fill_mask(query_ref, key_ref, mask_ref):

    @pl.when(pl.program_id(0) == 0)
    def _():
        allowed = (key_ref[:, 0:1] == query_ref[0:1, :]) & (key_ref[:, 1:2] <= query_ref[1:2, :])
        mask_ref[...] = jnp.where(allowed, 1.0, 0.0)


def attention_kernel(
    query_ref,
    key_ref,
    q_ref,
    k_own_ref,
    k_came_ref,
    v_own_ref,
    v_came_ref,
    out_ref,
    turned_ref,
    logsum_ref,
    mask_ref,
    *,
    head_size,
):
    fill_mask(query_ref, key_ref, mask_ref)
    half = k_own_ref.shape[0]
    outs = []
    for head in range(q_ref.shape[1] // head_size):
        lanes = slice(head * head_size, (head + 1) * head_size)
        q = q_ref[:, lanes]
        keys = jnp.concatenate([k_own_ref[:, lanes], k_came_ref[:, lanes]], 0)
        scores = jnp.where(mask_ref[...] != 0.0, dot(keys, q, RIGHT_T), MASKED_SCORE)
        top = jnp.max(scores, 0, keepdims=True)
        terms = jnp.exp(scores - top)
        total = jnp.sum(terms, 0, keepdims=True)
        probs = (terms * (1.0 / total)).astype(jnp.bfloat16)
        outs.append(
            dot(v_own_ref[:, lanes], probs[:half], LEFT_T)
            + dot(v_came_ref[:, lanes], probs[half:], LEFT_T)
        )
        logsum_ref[0, head : head + 1, :] = top + jnp.log(total)
    out = jnp.concatenate(outs, 0)
    turned_ref[...] = out.astype(jnp.bfloat16)
    out_ref[...] = out.T.astype(jnp.bfloat16)


def attention_back_kernel(
    query_ref,
    key_ref,
    q_ref,
    k_own_ref,
    k_came_ref,
    v_own_ref,
    v_came_ref,
    grad_ref,
    logsum_ref,
    grad_q_ref,
    own_ref,
    other_ref,
    mask_ref,
    *,
    head_size,
):
    fill_mask(query_ref, key_ref, mask_ref)
    half = k_own_ref.shape[0]
    q_parts, k_parts, v_parts = [], [], []
    for head in range(q_ref.shape[1] // head_size):
        lanes = slice(head * head_size, (head + 1) * head_size)
        q, grad = q_ref[:, lanes], grad_ref[:, lanes]
        keys = jnp.concatenate([k_own_ref[:, lanes], k_came_ref[:, lanes]], 0)
        values = jnp.concatenate([v_own_ref[:, lanes], v_came_ref[:, lanes]], 0)
        scores = jnp.where(mask_ref[...] != 0.0, dot(keys, q, RIGHT_T), MASKED_SCORE)
        probs = jnp.exp(scores - logsum_ref[0, head : head + 1, :])
        grad_probs = dot(values, grad, RIGHT_T)
        shift = jnp.sum(grad_probs * probs, 0, keepdims=True)
        grad_scores = (probs * (grad_probs - shift)).astype(jnp.bfloat16)
        v_parts.append(dot(probs.astype(jnp.bfloat16), grad, NORMAL))
        k_parts.append(dot(grad_scores, q, NORMAL))
        q_parts.append(dot(keys, grad_scores, LEFT_T))
    grad_q_ref[...] = jnp.concatenate(q_parts, 0).T.astype(jnp.bfloat16) * jnp.bfloat16(0.125)
    for at, parts in enumerate((k_parts, v_parts)):
        grad_pair = jnp.concatenate(parts, 1)
        own_ref[at] = grad_pair[:half]
        other_ref[at] = grad_pair[half:]


def attention_call(kernel, results, marks, head_count, products, queries, pairs, extra=()):
    query_rows, width = queries.shape
    own, came = pairs
    key_rows = own.shape[0]
    head_size = width // head_count
    per_step = max(1, 128 // head_size)
    steps = head_count // per_step
    lanes = per_step * head_size
    heads = pl.BlockSpec((query_rows, lanes), lambda i: (0, i))
    keys = pl.BlockSpec((key_rows, lanes), lambda i: (0, i))
    values = pl.BlockSpec((key_rows, lanes), lambda i: (0, i + steps))
    sums = pl.BlockSpec((1, per_step, query_rows), lambda i: (i, 0, 0))
    kinds = {
        "q": (heads, (query_rows, width), jnp.bfloat16),
        "t": (pl.BlockSpec((lanes, query_rows), lambda i: (i, 0)), (width, query_rows), jnp.bfloat16),
        "s": (sums, (steps, per_step, query_rows), jnp.float32),
        "p": (
            pl.BlockSpec((2, key_rows, lanes), lambda i: (0, 0, i)),
            (2, key_rows, width),
            jnp.float32,
        ),
    }
    count = 2 * query_rows * key_rows
    return pl.pallas_call(
        functools.partial(kernel, head_size=head_size),
        grid=(steps,),
        in_specs=[pl.BlockSpec(part.shape, lambda i: (0, 0)) for part in marks]
        + [heads, keys, keys, values, values]
        + [heads, sums][: len(extra)],
        out_specs=[kinds[kind][0] for kind in results],
        out_shape=[jax.ShapeDtypeStruct(*kinds[kind][1:]) for kind in results],
        scratch_shapes=[pltpu.VMEM((2 * key_rows, query_rows), jnp.float32)],
        compiler_params=pltpu.CompilerParams(vmem_limit_bytes=KERNEL_BYTES),
        cost_estimate=pl.CostEstimate(
            flops=2 * products * count * width,
            bytes_accessed=2 * width * (query_rows + 2 * key_rows) * products,
            transcendentals=count * head_count,
        ),
    )(*marks, queries, own, came, own, came, *extra)


def branch_forward(queries, pairs, marks, weight_o, bias_o, head_count):
    mixed_b, mixed_t, logsum = attention_call(
        attention_kernel, "qts", marks, head_count, 2, queries, pairs
    )
    return (product(mixed_b, weight_o) + bias_o, mixed_t, logsum)


def branch_backward(grad_branch, queries, pairs, marks, logsum, weight_o, head_count):
    branch_grad = grad_branch.astype(jnp.bfloat16)
    grad_mixed = product_t(branch_grad, weight_o).astype(jnp.bfloat16)
    query_grad, own, other = attention_call(
        attention_back_kernel, "qpp", marks, head_count, 5, queries, pairs, (grad_mixed, logsum)
    )
    return (query_grad, (own, other), branch_grad, column_sums(branch_grad))


ALL = ("q", "p", "z", "x", "c")
SWAP = [(0, 1), (1, 0)]
SLOTS = 40


def swapped(part, axis):
    return lax.ppermute(part, axis, SWAP)


def one_hot(places, count):
    return (places[:, None] == jnp.arange(count, dtype=places.dtype)[None, :]).astype(jnp.bfloat16)


def shifted(part, axis, step):
    count = lax.axis_size(axis)
    return lax.ppermute(part, axis, [(i, (i + step) % count) for i in range(count)])


def line_in(part, axis):
    count = lax.axis_size(axis)
    return jnp.stack([part] + [shifted(part, axis, count - k) for k in range(1, count)])


def pair_in(part, axis, at):
    return jnp.stack([part, swapped(part, axis)], at)


def group_in(part, first):
    part = line_in(line_in(part, "p"), "z")
    if first == "q":
        part = pair_in(pair_in(part, "q", 0), "x", 0)
    else:
        part = pair_in(pair_in(part, "x", 0), "q", 1)
    return part


def group_rows(rows):
    half = rows.shape[1] // 2
    both = [group_in(rows[:, :half], "q"), group_in(rows[:, half:], "x")]
    return jnp.concatenate(both, -1).reshape(-1, rows.shape[1])


def send_half(part, axis, at):
    own = lax.index_in_dim(part, 0, at, keepdims=False)
    other = lax.index_in_dim(part, 1, at, keepdims=False)
    return own + swapped(other.astype(jnp.bfloat16), axis).astype(jnp.float32)


def send_line(part, axis):
    total = part[0]
    for k in range(1, lax.axis_size(axis)):
        total = total + shifted(part[k].astype(jnp.bfloat16), axis, k).astype(jnp.float32)
    return total


def group_sum(rows):
    ways = (2, 2, lax.axis_size("z"), lax.axis_size("p"))
    rows = rows.reshape(ways + (-1, rows.shape[-1]))
    half = rows.shape[-1] // 2
    first, second = rows[..., :half], rows[..., half:]
    first = send_half(send_half(first, "x", 0), "q", 0)
    second = send_half(send_half(second, "q", 1), "x", 0)
    return jnp.concatenate([send_line(send_line(part, "z"), "p") for part in (first, second)], -1)


def from_others(parts, axes):
    return [
        lax.ppermute(part, axes, [(i, i ^ (k + 1)) for i in range(4)])
        for k, part in enumerate(parts)
    ]


def merge_stats(stats):

    def merge(first, second):
        return jnp.stack(combine_partial(first, second))

    ways = (2, 2, lax.axis_size("z"), lax.axis_size("p"))
    stats = stats.reshape((3,) + ways + (-1,))
    came = from_others([stats[:, 1, 0], stats[:, 0, 1], stats[:, 1, 1]], ("q", "x"))
    stats = merge(merge(stats[:, 0, 0], came[0]), merge(came[1], came[2]))
    for axis in ("z", "p"):
        total = stats[:, 0]
        came = [shifted(stats[:, k], axis, k) for k in range(1, lax.axis_size(axis))]
        for part in came:
            total = merge(total, part)
        stats = total
    return stats


def unpack_kernel(pack_ref, out_ref, *, columns):
    sides, owners, rows, total = pack_ref.shape
    for side in range(sides):
        for owner in range(owners):
            for at in range(total // columns):
                row = (owner * (total // columns) + at) * rows
                out_ref[row : row + rows, side * columns : (side + 1) * columns] = pack_ref[
                    side, owner, :, at * columns : (at + 1) * columns
                ]


def unpack_rows(pack, columns):
    sides, owners, rows, total = pack.shape
    each = rows * total // columns
    step = math.gcd(owners, 4)
    if rows % 16:
        pack = pack.reshape(sides, owners, rows, -1, columns)
        return jnp.transpose(pack, (1, 3, 2, 0, 4)).reshape(owners * each, sides * columns)
    return pl.pallas_call(
        functools.partial(unpack_kernel, columns=columns),
        grid=(owners // step,),
        in_specs=[pl.BlockSpec((sides, step, rows, total), lambda i: (0, i, 0, 0))],
        out_specs=pl.BlockSpec((step * each, sides * columns), lambda i: (i, 0)),
        out_shape=jax.ShapeDtypeStruct((owners * each, sides * columns), pack.dtype),
        cost_estimate=pl.CostEstimate(flops=0, bytes_accessed=4 * pack.size, transcendentals=0),
    )(pack)


def places_kernel(pack_ref, out_ref):
    sides, owners, _, _ = pack_ref.shape
    rows, columns = out_ref.shape[0] // owners, out_ref.shape[1] // sides
    across = columns // 128
    for side in range(sides):
        for owner in range(owners):
            for tile in range(rows // 16 * across):
                row, lane = tile // 4 * 16, tile % 4 * 128
                to_row = owner * rows + tile // across * 16
                to_lane = side * columns + tile % across * 128
                out_ref[to_row : to_row + 16, to_lane : to_lane + 128] = pack_ref[
                    side, owner, row : row + 16, lane : lane + 128
                ]


def unpack_places(pack, at, rows, columns):
    sides, owners, height, _ = pack.shape
    step = math.gcd(owners, 8)
    return pl.pallas_call(
        places_kernel,
        grid=(owners // step,),
        in_specs=[pl.BlockSpec((sides, step, height, 512), lambda i: (0, i, 0, at // 512))],
        out_specs=pl.BlockSpec((step * rows, sides * columns), lambda i: (i, 0)),
        out_shape=jax.ShapeDtypeStruct((owners * rows, sides * columns), pack.dtype),
        cost_estimate=pl.CostEstimate(
            flops=0, bytes_accessed=4 * owners * rows * sides * columns, transcendentals=0
        ),
    )(pack)


def hold(*trees):
    return lax.optimization_barrier(trees)


def all_sum(part):
    part = part + swapped(part, "c")
    for axes in (("q", "x"), ("z",)):
        if axes == ("q", "x") or lax.axis_size("z") == 4:
            first, second, third = from_others([part] * 3, axes)
            part = (part + first) + (second + third)
        else:
            part = lax.psum(part, axes)
    return lax.psum(part, "p") if lax.axis_size("p") > 1 else part


def pick(part, axis, index):
    return lax.dynamic_index_in_dim(part, index, axis, keepdims=False)


def own_first(part, axis):
    half = part.shape[axis] // 2
    first = lax.slice_in_dim(part, 0, half, axis=axis)
    second = lax.slice_in_dim(part, half, 2 * half, axis=axis)
    here = lax.axis_index("q") == 0
    return jnp.where(here, first, second), jnp.where(here, second, first)


def line_kernel(place_ref, *refs, unit):
    count = (len(refs) - 2) // 2
    kept_ref, sent_ref = refs[-2:]
    blocks = []
    for own, other in zip(refs[:count], refs[count : 2 * count]):
        total = own[0] + other[0].astype(jnp.float32)
        blocks += [total[at : at + unit] for at in range(0, total.shape[0], unit)]

    @pl.when(pl.program_id(0) == 0)
    def _():
        at = 0
        for block in blocks:
            kept_ref[:, at : at + block.shape[1]] = block
            at += block.shape[1]

    @pl.when(pl.program_id(0) > 0)
    def _():
        at = 0
        for block in blocks:
            sent_ref[0, :, at : at + block.shape[1]] = block.astype(jnp.bfloat16)
            at += block.shape[1]


def line_parts(owns, others, unit):
    lines = owns[0].shape[0]
    columns = sum(own.shape[1] // unit * own.shape[2] for own in owns)
    specs = [
        pl.BlockSpec((1,) + own.shape[1:], lambda k, place: ((place[0] + k) % lines, 0, 0))
        for own in owns
    ]
    return pl.pallas_call(
        functools.partial(line_kernel, unit=unit),
        grid_spec=pltpu.PrefetchScalarGridSpec(
            num_scalar_prefetch=1,
            grid=(lines,),
            in_specs=specs * 2,
            out_specs=[
                pl.BlockSpec((unit, columns), lambda k, place: (0, 0)),
                pl.BlockSpec((1, unit, columns), lambda k, place: (jnp.maximum(k - 1, 0), 0, 0)),
            ],
        ),
        out_shape=[
            jax.ShapeDtypeStruct((unit, columns), jnp.float32),
            jax.ShapeDtypeStruct((lines - 1, unit, columns), jnp.bfloat16),
        ],
        compiler_params=pltpu.CompilerParams(vmem_limit_bytes=KERNEL_BYTES),
        cost_estimate=pl.CostEstimate(
            flops=lines * unit * columns, bytes_accessed=8 * lines * unit * columns, transcendentals=0
        ),
    )(lax.axis_index("z").astype(jnp.int32).reshape(1), *owns, *others)


def factor_kernel(place_ref, *refs, turned, halves):
    (near, near_came, far, far_came), rights = refs[:4], refs[4:-2]
    kept_ref, sent_ref = refs[-2:]
    dims = RIGHT_T if turned else NORMAL

    def rows(ref):
        block = ref[...]
        return block.reshape(-1, block.shape[-1])

    def side(own, came, at):
        right, right_came = (ref[...].reshape(ref.shape[-2:]) for ref in rights[2 * at : 2 * at + 2])
        return dot(rows(own), right, dims) + dot(rows(came), right_came, dims)

    if halves:
        kept_ref[0], kept_ref[1] = side(near, near_came, 0), side(far, far_came, 0)
        sent_ref[0] = side(near, near_came, 1).astype(jnp.bfloat16)
        sent_ref[1] = side(far, far_came, 1).astype(jnp.bfloat16)
    else:
        kept_ref[...] = side(near, near_came, 0)
        sent_ref[...] = side(far, far_came, 0).astype(jnp.bfloat16)


def factor_parts(left, right, names, halves):
    own, came = left
    right, right_came = right
    _, lines, _, rows, tokens = own.shape
    turned = right.ndim == 2
    width = right.shape[0] if turned else right.shape[2]
    step = width // 2 if halves or width < 3072 else 384
    blocks = width // step
    place = [lax.axis_index("x"), lax.axis_index("q")]
    place += [left_at for _, left_at, _ in names] + [right_at or 0 for _, _, right_at in names]
    place = jnp.stack([jnp.asarray(part, jnp.int32) for part in place])
    count, groups = lines * rows, len(names)
    inner = 1 if halves else blocks

    def left_spec(far):

        def at_place(j, at):
            return at[2 + j // inner], 0, 1 - at[0] if far else at[0], 0, 0

        return pl.BlockSpec((1, lines, 1, rows, tokens), at_place)

    def right_spec(other):

        def at_place(j, at):
            if turned:
                return j, 0
            part = (1 - at[1] if other else at[1]) if halves else j % inner
            return at[2 + groups + j // inner], 0, part

        return pl.BlockSpec((step, tokens) if turned else (1, tokens, step), at_place)

    steps = groups * inner
    shape = (2, count, steps * step) if halves else (count, steps * step)
    out_spec = (
        pl.BlockSpec((2, count, step), lambda j, at: (0, 0, j))
        if halves
        else pl.BlockSpec((count, step), lambda j, at: (0, j))
    )
    rights = [right, right_came] * (2 if halves else 1)
    return pl.pallas_call(
        functools.partial(factor_kernel, turned=turned, halves=halves),
        grid_spec=pltpu.PrefetchScalarGridSpec(
            num_scalar_prefetch=1,
            grid=(steps,),
            in_specs=[left_spec(False), left_spec(False), left_spec(True), left_spec(True)]
            + [right_spec(at >= 2) for at in range(len(rights))],
            out_specs=[out_spec, out_spec],
        ),
        out_shape=[
            jax.ShapeDtypeStruct(shape, jnp.float32),
            jax.ShapeDtypeStruct(shape, jnp.bfloat16),
        ],
        compiler_params=pltpu.CompilerParams(vmem_limit_bytes=KERNEL_BYTES),
        cost_estimate=pl.CostEstimate(
            flops=8 * count * tokens * width * groups,
            bytes_accessed=8 * count * tokens + (4 * tokens + 12 * count) * width * groups,
            transcendentals=0,
        ),
    )(place, own, came, own, came, *rights)


class Group:
    def __init__(self, *factors, ready=(), mixed=0):
        core, side = lax.axis_index("c"), lax.axis_index("x")
        self.names, self.kept, self.flight, self.ways, self.rows = [], [], [], [], []
        self.mixed = mixed
        self.stage = 0
        for way, left, right, names in factors:
            kept, sent = factor_parts(left, right, names, not way)
            self.take([name for name, _, _ in names], kept, sent, way)
        for name, grad in ready:
            grad = grad.reshape(lax.axis_size("z"), 2, 2, -1, grad.shape[1])
            grad = pick(grad, 2, core) + swapped(pick(grad, 2, 1 - core), "c")
            self.take([name], pick(grad, 1, side), pick(grad, 1, 1 - side), True)
        self.unit = min(self.rows)

    def before(self, *live):
        self.kept, live = hold(self.kept, live)
        return live if len(live) > 1 else live[0]

    def take(self, names, kept, sent, way):
        self.names.append(names[:1] if way else names)
        kept, sent = (part.reshape(-1, part.shape[-1]) for part in (kept, sent))
        self.kept.append(kept)
        self.ways.append(way)
        self.rows.append(kept.shape[0] // lax.axis_size("z") // (1 if way else 2))
        self.flight.append(swapped(sent.astype(jnp.bfloat16), "x" if way else "q"))

    def advance(self):
        self.stage += 1
        lines = lax.axis_size("z")
        if self.stage == 1:
            for at, way in enumerate(self.ways):
                kept, came = self.kept[at], self.flight[at]
                total = kept + came.astype(jnp.float32)
                half = total.shape[0] // 2
                near, far = own_first(total, 1) if way else (total[:half], total[half:])
                self.kept[at] = near.reshape(lines, -1, near.shape[1])
                far = far.astype(jnp.bfloat16).reshape(lines, -1, far.shape[1])
                self.flight[at] = swapped(far, "q" if way else "x")
        elif self.stage == 2:
            self.shapes = [part.shape[1:] for part in self.kept]
            self.total, sent = line_parts(self.kept, self.flight, self.unit)
            self.flight = [shifted(sent[k], "z", k + 1) for k in range(sent.shape[0])]
        elif self.stage == 3:
            for part in self.flight:
                self.total = self.total + part.astype(jnp.float32)
            if lax.axis_size("p") > 1:
                self.total = lax.psum(self.total, "p")
                self.mixed = sum(len(names) for names in self.names)
            self.spans = []
            for names, (rows, columns) in zip(self.names, self.shapes):
                for name in names:
                    self.spans.append((name, rows // self.unit, columns // len(names)))
            width = sum(blocks * columns for _, blocks, columns in self.spans[: self.mixed])
            sent = self.total[:, :width].astype(jnp.bfloat16)
            self.flight = swapped(sent, "q") if self.mixed else ()
        else:
            at, self.done = 0, {}
            for turn, (name, blocks, columns) in enumerate(self.spans):
                parts = []
                for _ in range(blocks):
                    near = self.total[:, at : at + columns]
                    if turn < self.mixed:
                        far = self.flight[:, at : at + columns].astype(jnp.float32)
                        near = jnp.where(
                            lax.axis_index("q") == 0,
                            jnp.concatenate([near, far], 1),
                            jnp.concatenate([far, near], 1),
                        )
                    parts.append(near)
                    at += columns
                self.done[name] = parts[0] if len(parts) == 1 else jnp.concatenate(parts, 0)


class Reducer:

    def __init__(self):
        self.moving = []
        self.done = {}

    def add(self, item):
        self.moving.append(item)
        return item

    def step(self, *live, only=()):
        items = [item for item in self.moving if not only or item in only]
        live, flights = hold(live, [item.flight for item in items])
        for item, flight in zip(items, flights):
            item.flight = flight
        self.advance(items)
        return live if len(live) > 1 else live[0]

    def advance(self, items=None):
        for item in list(self.moving) if items is None else items:
            item.advance()
            if item.stage == 4:
                self.done.update(item.done)
        self.moving = [item for item in self.moving if item.stage < 4]


def pairs_in(pairs):
    both = (pairs, swapped(pairs, "c"))
    if lax.axis_size("p") > 1:
        both = tuple(lax.all_gather(part, "p", axis=0, tiled=True) for part in both)
    return both


def pairs_back(grads):
    if lax.axis_size("p") > 1:
        grads = tuple(
            lax.psum_scatter(part, "p", scatter_dimension=1, tiled=True) for part in grads
        )
    own, other = grads
    return (own + swapped(other, "c")).astype(jnp.bfloat16)


def both_cores(part):
    return part, swapped(part, "c")


def turn_kernel(core_ref, *refs, rows):
    parts, (own_ref, other_ref) = refs[:-2], refs[-2:]
    lines = own_ref.shape[1]
    for at, ref in enumerate(parts):
        part = ref[...]
        if part.shape[0] != lines * 4 * rows:
            part = part.astype(jnp.float32).T.astype(jnp.bfloat16)
        blocks = [part[k * rows : (k + 1) * rows] for k in range(4 * lines)]
        for here in range(2):

            @pl.when(core_ref[0] == here)
            def _():
                for line in range(lines):
                    for side in range(2):
                        first = (line * 2 + side) * 2
                        own_ref[at, line, side] = blocks[first + here]
                        other_ref[at, line, side] = blocks[first + 1 - here]


def turn_rows(parts, turned, rows):
    tokens, width = parts[0].shape
    lines = width // (4 * rows)
    count = len(parts) + len(turned)
    shape = (count, lines, 2, rows, tokens)
    if rows % 16 or tokens == width:
        whole = jnp.stack([part.T for part in parts] + list(turned))
        whole = whole.reshape(count, lines, 2, 2, rows, tokens)
        core = lax.axis_index("c")
        return pick(whole, 3, core), pick(whole, 3, 1 - core)
    vmem = pl.BlockSpec(memory_space=pltpu.VMEM)
    return pl.pallas_call(
        functools.partial(turn_kernel, rows=rows),
        in_specs=[pl.BlockSpec(memory_space=pltpu.SMEM)] + [vmem] * count,
        out_specs=[vmem, vmem],
        out_shape=[jax.ShapeDtypeStruct(shape, jnp.bfloat16)] * 2,
        compiler_params=pltpu.CompilerParams(vmem_limit_bytes=KERNEL_BYTES),
        cost_estimate=pl.CostEstimate(
            flops=0, bytes_accessed=4 * count * tokens * width, transcendentals=0
        ),
    )(lax.axis_index("c").astype(jnp.int32).reshape(1), *parts, *turned)


def pack_kernel(*refs, width):
    out_ref = refs[-1]
    at = 0
    for ref in refs[:-1]:
        for column in range(0, ref.shape[1], width):
            out_ref[at : at + 1, :] = ref[0:1, column : column + width]
            at += 1


def pack_rows(parts, width):
    count = sum(part.shape[1] // width for part in parts)
    vmem = pl.BlockSpec(memory_space=pltpu.VMEM)
    return pl.pallas_call(
        functools.partial(pack_kernel, width=width),
        in_specs=[vmem] * len(parts),
        out_specs=vmem,
        out_shape=jax.ShapeDtypeStruct((count, width), jnp.float32),
    )(*parts)


def head_kernel(
    table_ref, rows_ref, ids_ref, labels_ref, terms_ref, mixed_ref, label_rows_ref, stats_ref
):
    scores = dot(rows_ref[...], table_ref[...], RIGHT_T)
    ids = ids_ref[0:1, :]
    scores = jnp.where(ids < V, scores, MASKED_SCORE)
    top = jnp.max(scores, 1, keepdims=True)
    terms = jnp.exp(scores - top)
    total = jnp.sum(terms, 1, keepdims=True)
    terms = terms.astype(jnp.bfloat16)
    terms_ref[...] = terms
    mixed_ref[...] = dot(terms, table_ref[...], NORMAL)
    hit = ids == labels_ref[:, 0:1]
    chosen = jnp.where(hit, 1.0, 0.0).astype(jnp.bfloat16)
    label_rows = dot(chosen, table_ref[...], NORMAL)
    label_rows_ref[...] = label_rows.astype(jnp.bfloat16)
    label = jnp.sum(label_rows * rows_ref[...].astype(jnp.float32), 1, keepdims=True)
    lane = lax.broadcasted_iota(jnp.int32, (scores.shape[0], 128), 1)
    stats = jnp.where(lane == 0, top, jnp.where(lane == 1, total, label))
    stats_ref[...] = stats.T[:8]


def head_forward(table, rows, ids, labels):
    columns, width = table.shape
    count = rows.shape[0]
    step = math.gcd(count, 256)
    return pl.pallas_call(
        head_kernel,
        grid=(count // step,),
        in_specs=[
            pl.BlockSpec((columns, width), lambda i: (0, 0)),
            pl.BlockSpec((step, width), lambda i: (i, 0)),
            pl.BlockSpec((1, columns), lambda i: (0, 0)),
            pl.BlockSpec((step, 1), lambda i: (i, 0)),
        ],
        out_specs=[
            pl.BlockSpec((step, columns), lambda i: (i, 0)),
            pl.BlockSpec((step, width), lambda i: (i, 0)),
            pl.BlockSpec((step, width), lambda i: (i, 0)),
            pl.BlockSpec((8, step), lambda i: (0, i)),
        ],
        out_shape=[
            jax.ShapeDtypeStruct((count, columns), jnp.bfloat16),
            jax.ShapeDtypeStruct((count, width), jnp.float32),
            jax.ShapeDtypeStruct((count, width), jnp.bfloat16),
            jax.ShapeDtypeStruct((8, count), jnp.float32),
        ],
        compiler_params=pltpu.CompilerParams(vmem_limit_bytes=KERNEL_BYTES),
        cost_estimate=pl.CostEstimate(
            flops=6 * columns * width * count,
            bytes_accessed=2 * (columns * width + 4 * count * width + columns * count),
            transcendentals=columns * count,
        ),
    )(table, rows, ids[None, :], labels[:, None])


def table_kernel(terms_ref, rows_ref, ids_ref, marks_ref, labels_ref, own_ref, other_ref, total_ref, *, scale):
    probs = terms_ref[...].astype(jnp.float32) * marks_ref[:, 0:1]
    hit = ids_ref[0:1, :] == labels_ref[:, 0:1]
    grad = ((probs - jnp.where(hit, 1.0, 0.0)) * scale).astype(jnp.bfloat16)
    part = dot(grad, rows_ref[...], LEFT_T)

    @pl.when(pl.program_id(0) == 0)
    def _():
        total_ref[...] = part

    @pl.when(pl.program_id(0) > 0)
    def _():
        total_ref[...] += part

    @pl.when(pl.program_id(0) == pl.num_programs(0) - 1)
    def _():
        own_ref[...] = total_ref[: own_ref.shape[0]]
        other_ref[...] = total_ref[own_ref.shape[0] :]


def head_table(terms, rows, ids, row_scale, labels, scale):
    count, columns = terms.shape
    width = rows.shape[1]
    step = math.gcd(count, 256)
    half = pl.BlockSpec((columns // 2, width), lambda i: (0, 0))
    return pl.pallas_call(
        functools.partial(table_kernel, scale=scale),
        grid=(count // step,),
        in_specs=[
            pl.BlockSpec((step, columns), lambda i: (i, 0)),
            pl.BlockSpec((step, width), lambda i: (i, 0)),
            pl.BlockSpec((1, columns), lambda i: (0, 0)),
            pl.BlockSpec((step, 1), lambda i: (i, 0)),
            pl.BlockSpec((step, 1), lambda i: (i, 0)),
        ],
        out_specs=[half, half],
        out_shape=[jax.ShapeDtypeStruct((columns // 2, width), jnp.float32)] * 2,
        scratch_shapes=[pltpu.VMEM((columns, width), jnp.float32)],
        compiler_params=pltpu.CompilerParams(vmem_limit_bytes=KERNEL_BYTES),
        cost_estimate=pl.CostEstimate(
            flops=2 * columns * width * count,
            bytes_accessed=4 * columns * width + 2 * count * (width + columns),
            transcendentals=0,
        ),
    )(terms, rows, ids[None, :], row_scale, labels[:, None])


class Lookup:
    def __init__(self, token_ids, own_rows):
        owners = 1
        for axis in ALL:
            owners *= lax.axis_size(axis)
        self.owners = owners
        self.own_rows = own_rows
        count = token_ids.shape[0]
        places = jnp.arange(count, dtype=jnp.int32)
        owner = token_ids // own_rows
        same = token_ids[:, None] == token_ids[None, :]
        first = jnp.min(jnp.where(same, places[None, :], count), 1)
        is_first = first == places
        ahead = (owner[:, None] == owner[None, :]) & is_first[None, :] & (places[None, :] < first[:, None])
        self.rank = jnp.sum(ahead.astype(jnp.int32), 1)
        self.owner = owner
        self.is_first = is_first
        self.local_id = token_ids - owner * own_rows
    def round_places(self, turn):
        rank = self.rank - turn * SLOTS
        inside = (rank >= 0) & (rank < SLOTS)
        slot = jnp.where(inside, self.owner * SLOTS + rank, -1)
        to_owner = jnp.where(
            (self.owner[:, None] == jnp.arange(self.owners)[None, :]) & self.is_first[:, None],
            (self.local_id + 1).astype(jnp.float32)[:, None],
            0.0,
        )
        to_slot = (rank[:, None] == jnp.arange(SLOTS)[None, :]).astype(jnp.float32)
        asked = lax.dot_general(to_owner, to_slot, (((0,), (0,)), ((), ())), precision=PRECISE)
        asked = jnp.round(asked).astype(jnp.int32) - 1
        last = jnp.broadcast_to(jnp.max(self.rank), (self.owners, 1))
        wanted = lax.all_to_all(jnp.concatenate([asked, last], 1), ALL, 0, 0, tiled=True)
        self.rounds = jnp.max(wanted[:, SLOTS:]) // SLOTS + 1
        wanted = wanted[:, :SLOTS].reshape(-1)
        return one_hot(slot, self.owners * SLOTS), one_hot(wanted, self.own_rows)

    def fetch_round(self, turn, table_low):
        to_slot, to_row = self.round_places(turn)
        sent = product(to_row, table_low).astype(jnp.bfloat16)
        rows = lax.all_to_all(sent, ALL, 0, 0, tiled=True)
        return product(to_slot, rows), (to_slot, to_row)

    def fetch(self, table_low):
        rows, self.kept = self.fetch_round(0, table_low)
        rounds = self.rounds
        rows = lax.cond(
            rounds > 1,
            lambda: lax.fori_loop(
                1, rounds, lambda turn, total: total + self.fetch_round(turn, table_low)[0], rows
            ),
            lambda: rows,
        )
        self.rounds = rounds
        return rows

    def give_round(self, places, grads_b):
        to_slot, to_row = places
        sent = row_contract(to_slot, grads_b).astype(jnp.bfloat16)
        back = lax.all_to_all(sent, ALL, 0, 0, tiled=True)
        return row_contract(to_row, back)

    def give(self, total, grads_b):
        total = total + self.give_round(self.kept, grads_b)
        rounds = self.rounds
        return lax.cond(
            rounds > 1,
            lambda: lax.fori_loop(
                1,
                rounds,
                lambda turn, sums: sums + self.give_round(self.round_places(turn), grads_b),
                total,
            ),
            lambda: total,
        )


def local(
    table_weight,
    table_moment,
    table_square,
    position_weight,
    position_moment,
    position_square,
    wide_weight,
    wide_moment,
    wide_square,
    down_weight,
    down_moment,
    down_square,
    vector_weight,
    vector_moment,
    vector_square,
    source_ids,
    target_ids,
    target_labels,
    source_segments,
    target_segments,
    completion_idx,
):
    cuts = lax.axis_size("p")
    ctx_count = 2 * cuts
    shard_count = lax.axis_size("z") * 4
    core = lax.axis_index("c")
    block = lax.axis_index("p") * 2 + core
    ctx_index = lax.axis_index("q") * cuts + lax.axis_index("p")
    tokens = source_ids.shape[1]
    comp_count = completion_idx.shape[1]
    width = vector_weight.shape[1]
    hidden = down_weight.shape[1] * shard_count
    head_count = H
    own_rows = table_weight.shape[0]
    table_low = table_weight.astype(jnp.bfloat16)

    small = jnp.concatenate(
        [source_ids, target_ids, target_labels, source_segments, target_segments, completion_idx], 1
    )
    small = lax.all_gather(small[0], ("q", "p", "c"))
    small = small.reshape(ctx_count, 2, -1)
    small = lax.dynamic_index_in_dim(small, lax.axis_index("q"), 1, keepdims=False)
    src_ids, tgt_ids, tgt_labels, src_seg, tgt_seg = (
        small[:, k * tokens : (k + 1) * tokens] for k in range(5)
    )

    def own_block(blocks):
        return lax.dynamic_index_in_dim(blocks, block, 0, keepdims=False)

    def key_order(blocks):
        pairs = blocks.reshape(cuts, 2, -1)
        pairs = jnp.where(core == 0, pairs, pairs[:, ::-1])
        return jnp.moveaxis(pairs, 1, 0).reshape(-1)

    comp_places = own_block(small[:, 5 * tokens :])
    comp_hit = one_hot(comp_places, tokens)
    own_labels = jnp.take(own_block(tgt_labels), comp_places)

    lookup = Lookup(jnp.concatenate([own_block(src_ids), own_block(tgt_ids)]), own_rows)
    token_rows = lookup.fetch(table_low)

    wide_low = wide_weight.astype(jnp.bfloat16)
    down_low = down_weight.astype(jnp.bfloat16)
    shard_rows, span = wide_low.shape
    bounds = [0, span * 2 // 5, span * 4 // 5, span]
    place_low = position_weight.astype(jnp.bfloat16)
    place_rows, place_columns = place_low.shape
    early_width = span - bounds[2] + bounds[1]
    by_tiles = (
        place_rows * place_columns == shard_rows * 512
        and place_columns % 128 == 0
        and shard_rows % 16 == 0
        and early_width % 512 == 0
    )
    if by_tiles:
        tiles = place_low.reshape(place_rows // 16, 16, place_columns // 128, 128)
        tiles = jnp.moveaxis(tiles, 1, 2).reshape(shard_rows // 16, 4, 16, 128)
        place_pack = jnp.moveaxis(tiles, 1, 2).reshape(shard_rows, 512)
    else:
        place_pack = place_low.reshape(shard_rows, -1)

    def gathered(parts):
        part = parts[0] if len(parts) == 1 else jnp.concatenate(parts, 1)
        return lax.all_gather(part, ALL).reshape(ctx_count, width, part.shape[1])

    def flat_down(part):
        part = part.reshape(-1, shard_rows, part.shape[1])
        return jnp.moveaxis(part, 0, 1).reshape(shard_rows, -1)

    def tall_down(pack):
        return unpack_rows(pack.reshape(ctx_count, shard_count, shard_rows, -1), width // ctx_count)

    early = gathered([wide_low[:, : bounds[1]], wide_low[:, bounds[2] :], place_pack])
    middle = gathered([wide_low[:, bounds[1] : bounds[2]], flat_down(down_low[0])])
    late = gathered([flat_down(down_low[1])])
    if by_tiles:
        position_full = unpack_places(
            early.reshape(ctx_count, shard_count, shard_rows, -1),
            early_width,
            place_rows,
            place_columns,
        )
    else:
        position_full = early[:, :, early_width:].reshape(
            (ctx_count, shard_count) + position_weight.shape
        )
        position_full = jnp.moveaxis(position_full, 0, 2).reshape(-1, width)

    def columns(name, size=None):
        start = starts[name]
        size = size or (hidden if name in FIRSTS else width)
        pieces = []
        while size:
            side, inner = divmod(start, span)
            turn = max(k for k in range(3) if bounds[k] <= inner)
            take = min(size, bounds[turn + 1] - inner)
            source = middle if turn == 1 else early
            at = inner - (0, bounds[1], bounds[2] - bounds[1])[turn]
            pieces.append(source[side, :, at : at + take])
            start, size = start + take, size - take
        return pieces[0] if len(pieces) == 1 else jnp.concatenate(pieces, 1)

    def vector_row(name):
        return vector_weight[name]

    blocks = hidden // width
    base_row = Row.dec_norm3_bias + 1
    enc_first_bias = vector_weight[base_row : base_row + blocks].reshape(-1)
    dec_first_bias = vector_weight[base_row + blocks : base_row + 2 * blocks].reshape(-1)
    names = range(Part.dec_first + 1)
    starts, offset = {}, 0
    for name in names:
        starts[name] = offset
        offset += hidden if name in FIRSTS else width


    table_count = position_full.shape[0]
    src_pos = own_block(doc_positions(src_seg.reshape(-1), table_count).reshape(ctx_count, -1))
    tgt_pos = own_block(doc_positions(tgt_seg.reshape(-1), table_count).reshape(ctx_count, -1))
    src_onehot = one_hot(src_pos, table_count)
    tgt_onehot = one_hot(tgt_pos, table_count)
    src_input = token_rows[:tokens] + product(src_onehot, position_full)
    tgt_input = token_rows[tokens:] + product(tgt_onehot, position_full)

    key_places = key_order(jnp.arange(ctx_count * tokens).reshape(ctx_count, tokens))
    src_keys_seg = key_order(src_seg)
    tgt_keys_seg = key_order(tgt_seg)
    own_src_seg = own_block(src_seg)
    own_tgt_seg = own_block(tgt_seg)
    def no_limit(seg):
        return jnp.full_like(seg, ctx_count * tokens)

    comp_seg = jnp.take(own_tgt_seg, comp_places)

    def marks(query_seg, query_last, key_seg):
        return (
            jnp.pad(jnp.stack([query_seg, query_last]), ((0, 6), (0, 0))),
            jnp.pad(jnp.stack([key_seg, key_places], 1), ((0, 0), (0, 126))),
        )

    enc_marks = marks(own_src_seg, no_limit(own_src_seg), src_keys_seg)
    self_marks = marks(comp_seg, block * tokens + comp_places, tgt_keys_seg)
    cross_marks = marks(comp_seg, no_limit(comp_seg), src_keys_seg)

    def norm(values, gain, bias):
        return norm_forward(values, vector_row(gain), vector_row(bias))

    enc_norm0, enc_saved0 = norm(src_input, Row.enc_norm0_gain, Row.enc_norm0_bias)
    enc_in_b = enc_norm0.astype(jnp.bfloat16)
    enc_queries = project_queries(enc_in_b, columns(Part.enc_wq), vector_row(Row.enc_query_bias))
    enc_pairs = project_pairs(
        enc_in_b, columns(Part.enc_wk, 2 * width), vector_row(Row.enc_value_bias)
    )
    enc_pairs_all = pairs_in(enc_pairs)
    dec_norm0, dec_saved0 = norm(tgt_input, Row.dec_norm0_gain, Row.dec_norm0_bias)
    dec_in_b = dec_norm0.astype(jnp.bfloat16)
    comp_exact = comp_hit.astype(jnp.float32)
    comp_norm0 = jnp.dot(comp_exact, dec_norm0, precision=PRECISE)
    comp_in_b = product(comp_hit, dec_in_b).astype(jnp.bfloat16)
    dec_queries = project_queries(comp_in_b, columns(Part.dec_wq), vector_row(Row.dec_query_bias))
    dec_pairs = project_pairs(
        dec_in_b, columns(Part.dec_wk, 2 * width), vector_row(Row.dec_value_bias)
    )
    dec_pairs_all = pairs_in(dec_pairs)
    enc_branch, enc_mixed_t, enc_logsum = branch_forward(
        enc_queries,
        enc_pairs_all,
        enc_marks,
        columns(Part.enc_out),
        vector_row(Row.enc_out_bias),
        head_count,
    )
    enc_norm1, enc_saved1 = norm(enc_norm0 + enc_branch, Row.enc_norm1_gain, Row.enc_norm1_bias)
    self_branch, self_mixed_t, self_logsum = branch_forward(
        dec_queries,
        dec_pairs_all,
        self_marks,
        columns(Part.dec_out),
        vector_row(Row.dec_out_bias),
        head_count,
    )
    dec_norm1, dec_saved1 = norm(comp_norm0 + self_branch, Row.dec_norm1_gain, Row.dec_norm1_bias)
    cross_in_b = dec_norm1.astype(jnp.bfloat16)
    cross_queries = project_queries(
        cross_in_b, columns(Part.cross_wq), vector_row(Row.cross_query_bias)
    )

    def both_lefts(parts, turned):
        own, other = turn_rows(parts, turned, shard_rows)
        return own, swapped(other, "c")

    left = both_lefts((enc_in_b, dec_in_b), (enc_mixed_t,))
    comp_left = both_lefts((comp_in_b,), (self_mixed_t,))
    table_pair = jnp.concatenate([table_low, swapped(table_low, "c")], 0)
    enc_norm1, cross_queries, middle, own_labels, left, comp_left, table_pair = hold(
        enc_norm1, cross_queries, middle, own_labels, left, comp_left, table_pair
    )
    head_labels = group_in(own_labels, "q").reshape(-1)
    enc_first, enc_second = (
        columns(Part.enc_first),
        tall_down(middle[:, :, bounds[2] - bounds[1] :]),
    )
    enc_mid_b = enc_norm1.astype(jnp.bfloat16)
    enc_ffn, enc_slope, enc_act_t = feed_forward(
        enc_mid_b, enc_first, enc_first_bias, enc_second, vector_row(Row.enc_ffn_bias)
    )
    encoded, enc_saved2 = norm(enc_norm1 + enc_ffn, Row.enc_norm2_gain, Row.enc_norm2_bias)
    encoded_b = encoded.astype(jnp.bfloat16)
    cross_pair_weights = columns(Part.cross_wk, 2 * width)
    cross_pairs = project_pairs(encoded_b, cross_pair_weights, vector_row(Row.cross_value_bias))
    cross_pairs_all = pairs_in(cross_pairs)
    cross_branch, cross_mixed_t, cross_logsum = branch_forward(
        cross_queries,
        cross_pairs_all,
        cross_marks,
        columns(Part.cross_out),
        vector_row(Row.cross_out_bias),
        head_count,
    )
    dec_norm2, dec_saved2 = norm(dec_norm1 + cross_branch, Row.dec_norm2_gain, Row.dec_norm2_bias)
    dec_norm2, late, head_labels = hold(dec_norm2, late, head_labels)
    dec_first, dec_second = columns(Part.dec_first), tall_down(late)
    dec_mid_b = dec_norm2.astype(jnp.bfloat16)
    dec_ffn, dec_slope, dec_act_t = feed_forward(
        dec_mid_b, dec_first, dec_first_bias, dec_second, vector_row(Row.dec_ffn_bias)
    )
    final, dec_saved3 = norm(dec_norm2 + dec_ffn, Row.dec_norm3_gain, Row.dec_norm3_bias)
    final_b = final.astype(jnp.bfloat16)
    head_rows = group_rows(final_b)

    to_turn = ((enc_mid_b, encoded_b), (cross_in_b, dec_mid_b))
    to_turn, head_labels, _ = hold(to_turn, head_labels, final_b)
    mid_left = both_lefts(to_turn[0], ())
    late_left = both_lefts(to_turn[1], (cross_mixed_t,))
    group_start = 0
    for axis in ("q", "p", "z", "x"):
        group_start = group_start * lax.axis_size(axis) + lax.axis_index(axis)
    own_ids = jnp.arange(own_rows, dtype=jnp.int32)
    column_ids = jnp.concatenate(
        [(group_start * 2 + core) * own_rows + own_ids, (group_start * 2 + 1 - core) * own_rows + own_ids]
    )

    def act_left(act_t):
        act_t = act_t.reshape(lax.axis_size("z"), 2, 2, -1, act_t.shape[1])
        own, other = pick(act_t, 2, core), pick(act_t, 2, 1 - core)
        return own[None], swapped(other, "c")[None]

    enc_act, dec_act = act_left(enc_act_t), act_left(dec_act_t)
    head_rows, mid_left, late_left, enc_act, dec_act = hold(
        head_rows, mid_left, late_left, enc_act, dec_act
    )
    terms, mixed_rows, label_rows, stats = head_forward(
        table_pair, head_rows, column_ids, head_labels
    )
    merged_top, merged_sum, merged_label = merge_stats(stats[:3])
    own_logsum = merged_top + jnp.log(merged_sum)
    loss_local = jnp.sum(own_logsum - merged_label)
    line = line_in(line_in(own_logsum, "p"), "z")
    came = from_others([line] * 3, ("q", "x"))
    logsum_rows = jnp.stack([line, came[1], came[0], came[2]]).reshape(-1)
    loss_scale = 1.0 / (comp_count * ctx_count * shard_count)
    row_scale = jnp.exp(stats[0] - logsum_rows)[:, None]
    mixed_rows = mixed_rows * row_scale - label_rows.astype(jnp.float32)
    grad_picked = group_sum(mixed_rows * loss_scale)
    table_grad, other_grad = head_table(
        terms, head_rows, column_ids, row_scale, head_labels, loss_scale
    )
    table_grad, other_grad, grad_picked = hold(table_grad, other_grad, grad_picked)
    table_grad = table_grad + swapped(other_grad, "c")
    vector_grads = {}
    reducer = Reducer()

    def norm_back(grad, saved, gain):
        grad, vector_grads[gain], vector_grads[gain + 1] = norm_backward(
            grad, saved, vector_row(gain)
        )
        return grad

    grad_sum3 = norm_back(grad_picked, dec_saved3, Row.dec_norm3_gain)
    grad_mid, dec_pre_grad, dec_first_bias_g, dec_ffn_grad, vector_grads[Row.dec_ffn_bias] = (
        feed_backward(grad_sum3, dec_slope, dec_first, dec_second)
    )
    grad_sum2 = norm_back(grad_sum3 + grad_mid, dec_saved2, Row.dec_norm2_gain)
    group1 = reducer.add(
        Group(
            (True, late_left, both_cores(dec_pre_grad), ((Part.dec_first, 1, None),)),
            (False, dec_act, both_cores(dec_ffn_grad[None]), ((Part.dec_second, 0, 0),)),
            mixed=1,
        )
    )
    cross_query_grad, cross_grad_pairs, cross_branch_grad, vector_grads[Row.cross_out_bias] = (
        branch_backward(
            grad_sum2,
            cross_queries,
            cross_pairs_all,
            cross_marks,
            cross_logsum,
            columns(Part.cross_out),
            head_count,
        )
    )
    cross_query_grad, cross_grad_pairs = reducer.step(cross_query_grad, cross_grad_pairs)
    cross_pairs_grad = pairs_back(cross_grad_pairs)
    vector_grads[Row.cross_query_bias], grad_cross_in = query_backward(
        columns(Part.cross_wq), cross_query_grad
    )
    grad_sum1 = norm_back(grad_sum2 + grad_cross_in, dec_saved1, Row.dec_norm1_gain)
    cross_pairs_grad, grad_sum1 = reducer.step(cross_pairs_grad, grad_sum1, only=(group1,))
    vector_grads[Row.cross_value_bias], grad_encoded = pairs_backward(
        cross_pair_weights, cross_pairs_grad
    )
    comp_right = both_cores(jnp.stack([cross_query_grad, cross_branch_grad]))
    group2 = group = reducer.add(
        Group(
            (True, mid_left, both_cores(cross_pairs_grad), ((Part.cross_wk, 1, 0), (Part.cross_wv, 1, 1))),
            (False, late_left, comp_right, ((Part.cross_wq, 0, 0), (Part.cross_out, 2, 1))),
            mixed=4,
        )
    )
    grad_sum1 = group.before(grad_sum1)
    dec_query_grad, dec_grad_pairs, dec_branch_grad, vector_grads[Row.dec_out_bias] = (
        branch_backward(
            grad_sum1,
            dec_queries,
            dec_pairs_all,
            self_marks,
            self_logsum,
            columns(Part.dec_out),
            head_count,
        )
    )
    grad_encoded, dec_query_grad, dec_grad_pairs, table_grad = reducer.step(
        grad_encoded, dec_query_grad, dec_grad_pairs, table_grad, only=(group2,)
    )
    dec_pairs_grad = pairs_back(dec_grad_pairs)
    vector_grads[Row.dec_query_bias], grad_dec_q_in = query_backward(
        columns(Part.dec_wq), dec_query_grad
    )
    vector_grads[Row.dec_value_bias], grad_dec_kv_in = pairs_backward(
        columns(Part.dec_wk, 2 * width), dec_pairs_grad
    )
    comp_right = both_cores(jnp.stack([dec_query_grad, dec_branch_grad]))
    group3 = reducer.add(
        Group(
            (True, left, both_cores(dec_pairs_grad), ((Part.dec_wk, 1, 0), (Part.dec_wv, 1, 1))),
            (False, comp_left, comp_right, ((Part.dec_wq, 0, 0), (Part.dec_out, 1, 1))),
            mixed=4,
        )
    )
    grad_enc2 = norm_back(grad_encoded, enc_saved2, Row.enc_norm2_gain)
    grad_comp0 = lax.dot_general(
        comp_exact, grad_sum1 + grad_dec_q_in, LEFT_T, precision=PRECISE
    )
    grad_tgt_input = norm_back(grad_comp0 + grad_dec_kv_in, dec_saved0, Row.dec_norm0_gain)
    grad_enc2, grad_tgt_input = reducer.step(grad_enc2, grad_tgt_input, only=(group1, group2))
    grad_enc_mid, enc_pre_grad, enc_first_bias_g, enc_ffn_grad, vector_grads[Row.enc_ffn_bias] = (
        feed_backward(grad_enc2, enc_slope, enc_first, enc_second)
    )
    grad_enc1 = norm_back(grad_enc2 + grad_enc_mid, enc_saved1, Row.enc_norm1_gain)
    grad_enc1, enc_pre_grad, enc_ffn_grad = reducer.step(grad_enc1, enc_pre_grad, enc_ffn_grad)
    group4 = reducer.add(
        Group(
            (True, mid_left, both_cores(enc_pre_grad), ((Part.enc_first, 0, None),)),
            (False, enc_act, both_cores(enc_ffn_grad[None]), ((Part.enc_second, 0, 0),)),
            mixed=1,
        )
    )
    enc_query_grad, enc_grad_pairs, enc_branch_grad, vector_grads[Row.enc_out_bias] = (
        branch_backward(
            grad_enc1,
            enc_queries,
            enc_pairs_all,
            enc_marks,
            enc_logsum,
            columns(Part.enc_out),
            head_count,
        )
    )
    enc_query_grad, enc_grad_pairs = reducer.step(enc_query_grad, enc_grad_pairs)
    enc_pairs_grad = pairs_back(enc_grad_pairs)
    vector_grads[Row.enc_query_bias], grad_enc_q_in = query_backward(
        columns(Part.enc_wq), enc_query_grad
    )
    vector_grads[Row.enc_value_bias], grad_enc_kv_in = pairs_backward(
        columns(Part.enc_wk, 2 * width), enc_pairs_grad
    )
    grad_src_input = norm_back(
        grad_enc1 + grad_enc_q_in + grad_enc_kv_in, enc_saved0, Row.enc_norm0_gain
    )
    right = both_cores(
        jnp.concatenate([enc_pairs_grad, enc_query_grad[None], enc_branch_grad[None]], 0)
    )
    group = reducer.add(
        Group(
            (True, left, right, ((Part.enc_wk, 0, 0), (Part.enc_wv, 0, 1))),
            (False, left, right, ((Part.enc_wq, 0, 2), (Part.enc_out, 2, 3))),
            mixed=4,
        )
    )
    table_grad = lookup.give(
        table_grad,
        jnp.concatenate(
            [grad_src_input.astype(jnp.bfloat16), grad_tgt_input.astype(jnp.bfloat16)], 0
        ),
    )
    grad_src_input, grad_tgt_input = group.before(grad_src_input, grad_tgt_input)
    position_grad = lax.dot_general(
        src_onehot.astype(jnp.float32), grad_src_input, LEFT_T, precision=PRECISE
    ) + lax.dot_general(
        tgt_onehot.astype(jnp.float32), grad_tgt_input, LEFT_T, precision=PRECISE
    )
    reducer.add(Group(ready=[(Part.position, position_grad)]))
    vector_grad = pack_rows(
        [vector_grads[name] for name in range(base_row)] + [enc_first_bias_g, dec_first_bias_g],
        width,
    )
    while reducer.moving:
        reducer.advance()
    summed = reducer.done

    def own_columns(part):
        if cuts == 1:
            return own_first(part, 1)[0]
        part = part.reshape(part.shape[0], ctx_count, -1)
        return lax.dynamic_index_in_dim(part, ctx_index, 1, keepdims=False)

    wide_grad = own_columns(
        jnp.concatenate(
            [
                summed[name]
                for name in (
                    Part.enc_wq,
                    Part.enc_wk,
                    Part.enc_out,
                    Part.enc_first,
                    Part.dec_wq,
                    Part.dec_wk,
                    Part.dec_out,
                    Part.cross_wq,
                    Part.cross_wk,
                    Part.cross_out,
                    Part.dec_first,
                )
            ],
            1,
        )
    )
    deep = [summed[name] for name in (Part.enc_second, Part.dec_second, Part.position)]
    if cuts > 1:
        deep = [own_columns(part) for part in deep]
    down_grad, position_grad = jnp.stack(deep[:2]), deep[2]
    owned_squares = (
        jnp.sum(wide_grad * wide_grad)
        + jnp.sum(down_grad * down_grad)
        + jnp.sum(position_grad * position_grad)
        + jnp.sum(table_grad * table_grad)
    )
    scalars = jnp.pad(jnp.stack([owned_squares, loss_local])[None, :], ((0, 0), (0, width - 2)))
    sums = all_sum(jnp.concatenate([vector_grad, scalars], 0))
    vector_grad, square_total, loss_sum = sums[:-1], sums[-1, 0], sums[-1, 1]
    grad_norm = jnp.sqrt(square_total + jnp.sum(vector_grad * vector_grad))
    clip_factor = jnp.minimum(1.0, CLIP_LIMIT / (grad_norm + 1e-06))
    outs = [loss_sum, grad_norm]
    for weight, moment, square, grad, decay, rate in (
        (table_weight, table_moment, table_square, table_grad, WEIGHT_DECAY, LEARN_RATE),
        (position_weight, position_moment, position_square, position_grad, WEIGHT_DECAY, LEARN_RATE),
        (wide_weight, wide_moment, wide_square, wide_grad, WEIGHT_DECAY, LEARN_RATE),
        (down_weight, down_moment, down_square, down_grad, WEIGHT_DECAY, LEARN_RATE),
        (vector_weight, vector_moment, vector_square, vector_grad, 0.0, VECTOR_RATE),
    ):
        outs.extend(adam_step(weight, moment, square, grad * clip_factor, decay, rate))
    return tuple(outs)


def solution(mesh):
    ctx_count, shard_count = mesh.devices.shape
    fine = Mesh(mesh.devices.reshape(2, ctx_count // 2, shard_count // 4, 2, 2), ALL)
    ctx, shard = ("q", "p"), ("z", "x", "c")
    table, plane, deep, whole = P(ALL, None), P(shard, ctx), P(None, shard, ctx), P()
    states = (table,) * 3 + (plane,) * 6 + (deep,) * 3 + (whole,) * 3
    return jax.shard_map(
        local,
        mesh=fine,
        in_specs=states + (plane,) * 6,
        out_specs=(whole, whole) + states,
        check_vma=False,
    )
```
